32 devices in a mesh: seq: 8 (over y, x, core), row: 4 (over z).
Axes of the slice: x: 2, y: 2, z: 4, core: 2. Of those that a mesh axis runs over, the one named last changes fastest.
Arguments:
- block_input: bfloat16 [16, 1024, 512], P('row', 'seq'), may hold values from -6 to 6
- segment_ids: int32 [16, 1024], P('row'), may hold values from 0 to 1, as said below
- ln1_gain: float32 [512], replicated, may hold values from 0.5 to 1.5
- ln1_shift: float32 [512], replicated, may hold values from -1.5 to 1.5
- w_qkv: bfloat16 [512, 1536], replicated, may hold values from -0.375 to 0.375
- bias_query: float32 [512], replicated, may hold values from -1.5 to 1.5
- bias_value: float32 [512], replicated, may hold values from -1.5 to 1.5
- w_out: bfloat16 [512, 512], replicated, may hold values from -1 to 1
- bias_out: float32 [512], replicated, may hold values from -1.5 to 1.5
- ln2_gain: float32 [512], replicated, may hold values from 0.5 to 1.5
- ln2_shift: float32 [512], replicated, may hold values from -1.5 to 1.5
- w_up: bfloat16 [512, 2048], replicated, may hold values from -0.25 to 0.25
- bias_up: float32 [2048], replicated, may hold values from -1.5 to 1.5
- w_down: bfloat16 [2048, 512], replicated, may hold values from -0.125 to 0.125
- bias_down: float32 [512], replicated, may hold values from -1.5 to 1.5
- out_grad: bfloat16 [16, 1024, 512], P('row', 'seq'), may hold values from -6 to 6
Outputs:
- output: bfloat16 [16, 1024, 512], P('row', 'seq')
- input_grad: bfloat16 [16, 1024, 512], P('row', 'seq')
- grad_ln1_gain: float32 [512], replicated
- grad_ln1_shift: float32 [512], replicated
- grad_w_qkv: float32 [512, 1536], replicated
- grad_bias_query: float32 [512], replicated
- grad_bias_value: float32 [512], replicated
- grad_w_out: float32 [512, 512], replicated
- grad_bias_out: float32 [512], replicated
- grad_ln2_gain: float32 [512], replicated
- grad_ln2_shift: float32 [512], replicated
- grad_w_up: float32 [512, 2048], replicated
- grad_bias_up: float32 [2048], replicated
- grad_w_down: float32 [2048, 512], replicated
- grad_bias_down: float32 [512], replicated
The draws below stay inside these ranges and needn't reach their ends.
Inputs may be any that keep to these rules, and one draw needn't show every extreme that they name: `segment_ids`: ids start at 0 and never fall along a row, rising by one at each new crop; equal ids mark one crop, whose tokens attend only to each other; in each aligned group of 4 rows one row, drawn from the seed, is a single crop, and every other row holds exactly 1024 // (4 * 128) crops.
All inputs are finite; a program needn't handle non-finite values.
Results may differ from the reference program's by a relative error of at most 0.015.
Values may be sent and summed in bfloat16 or wider, within the bound.
No kernel may reach another device: no remote copies, remote signals or barrier semaphores. Data moves between devices by JAX's collectives and lax.ppermute only.
A program may use at most 256 MiB of HBM per device.

```python
import jax
import jax.numpy as jnp
from jax import lax

D = 512
HEADS = 8
HEAD = 64
FF = 2048
BAND = 128
ROWS_DEV = 4
LENGTH = 1024
ROWS = 16


def draw_segment_ids(key, part):
    key = jax.random.fold_in(key, 11)
    first_key, second_key = jax.random.split(key)
    crops = LENGTH // (4 * BAND)
    row_keys = jax.random.split(first_key, ROWS)
    orders = jax.vmap(lambda row_key: jax.random.permutation(row_key, LENGTH - 1))(row_keys) + 1
    chosen_starts = orders[:, :crops - 1]
    positions = jnp.arange(LENGTH, dtype=jnp.int32)
    starts = jnp.sum((positions[None, None, :] == chosen_starts[:, :, None]).astype(jnp.int32), axis=1)
    counts = jnp.cumsum(starts, axis=1)
    chosen = jax.random.randint(second_key, (ROWS // ROWS_DEV,), 0, ROWS_DEV)
    single = jnp.arange(ROWS) % ROWS_DEV == jnp.repeat(chosen, ROWS_DEV)
    return jnp.where(single[:, None], 0, counts).astype(jnp.int32)


def steps_of(stream_key, shape, shards, low, top_value):
    def one(position, blocks):
        draws = jax.random.uniform(jax.random.fold_in(jax.random.fold_in(stream_key, 6), position), (blocks,), jnp.float32, low / len(shards), top_value / len(shards))
        return jnp.repeat(jnp.exp(draws), shape[position] // blocks).reshape((-1,) + (1,) * (len(shape) - position - 1))

    factor_of = one(*shards[0])
    for cut in shards[1:]:
        factor_of = factor_of * one(*cut)
    return factor_of


def bell_draw(own_key, shape, width, most, cuts=(), kind=jnp.bfloat16):
    array = jax.random.normal(own_key, shape, jnp.float32) * width
    if len(cuts) > 0:
        array = steps_of(own_key, shape, cuts, -0.22, 0.18) * array
    return jnp.clip(array, min=-most, max=most).astype(kind)


def setup_inputs(seed: int = 0) -> dict:
    splits = jax.random.split(jax.random.key(seed), 17)
    return {
        "block_input": bell_draw(splits[0], (ROWS, LENGTH, D), 1.0, 6.0, ((0, 4), (1, 8))),
        "segment_ids": draw_segment_ids(jax.random.fold_in(splits[16], 71), 0),
        "ln1_gain": jnp.clip(1.0 + 0.1 * jax.random.normal(splits[2], (D,), jnp.float32), 0.5, 1.5),
        "ln1_shift": bell_draw(splits[3], (D,), 0.3, 1.5, (), jnp.float32),
        "w_qkv": bell_draw(splits[4], (D, 3 * D), (D // 2) ** -0.5, 0.375),
        "bias_query": bell_draw(splits[5], (D,), 0.3, 1.5, (), jnp.float32),
        "bias_value": bell_draw(splits[6], (D,), 0.3, 1.5, (), jnp.float32),
        "w_out": bell_draw(splits[7], (D, D), (D // 16) ** -0.5, 1.0),
        "bias_out": bell_draw(splits[8], (D,), 0.3, 1.5, (), jnp.float32),
        "ln2_gain": jnp.clip(1.0 + 0.1 * jax.random.normal(splits[9], (D,), jnp.float32), 0.5, 1.5),
        "ln2_shift": bell_draw(splits[10], (D,), 0.3, 1.5, (), jnp.float32),
        "w_up": bell_draw(splits[11], (D, FF), D ** -0.5, 0.25),
        "bias_up": bell_draw(splits[12], (FF,), 0.3, 1.5, (), jnp.float32),
        "w_down": bell_draw(splits[13], (FF, D), FF ** -0.5, 0.125),
        "bias_down": bell_draw(splits[14], (D,), 0.3, 1.5, (), jnp.float32),
        "out_grad": bell_draw(splits[15], (ROWS, LENGTH, D), 1.0, 6.0, ((0, 4), (1, 8))),
    }


EPSILON = 1e-06
NEGATIVE = -1e+30
HIGHEST = lax.Precision.HIGHEST

@jax.custom_vjp
def low(v):
    return lax.optimization_barrier(v.astype(jnp.bfloat16)).astype(jnp.float32)

@jax.custom_vjp
def low_back(v):
    return v

def low_keep(v):
    return (low(v), None)

def low_pass(kept, grad):
    return (grad,)

def back_keep(v):
    return (v, None)

def back_low(kept, grad):
    return (low(grad),)
low.defvjp(low_keep, low_pass)
low_back.defvjp(back_keep, back_low)

def layer_norm(inputs, scaling, offset_row):
    centre = lax.optimization_barrier(jnp.mean(inputs, axis=-1, keepdims=True))
    centred = inputs - centre
    spread = lax.optimization_barrier(jnp.mean(centred * centred, axis=-1, keepdims=True))
    return centred * lax.rsqrt(spread + EPSILON) * scaling + offset_row

def row_forward(inputs, segments, params):
    ln1_gain, ln1_shift, w_qkv, bias_query, bias_value, w_out, bias_out, ln2_gain, ln2_shift, w_up, bias_up, w_down, bias_down = params
    score_scale = HEAD ** (-0.5)
    normed = low(layer_norm(inputs, ln1_gain, ln1_shift))
    packed = jnp.dot(normed, w_qkv, precision=HIGHEST)
    queries = low_back(low((packed[:, :D] + bias_query) * score_scale))
    keys_all = low_back(low(packed[:, D:2 * D]))
    values_all = low_back(low(packed[:, 2 * D:] + bias_value))
    key_heads = keys_all.reshape(LENGTH, HEADS, HEAD)
    value_heads = values_all.reshape(LENGTH, HEADS, HEAD)
    block_rows = min(512, LENGTH)
    query_blocks = queries.reshape(LENGTH // block_rows, block_rows, HEADS, HEAD)
    segment_blocks = segments.reshape(LENGTH // block_rows, block_rows)

    def attend(row_pair):
        query_block, segment_block = row_pair
        scores = low_back(jnp.einsum('bhd,khd->hbk', query_block, key_heads, precision=HIGHEST))
        allowed = segment_block[:, None] == segments[None, :]
        scores = jnp.where(allowed[None], scores, NEGATIVE)
        biggest = lax.optimization_barrier(jnp.max(scores, axis=-1, keepdims=True))
        exponents = jnp.exp(scores - biggest)
        totals = lax.optimization_barrier(jnp.sum(exponents, axis=-1))
        summed = jnp.einsum('hbk,khd->bhd', low(exponents), value_heads, precision=HIGHEST)
        return summed / jnp.transpose(totals)[:, :, None]
    attention_mix = lax.map(jax.checkpoint(attend), (query_blocks, segment_blocks)).reshape(LENGTH, D)
    attended = low_back(jnp.dot(low_back(low(attention_mix)), w_out, precision=HIGHEST) + bias_out)
    middle = inputs + attended
    normed_two = low(layer_norm(middle, ln2_gain, ln2_shift))
    hidden = low_back(jnp.dot(normed_two, w_up, precision=HIGHEST) + bias_up)
    active = low(jax.nn.gelu(hidden, approximate=True))
    return middle + low_back(jnp.dot(active, w_down, precision=HIGHEST) + bias_down)

def reference(block_input, segment_ids, ln1_gain, ln1_shift, w_qkv, bias_query, bias_value, w_out, bias_out, ln2_gain, ln2_shift, w_up, bias_up, w_down, bias_down, out_grad):
    params = tuple((weight.astype(jnp.float32) for weight in (ln1_gain, ln1_shift, w_qkv, bias_query, bias_value, w_out, bias_out, ln2_gain, ln2_shift, w_up, bias_up, w_down, bias_down)))

    def whole(inputs, weights):

        def one_row(row_pair):
            return row_forward(row_pair[0], row_pair[1], weights)
        return lax.map(jax.checkpoint(one_row), (inputs, segment_ids))
    output, pull = jax.vjp(whole, block_input.astype(jnp.float32), params)
    input_grad, param_grads = pull(out_grad.astype(jnp.float32))
    return (output.astype(jnp.bfloat16), input_grad.astype(jnp.bfloat16), param_grads[0], param_grads[1], param_grads[2], param_grads[3], param_grads[4], param_grads[5], param_grads[6], param_grads[7], param_grads[8], param_grads[9], param_grads[10], param_grads[11], param_grads[12])
```

```python
import functools

import jax
import jax.numpy as jnp
from jax import lax
from jax.experimental import pallas as pl
from jax.experimental.pallas import tpu as pltpu
from jax.sharding import PartitionSpec as P

HEADS = 8
EPSILON = 1e-06
BIG = 1e30
LSE_LANE = 16
F32 = jnp.float32
BF16 = jnp.bfloat16
VMEM_LIMIT = 48 * 1024 * 1024


def dot_nn(a, b):
    return lax.dot_general(a, b, (((1,), (0,)), ((), ())), preferred_element_type=F32)


def dot_nt(a, b):
    return lax.dot_general(a, b, (((1,), (1,)), ((), ())), preferred_element_type=F32)


def dot_tn(a, b):
    return lax.dot_general(a, b, (((0,), (0,)), ((), ())), preferred_element_type=F32)


def split_three(value):
    high = value.astype(BF16)
    rest = value - high.astype(F32)
    middle = rest.astype(BF16)
    low = (rest - middle.astype(F32)).astype(BF16)
    return high, middle, low


def lane_index(shape):
    return lax.broadcasted_iota(jnp.int32, shape, len(shape) - 1)


def three_lanes(value, lanes):
    high, middle, low = split_three(value)
    spot = lanes % 64
    out = jnp.where(spot == LSE_LANE, high.astype(F32), 0.0)
    out = jnp.where(spot == LSE_LANE + 1, middle.astype(F32), out)
    return jnp.where(spot == LSE_LANE + 2, low.astype(F32), out)


def norm_parts(value):
    centre = jnp.mean(value, axis=-1, keepdims=True)
    centred = value - centre
    spread = jnp.mean(centred * centred, axis=-1, keepdims=True)
    scale = lax.rsqrt(spread + EPSILON)
    return centred * scale, scale


def norm_back(grad, unit, scale, gain):
    grad_unit = grad * gain
    first = jnp.mean(grad_unit, axis=-1, keepdims=True)
    second = jnp.mean(grad_unit * unit, axis=-1, keepdims=True)
    return scale * (grad_unit - first - unit * second)


def qkv_kernel(pieces, width, *refs):
    x_refs = refs[:pieces]
    gain, shift, w_ref, bq_ref, bv_ref, normed_ref, q_ref, kv_ref = refs[pieces:]
    band = x_refs[0].shape[0]
    for j in range(pieces):
        unit, _ = norm_parts(x_refs[j][...].astype(F32))
        normed_ref[j * band : (j + 1) * band, :] = (unit * gain[...] + shift[...]).astype(BF16)
    normed = normed_ref[...]
    q = dot_nn(normed, w_ref[:, :width])
    q_ref[...] = ((q + bq_ref[...]) * (width // HEADS) ** -0.5).astype(BF16)
    kv_ref[:, :width] = dot_nn(normed, w_ref[:, width : 2 * width]).astype(BF16)
    kv_ref[:, width:] = (dot_nn(normed, w_ref[:, 2 * width :]) + bv_ref[...]).astype(BF16)


def forward_kernel(parts, rows, *refs):
    q_ref = refs[0]
    k_refs = refs[1 : 1 + parts]
    v_refs = refs[1 + parts : 1 + 2 * parts]
    qf_ref, kf_ref, mix_ref, qfb_ref, k_aug, v_aug = refs[1 + 2 * parts :]
    tokens = q_ref.shape[0]
    low_half = (lane_index((1, 128)) < 64).astype(F32)
    halves = (low_half.astype(BF16), (1.0 - low_half).astype(BF16))
    for parity in range(2):
        mine, other = halves[parity], halves[1 - parity]
        start = 0
        for k_ref, v_ref in zip(k_refs, v_refs):
            stop = start + k_ref.shape[0]
            k_aug[parity, start:stop, :] = k_ref[...] * mine + kf_ref[start:stop, :] * other
            v_aug[parity, start:stop, :] = v_ref[...] * mine + other
            start = stop
    lanes = lane_index((rows, 128))
    low = lanes < 64

    def block(step, carry):
        at = pl.ds(pl.multiple_of(step * rows, rows), rows)
        q = q_ref[at, :]
        qf = qf_ref[at, :]
        sums, tops = [], []
        for parity in range(2):
            mine, other = halves[parity], halves[1 - parity]
            scores = dot_nt(q * mine + qf * other, k_aug[parity])
            top = jnp.max(scores, axis=-1, keepdims=True)
            exps = jnp.exp(scores - top).astype(BF16)
            sums.append(dot_nn(exps, v_aug[parity]))
            tops.append(jnp.broadcast_to(top, (rows, 128)))
        total = jnp.where(low, sums[1], sums[0])
        mix_ref[at, :] = jnp.where(low, sums[0], sums[1]) / pltpu.roll(total, 64, 1)
        log_total = jnp.where(low, tops[1], tops[0]) + jnp.log(total)
        qfb_ref[at, :] = (qf.astype(F32) + three_lanes(-log_total, lanes)).astype(BF16)
        return carry

    lax.fori_loop(0, tokens // rows, block, 0)


def attention_forward(q, kvs, qf, kf, rows=256):
    tokens, width = q.shape
    pairs = width // 128
    length = kf.shape[0]
    parts = len(kvs)
    in_specs = [pl.BlockSpec((tokens, 128), lambda h: (0, h))]
    in_specs += [pl.BlockSpec((kv.shape[0], 128), lambda h: (0, h)) for kv in kvs]
    in_specs += [pl.BlockSpec((kv.shape[0], 128), lambda h: (0, pairs + h)) for kv in kvs]
    in_specs += [
        pl.BlockSpec((tokens, 128), lambda h: (0, 0)),
        pl.BlockSpec((length, 128), lambda h: (0, 0)),
    ]
    return pl.pallas_call(
        functools.partial(forward_kernel, parts, rows),
        grid=(pairs,),
        in_specs=in_specs,
        out_specs=[
            pl.BlockSpec((tokens, 128), lambda h: (0, h)),
            pl.BlockSpec((tokens, 128), lambda h: (0, h)),
        ],
        out_shape=[
            jax.ShapeDtypeStruct((tokens, width), F32),
            jax.ShapeDtypeStruct((tokens, width), BF16),
        ],
        scratch_shapes=[pltpu.VMEM((2, length, 128), BF16), pltpu.VMEM((2, length, 128), BF16)],
        compiler_params=pltpu.CompilerParams(vmem_limit_bytes=VMEM_LIMIT),
        name="attention_forward",
        cost_estimate=pl.CostEstimate(
            flops=4 * tokens * length * width, bytes_accessed=8 * tokens * width,
            transcendentals=tokens * length * HEADS,
        ),
    )(q, *kvs, *kvs, qf, kf)


def backward_kernel(parts, rows, *refs):
    q_ref, gm_ref, qfb_ref, gmf_ref = refs[:4]
    k_refs = refs[4 : 4 + parts]
    v_refs = refs[4 + parts : 4 + 2 * parts]
    kf_ref = refs[4 + 2 * parts]
    rest = refs[5 + 2 * parts :]
    dq_ref = rest[0]
    dk_refs = rest[1 : 1 + parts]
    dv_refs = rest[1 + parts : 1 + 2 * parts]
    q_aug, gm_aug, dqt = rest[1 + 2 * parts :]
    low_half = (lane_index((1, 128)) < 64).astype(F32)
    halves = (low_half.astype(BF16), (1.0 - low_half).astype(BF16))
    for parity in range(2):
        mine, other = halves[parity], halves[1 - parity]
        q_aug[parity] = q_ref[...] * mine + qfb_ref[...] * other
        gm_aug[parity] = gm_ref[...] * mine + gmf_ref[...] * other
    dqt[...] = jnp.zeros_like(dqt)
    low = lane_index((rows, 128)) < 64
    start = 0
    for k_ref, v_ref, dk_ref, dv_ref in zip(k_refs, v_refs, dk_refs, dv_refs):

        def block(step, carry, start=start, k_ref=k_ref, v_ref=v_ref, dk_ref=dk_ref, dv_ref=dv_ref):
            at = pl.ds(pl.multiple_of(step * rows, rows), rows)
            at_all = pl.ds(pl.multiple_of(start + step * rows, rows), rows)
            k, v, kf = k_ref[at, :], v_ref[at, :], kf_ref[at_all, :]
            dks, dvs = [], []
            for parity in range(2):
                mine, other = halves[parity], halves[1 - parity]
                k_aug = k * mine + kf * other
                v_aug = v * mine + other
                probs = jnp.exp(dot_nt(k_aug, q_aug[parity]))
                slopes = dot_nt(v_aug, gm_aug[parity])
                grads = (probs * slopes).astype(BF16)
                dvs.append(dot_nn(probs.astype(BF16), gm_ref[...]))
                dks.append(dot_nn(grads, q_ref[...]))
                dqt[parity] += dot_tn(k, grads)
            dk_ref[at, :] = jnp.where(low, dks[0], dks[1]).astype(dk_ref.dtype)
            dv_ref[at, :] = jnp.where(low, dvs[0], dvs[1]).astype(dv_ref.dtype)
            return carry

        lax.fori_loop(0, k_ref.shape[0] // rows, block, 0)
        start += k_ref.shape[0]
    dq_t = jnp.concatenate([dqt[0, :64, :], dqt[1, 64:, :]], axis=0)
    dq_ref[...] = dq_t.T.astype(BF16) * (64.0**-0.5)


def attention_backward(q, gm, qfb, gmf, kvs, kf, first, count, rows=256):
    tokens, width = q.shape
    pairs = width // 128
    length = kf.shape[0]
    parts = len(kvs)
    of_pair = lambda h: (0, first + h)
    in_specs = [pl.BlockSpec((tokens, 128), of_pair)] * 4
    in_specs += [pl.BlockSpec((kv.shape[0], 128), of_pair) for kv in kvs]
    in_specs += [pl.BlockSpec((kv.shape[0], 128), lambda h: (0, pairs + first + h)) for kv in kvs]
    in_specs += [pl.BlockSpec((length, 128), lambda h: (0, 0))]
    kinds = [F32] + [BF16] * (parts - 1)
    wide = 128 * count
    outs = [jax.ShapeDtypeStruct((tokens, wide), BF16)]
    outs += [jax.ShapeDtypeStruct((kv.shape[0], wide), kind) for kv, kind in zip(kvs, kinds)] * 2
    out_specs = [pl.BlockSpec((tokens, 128), lambda h: (0, h))]
    out_specs += [pl.BlockSpec((kv.shape[0], 128), lambda h: (0, h)) for kv in kvs] * 2
    got = pl.pallas_call(
        functools.partial(backward_kernel, parts, rows),
        grid=(count,),
        in_specs=in_specs,
        out_specs=out_specs,
        out_shape=outs,
        scratch_shapes=[
            pltpu.VMEM((2, tokens, 128), BF16),
            pltpu.VMEM((2, tokens, 128), BF16),
            pltpu.VMEM((2, 128, tokens), F32),
        ],
        compiler_params=pltpu.CompilerParams(vmem_limit_bytes=VMEM_LIMIT),
        name="attention_backward",
        cost_estimate=pl.CostEstimate(
            flops=10 * tokens * length * wide, bytes_accessed=12 * tokens * wide,
            transcendentals=tokens * length * wide // 64,
        ),
    )(q, gm, qfb, gmf, *kvs, *kvs, kf)
    return got[0], got[1 : 1 + parts], got[1 + parts :]


def middle_kernel(pieces, rows, *refs):
    x_refs = refs[:pieces]
    dy_refs = refs[pieces : 2 * pieces]
    (mix_ref, w_out, b_out, gain, shift, w_up, b_up, w_down, b_down) = refs[2 * pieces : 2 * pieces + 9]
    outs = refs[2 * pieces + 9 :]
    (out_ref, mixed_ref, two_ref, active_ref, gh_ref, ga_ref, gmid_ref, gm_ref, gmf_ref, vec_ref, dy_ref) = outs
    band = x_refs[0].shape[0]
    tokens, width = mix_ref.shape
    ff = w_up.shape[1]
    vec_ref[...] = jnp.zeros_like(vec_ref)
    c0 = 0.7978845608028654
    c1 = 0.044715
    row = lax.broadcasted_iota(jnp.int32, (width, width), 0) // 64
    column = lane_index((width, width)) // 64
    opposite = (row == (column + 1 - 2 * (column % 2))).astype(F32).astype(BF16)
    per = rows // band
    for t in range(tokens // rows):
        at = slice(t * rows, (t + 1) * rows)
        x = jnp.concatenate([x_refs[t * per + j][...] for j in range(per)], axis=0).astype(F32)
        dy = jnp.concatenate([dy_refs[t * per + j][...] for j in range(per)], axis=0)
        dy_ref[at, :] = dy
        mix = mix_ref[at, :]
        mixed = mix.astype(BF16)
        mixed_ref[at, :] = mixed
        middle = x + (dot_nn(mixed, w_out[...]) + b_out[...])
        unit, scale = norm_parts(middle)
        two = (unit * gain[...] + shift[...]).astype(BF16)
        two_ref[at, :] = two
        out = middle + b_down[...]
        grad_two = jnp.zeros((rows, width), F32)
        step = 512
        for f in range(0, ff, step):
            fs = slice(f, f + step)
            hidden = dot_nn(two, w_up[:, fs]) + b_up[:, fs]
            square = hidden * hidden
            tanh = jnp.tanh(c0 * hidden * (1.0 + c1 * square))
            half = 0.5 * (1.0 + tanh)
            active = (hidden * half).astype(BF16)
            active_ref[at, fs] = active
            out = out + dot_nn(active, w_down[fs, :])
            slope = half + hidden * (0.5 * (1.0 - tanh * tanh)) * (c0 + (3.0 * c0 * c1) * square)
            grad = dot_nt(dy, w_down[fs, :]) * slope
            grad_low = grad.astype(BF16)
            gh_ref[at, fs] = grad_low
            vec_ref[0:1, fs] += jnp.sum(grad_low.astype(F32), axis=0, keepdims=True)
            grad_two = grad_two + dot_nt(grad_low, w_up[:, fs])
        out_ref[at, :] = out.astype(BF16)
        dy_wide = dy.astype(F32)
        grad_middle = dy_wide + norm_back(grad_two, unit, scale, gain[...])
        gmid_ref[at, :] = grad_middle
        vec_ref[1:2, :width] += jnp.sum(grad_two * unit, axis=0, keepdims=True)
        vec_ref[2:3, :width] += jnp.sum(grad_two, axis=0, keepdims=True)
        vec_ref[3:4, :width] += jnp.sum(dy_wide, axis=0, keepdims=True)
        grad_attn = grad_middle.astype(BF16)
        ga_ref[at, :] = grad_attn
        vec_ref[4:5, :width] += jnp.sum(grad_attn.astype(F32), axis=0, keepdims=True)
        gm = dot_nt(grad_attn, w_out[...]).astype(BF16)
        gm_ref[at, :] = gm
        high, mid, low = split_three(gm.astype(F32) * mix)
        inner = dot_nn(high, opposite) + (dot_nn(mid, opposite) + dot_nn(low, opposite))
        gmf_ref[at, :] = three_lanes(-inner, lane_index((rows, width))).astype(BF16)


def middle_part(xs, dys, mix, w_out, b_out, gain, shift, w_up, b_up, w_down, b_down, rows=256):
    tokens, width = mix.shape
    ff = w_up.shape[1]
    shape = jax.ShapeDtypeStruct
    return pl.pallas_call(
        functools.partial(middle_kernel, len(xs), rows),
        out_shape=[
            shape((tokens, width), BF16),
            shape((tokens, width), BF16),
            shape((tokens, width), BF16),
            shape((tokens, ff), BF16),
            shape((tokens, ff), BF16),
            shape((tokens, width), BF16),
            shape((tokens, width), F32),
            shape((tokens, width), BF16),
            shape((tokens, width), BF16),
            shape((8, ff), F32),
            shape((tokens, width), BF16),
        ],
        compiler_params=pltpu.CompilerParams(vmem_limit_bytes=VMEM_LIMIT),
        name="middle_part",
        cost_estimate=pl.CostEstimate(
            flops=2 * tokens * width * (4 * ff + 5 * width), bytes_accessed=8 * 1024 * 1024,
            transcendentals=tokens * ff,
        ),
    )(*xs, *dys, mix, w_out, b_out, gain, shift, w_up, b_up, w_down, b_down)


def last_kernel(pieces, *refs):
    x_refs = refs[:pieces]
    dq_ref, dk_ref, dv_ref, gmid_ref, gain, w_ref = refs[pieces : pieces + 6]
    out_ref, vec_ref = refs[pieces + 6 :]
    width = dq_ref.shape[1]
    grad = dot_nt(dq_ref[...], w_ref[:, :width])
    grad = grad + dot_nt(dk_ref[...], w_ref[:, width : 2 * width])
    grad = grad + dot_nt(dv_ref[...], w_ref[:, 2 * width :])
    x = jnp.concatenate([ref[...] for ref in x_refs], axis=0).astype(F32)
    unit, scale = norm_parts(x)
    out_ref[...] = (gmid_ref[...] + norm_back(grad, unit, scale, gain[...])).astype(BF16)
    vec_ref[...] = jnp.zeros_like(vec_ref)
    vec_ref[0:1, :] = jnp.sum(dq_ref[...].astype(F32), axis=0, keepdims=True)
    vec_ref[1:2, :] = jnp.sum(dv_ref[...].astype(F32), axis=0, keepdims=True)
    vec_ref[2:3, :] = jnp.sum(grad * unit, axis=0, keepdims=True)
    vec_ref[3:4, :] = jnp.sum(grad, axis=0, keepdims=True)


def swap(value, axis, size, mask):
    return lax.ppermute(value, axis, [(i, i ^ mask) for i in range(size)])


def scatter_sum(value, bits):
    for axis, size, mask, own in bits:
        half = value.shape[0] // 2
        sent = lax.dynamic_slice_in_dim(value, (1 - own) * half, half, 0)
        kept = lax.dynamic_slice_in_dim(value, own * half, half, 0)
        got = swap(sent, axis, size, mask)
        value = (kept.astype(F32) + got.astype(F32)).astype(BF16)
    return value


def gather_back(value, bits):
    for axis, size, mask, own in reversed(bits):
        got = swap(value, axis, size, mask)
        value = jnp.where(
            own == 0, jnp.concatenate([value, got], 0), jnp.concatenate([got, value], 0)
        )
    return value


def exchange_sum(value, bits):
    for axis, size, mask, own in bits:
        value = (value.astype(F32) + swap(value, axis, size, mask).astype(F32)).astype(value.dtype)
    return value


def bits_of(axis, size):
    found, mask = [], 1
    while mask < size:
        found.append((axis, size, mask, (lax.axis_index(axis) // mask) % 2))
        mask *= 2
    return found


def per_device(
    seq_size, row_size,
    block_input, segment_ids, ln1_gain, ln1_shift, w_qkv, bias_query, bias_value, w_out, bias_out,
    ln2_gain, ln2_shift, w_up, bias_up, w_down, bias_down, out_grad,
):
    rows, band, width = block_input.shape
    length = segment_ids.shape[1]
    share = seq_size // rows
    tokens = rows * band
    crops = max(length // (4 * band), 1)
    place = lax.axis_index("seq")
    my_row, my_part = place // share, place % share

    def deal(pieces):
        got = [pieces[0]]
        for j in range(1, rows):
            turn = [(s, ((s // share) ^ j) * share + s % share) for s in range(seq_size)]
            got.append(lax.ppermute(pieces[j], "seq", turn))
        return got

    def pick(array):
        return [lax.dynamic_index_in_dim(array, my_row ^ j, 0, False) for j in range(rows)]

    xs = deal(pick(block_input))
    dys = deal(pick(out_grad))

    own_row = lax.dynamic_index_in_dim(segment_ids, my_row, 0, False).reshape(seq_size, band)
    key_ids = jnp.concatenate(
        [
            lax.dynamic_index_in_dim(own_row, (my_row ^ j) * share + (my_part ^ i), 0, False)
            for i in range(share)
            for j in range(rows)
        ]
    )
    spot = jnp.arange(128) % 64
    same = key_ids[:, None] == spot[None, :]
    used = spot[None, :] < crops
    ones = (spot >= LSE_LANE) & (spot < LSE_LANE + 3)
    kf = jnp.where(used, jnp.where(same, 0.0, -1.0), jnp.where(ones, 1.0, 0.0)).astype(BF16)
    qf = jnp.where(used & same, BIG, 0.0).astype(BF16)[:tokens]

    row_of = lambda v: v.reshape(1, -1)
    shape = jax.ShapeDtypeStruct
    normed, q, kv = pl.pallas_call(
        functools.partial(qkv_kernel, rows, width),
        out_shape=[
            shape((tokens, width), BF16),
            shape((tokens, width), BF16),
            shape((tokens, 2 * width), BF16),
        ],
        compiler_params=pltpu.CompilerParams(vmem_limit_bytes=VMEM_LIMIT),
        name="norm_and_project",
    )(*xs, row_of(ln1_gain), row_of(ln1_shift), w_qkv, row_of(bias_query), row_of(bias_value))

    seq_bits = bits_of("seq", seq_size)
    row_bits = bits_of("row", row_size)
    part_bits = [bit for bit in seq_bits if bit[2] < share]
    kvs, whole = [kv], kv
    for axis, size, mask, own in part_bits:
        got = swap(whole, axis, size, mask)
        kvs.append(got)
        if mask * 2 < share:
            whole = jnp.concatenate([whole, got], 0)

    mix, qfb = attention_forward(q, kvs, qf, kf)
    (out, mixed, two, active, grad_hidden, grad_attn, grad_middle, gm, gmf, vec, dy) = middle_part(
        xs, dys, mix, w_out, row_of(bias_out), row_of(ln2_gain), row_of(ln2_shift),
        w_up, row_of(bias_up), w_down, row_of(bias_down),
    )

    bits = seq_bits + row_bits
    cut, rest = bits[:5], bits[5:]
    turned = [cut[0], cut[2], cut[1]] + cut[3:]
    grad_down = dot_tn(active, dy).astype(BF16)
    grad_up_out = jnp.concatenate(
        [dot_tn(two, grad_hidden).astype(BF16), dot_tn(mixed, grad_attn).astype(BF16)], axis=1
    )

    dq, dks, dvs = attention_backward(q, gm, qfb, gmf, kvs, kf, 0, width // 128)

    if share == 2:
        axis, size, mask, own = part_bits[0]
        got = swap(jnp.concatenate([dks[1], dvs[1]], axis=1), axis, size, mask)
        dk = (dks[0] + got[:, :width].astype(F32)).astype(BF16)
        dv = (dvs[0] + got[:, width:].astype(F32)).astype(BF16)
    else:
        both = jnp.concatenate(
            [jnp.concatenate([part.astype(BF16) for part in terms], 0) for terms in (dks, dvs)], axis=1
        )
        for axis, size, mask, own in reversed(part_bits):
            half = both.shape[0] // 2
            both = (both[:half].astype(F32) + swap(both[half:], axis, size, mask).astype(F32)).astype(BF16)
        dk, dv = both[:, :width], both[:, width:]

    grad_w_qkv = jnp.concatenate([dot_tn(normed, part).astype(BF16) for part in (dq, dk, dv)], axis=1)

    input_grad, vec_last = pl.pallas_call(
        functools.partial(last_kernel, rows),
        out_shape=[shape((tokens, width), BF16), shape((8, width), F32)],
        compiler_params=pltpu.CompilerParams(vmem_limit_bytes=VMEM_LIMIT),
        name="norm_one_back",
    )(*xs, dq, dk, dv, grad_middle, row_of(ln1_gain), w_qkv)

    def reduce_all(value, order):
        return gather_back(exchange_sum(scatter_sum(value, order), rest), order).astype(F32)

    def back(value):
        got = deal([value[j * band : (j + 1) * band] for j in range(rows)])
        stacked = jnp.stack(got)
        return jnp.stack([lax.dynamic_index_in_dim(stacked, my_row ^ j, 0, False) for j in range(rows)])

    sum_down = reduce_all(grad_down, cut)
    sum_up_out = reduce_all(grad_up_out, turned)
    sum_qkv = reduce_all(grad_w_qkv, cut)
    ff = w_up.shape[1]
    vectors = jnp.concatenate([vec[0], vec[1:5, :width].reshape(-1), vec_last[:4].reshape(-1)])
    vectors = exchange_sum(vectors.reshape(-1, 512), bits).reshape(-1)
    cuts = [ff + i * width for i in range(9)]
    bias_up_sum = vectors[:ff]
    ln2_gain_sum, ln2_shift_sum, bias_down_sum, bias_out_sum, bias_q_sum, bias_v_sum, ln1_gain_sum, ln1_shift_sum = [
        vectors[a:b] for a, b in zip(cuts[:-1], cuts[1:])
    ]
    return (
        back(out),
        back(input_grad),
        ln1_gain_sum,
        ln1_shift_sum,
        sum_qkv,
        bias_q_sum,
        bias_v_sum,
        sum_up_out[:, ff:],
        bias_out_sum,
        ln2_gain_sum,
        ln2_shift_sum,
        sum_up_out[:, :ff],
        bias_up_sum,
        sum_down,
        bias_down_sum,
    )


def solution(mesh):
    split = P("row", "seq", None)
    placed = (split, P("row", None)) + (P(),) * 13 + (split,)
    return jax.shard_map(
        functools.partial(per_device, mesh.shape["seq"], mesh.shape["row"]),
        mesh=mesh,
        in_specs=placed,
        out_specs=(split, split) + (P(),) * 13,
        check_vma=False,
    )
```

```python
import functools

import jax
import jax.numpy as jnp
from jax import lax
from jax.experimental import pallas as pl
from jax.experimental.pallas import tpu as pltpu
from jax.sharding import PartitionSpec as P

HEADS = 8
EPSILON = 1e-06
BIG = 1e30
LSE_LANE = 16
PIECES = 16
SCHEDULE = (
    "D", "U", "d", "b", "b", "d", "w0", "u", "w1", "b", "d", "b", "d", "u", "G", "u",
    "wd", "o", "L", "wq", "d", "u", "wo", "q", "O", "d", "q", "u", "d", "q", "u", "q",
    "d", "u", "q", "d", "q", "u", "q", "u", "i", "q", "q", "I",
)
VECTOR_LANES = 128
F32 = jnp.float32
BF16 = jnp.bfloat16
MIB = 1024 * 1024
VMEM_LIMIT = 24 * MIB
LN1_GAIN, LN1_SHIFT, BIAS_Q, BIAS_V, BIAS_OUT, LN2_GAIN, LN2_SHIFT, BIAS_DOWN = (
    slice(i, i + 1) for i in range(8)
)
BIAS_UP = 8


def dot_nn(a, b):
    return lax.dot_general(a, b, (((1,), (0,)), ((), ())), preferred_element_type=F32)


def dot_nt(a, b):
    return lax.dot_general(a, b, (((1,), (1,)), ((), ())), preferred_element_type=F32)


def dot_tn(a, b):
    return lax.dot_general(a, b, (((0,), (0,)), ((), ())), preferred_element_type=F32)


def split_three(value):
    high = value.astype(BF16)
    rest = value - high.astype(F32)
    middle = rest.astype(BF16)
    low = (rest - middle.astype(F32)).astype(BF16)
    return high, middle, low


def lane_index(shape):
    return lax.broadcasted_iota(jnp.int32, shape, len(shape) - 1)


def three_lanes(value, lanes):
    high, middle, low = split_three(value)
    spot = lanes % 64
    out = jnp.where(spot == LSE_LANE, high.astype(F32), 0.0)
    out = jnp.where(spot == LSE_LANE + 1, middle.astype(F32), out)
    return jnp.where(spot == LSE_LANE + 2, low.astype(F32), out)


def norm_parts(value):
    centre = jnp.mean(value, axis=-1, keepdims=True)
    centred = value - centre
    spread = jnp.mean(centred * centred, axis=-1, keepdims=True)
    scale = lax.rsqrt(spread + EPSILON)
    return centred * scale, scale


def norm_back(grad, unit, scale, gain):
    grad_unit = grad * gain
    first = jnp.mean(grad_unit, axis=-1, keepdims=True)
    second = jnp.mean(grad_unit * unit, axis=-1, keepdims=True)
    return scale * (grad_unit - first - unit * second)


def qkv_kernel(pieces, width, *refs):
    x_refs = refs[:pieces]
    small, w_ref, normed_ref, q_ref, kv_ref = refs[pieces:]
    band = x_refs[0].shape[0]
    for j in range(pieces):
        unit, _ = norm_parts(x_refs[j][...].astype(F32))
        normed_ref[j * band : (j + 1) * band, :] = (unit * small[LN1_GAIN] + small[LN1_SHIFT]).astype(BF16)
    normed = normed_ref[...]
    q = dot_nn(normed, w_ref[:, :width])
    q_ref[...] = ((q + small[BIAS_Q]) * (width // HEADS) ** -0.5).astype(BF16)
    kv_ref[:, :width] = dot_nn(normed, w_ref[:, width : 2 * width]).astype(BF16)
    kv_ref[:, width:] = (dot_nn(normed, w_ref[:, 2 * width :]) + small[BIAS_V]).astype(BF16)


def forward_kernel(parts, rows, *refs):
    q_ref = refs[0]
    k_refs = refs[1 : 1 + parts]
    v_refs = refs[1 + parts : 1 + 2 * parts]
    qf_ref, kf_ref, mix_ref, qfb_ref, k_aug, v_aug = refs[1 + 2 * parts :]
    tokens = q_ref.shape[0]
    low_half = (lane_index((1, 128)) < 64).astype(F32)
    halves = (low_half.astype(BF16), (1.0 - low_half).astype(BF16))
    for parity in range(2):
        mine, other = halves[parity], halves[1 - parity]
        start = 0
        for k_ref, v_ref in zip(k_refs, v_refs):
            stop = start + k_ref.shape[0]
            k_aug[parity, start:stop, :] = k_ref[...] * mine + kf_ref[start:stop, :] * other
            v_aug[parity, start:stop, :] = v_ref[...] * mine + other
            start = stop
    lanes = lane_index((rows, 128))
    low = lanes < 64

    def block(step, carry):
        at = pl.ds(pl.multiple_of(step * rows, rows), rows)
        q = q_ref[at, :]
        qf = qf_ref[at, :]
        sums, tops = [], []
        for parity in range(2):
            mine, other = halves[parity], halves[1 - parity]
            scores = dot_nt(q * mine + qf * other, k_aug[parity])
            top = jnp.max(scores, axis=-1, keepdims=True)
            exps = jnp.exp(scores - top).astype(BF16)
            sums.append(dot_nn(exps, v_aug[parity]))
            tops.append(jnp.broadcast_to(top, (rows, 128)))
        total = jnp.where(low, sums[1], sums[0])
        mix_ref[at, :] = jnp.where(low, sums[0], sums[1]) / pltpu.roll(total, 64, 1)
        log_total = jnp.where(low, tops[1], tops[0]) + jnp.log(total)
        qfb_ref[at, :] = (qf.astype(F32) + three_lanes(-log_total, lanes)).astype(BF16)
        return carry

    lax.fori_loop(0, tokens // rows, block, 0)


def attention_forward(q, kvs, qf, kf, rows=512):
    tokens, width = q.shape
    pairs = width // 128
    length = kf.shape[0]
    parts = len(kvs)
    in_specs = [pl.BlockSpec((tokens, 128), lambda h: (0, h))]
    in_specs += [pl.BlockSpec((kv.shape[0], 128), lambda h: (0, h)) for kv in kvs]
    in_specs += [pl.BlockSpec((kv.shape[0], 128), lambda h: (0, pairs + h)) for kv in kvs]
    in_specs += [
        pl.BlockSpec((tokens, 128), lambda h: (0, 0)),
        pl.BlockSpec((length, 128), lambda h: (0, 0)),
    ]
    return pl.pallas_call(
        functools.partial(forward_kernel, parts, rows),
        grid=(pairs,),
        in_specs=in_specs,
        out_specs=[
            pl.BlockSpec((tokens, 128), lambda h: (0, h)),
            pl.BlockSpec((tokens, 128), lambda h: (0, h)),
        ],
        out_shape=[
            jax.ShapeDtypeStruct((tokens, width), F32),
            jax.ShapeDtypeStruct((tokens, width), BF16),
        ],
        scratch_shapes=[pltpu.VMEM((2, length, 128), BF16), pltpu.VMEM((2, length, 128), BF16)],
        compiler_params=pltpu.CompilerParams(vmem_limit_bytes=VMEM_LIMIT),
        name="attention_forward",
        cost_estimate=pl.CostEstimate(
            flops=4 * tokens * length * width, bytes_accessed=8 * tokens * width,
            transcendentals=tokens * length * HEADS,
        ),
    )(q, *kvs, *kvs, qf, kf)


def backward_kernel(parts, rows, *refs):
    q_ref, gm_ref, qfb_ref, gmf_ref = refs[:4]
    k_refs = refs[4 : 4 + parts]
    v_refs = refs[4 + parts : 4 + 2 * parts]
    kf_ref = refs[4 + 2 * parts]
    rest = refs[5 + 2 * parts :]
    dq_ref = rest[0]
    pair_refs = rest[1 : 1 + parts]
    q_aug, gm_aug, dqt = rest[1 + parts :]
    low_half = (lane_index((1, 128)) < 64).astype(F32)
    halves = (low_half.astype(BF16), (1.0 - low_half).astype(BF16))
    for parity in range(2):
        mine, other = halves[parity], halves[1 - parity]
        q_aug[parity] = q_ref[...] * mine + qfb_ref[...] * other
        gm_aug[parity] = gm_ref[...] * mine + gmf_ref[...] * other
    dqt[...] = jnp.zeros_like(dqt)
    low = lane_index((rows, 128)) < 64
    start = 0
    for k_ref, v_ref, pair_ref in zip(k_refs, v_refs, pair_refs):

        def block(step, carry, start=start, k_ref=k_ref, v_ref=v_ref, pair_ref=pair_ref):
            at = pl.ds(pl.multiple_of(step * rows, rows), rows)
            at_all = pl.ds(pl.multiple_of(start + step * rows, rows), rows)
            k, v, kf = k_ref[at, :], v_ref[at, :], kf_ref[at_all, :]
            dks, dvs = [], []
            for parity in range(2):
                mine, other = halves[parity], halves[1 - parity]
                k_aug = k * mine + kf * other
                v_aug = v * mine + other
                probs = jnp.exp(dot_nt(k_aug, q_aug[parity]))
                slopes = dot_nt(v_aug, gm_aug[parity])
                grads = (probs * slopes).astype(BF16)
                dvs.append(dot_nn(probs.astype(BF16), gm_ref[...]))
                dks.append(dot_nn(grads, q_ref[...]))
                dqt[parity] += dot_tn(k, grads)
            pair_ref[at, :128] = jnp.where(low, dks[0], dks[1]).astype(pair_ref.dtype)
            pair_ref[at, 128:] = jnp.where(low, dvs[0], dvs[1]).astype(pair_ref.dtype)
            return carry

        lax.fori_loop(0, k_ref.shape[0] // rows, block, 0)
        start += k_ref.shape[0]
    dq_t = jnp.concatenate([dqt[0, :64, :], dqt[1, 64:, :]], axis=0)
    dq_ref[...] = dq_t.T.astype(BF16) * (64.0**-0.5)


def attention_backward(q, gm, qfb, gmf, kvs, kf, pair, rows=512):
    tokens, width = q.shape
    pairs = width // 128
    length = kf.shape[0]
    parts = len(kvs)
    of_pair = lambda i: (0, pair)
    in_specs = [pl.BlockSpec((tokens, 128), of_pair)] * 4
    in_specs += [pl.BlockSpec((kv.shape[0], 128), of_pair) for kv in kvs]
    in_specs += [pl.BlockSpec((kv.shape[0], 128), lambda i: (0, pairs + pair)) for kv in kvs]
    in_specs += [pl.BlockSpec((length, 128), lambda i: (0, 0))]
    kinds = [F32] + [BF16] * (parts - 1)
    outs = [jax.ShapeDtypeStruct((tokens, 128), BF16)]
    outs += [jax.ShapeDtypeStruct((kv.shape[0], 256), kind) for kv, kind in zip(kvs, kinds)]
    return pl.pallas_call(
        functools.partial(backward_kernel, parts, rows),
        grid=(1,),
        in_specs=in_specs,
        out_specs=[pl.BlockSpec(out.shape, lambda i: (0, 0)) for out in outs],
        out_shape=outs,
        scratch_shapes=[
            pltpu.VMEM((2, tokens, 128), BF16),
            pltpu.VMEM((2, tokens, 128), BF16),
            pltpu.VMEM((2, 128, tokens), F32),
        ],
        compiler_params=pltpu.CompilerParams(vmem_limit_bytes=VMEM_LIMIT),
        name="attention_backward",
        cost_estimate=pl.CostEstimate(
            flops=10 * tokens * length * 128, bytes_accessed=12 * tokens * 128,
            transcendentals=tokens * length * 2,
        ),
    )(q, gm, qfb, gmf, *kvs, *kvs, kf)


def middle_kernel(pieces, rows, *refs):
    x_refs = refs[:pieces]
    dy_refs = refs[pieces : 2 * pieces]
    mix_ref, small, w_out, w_up, w_down = refs[2 * pieces : 2 * pieces + 5]
    outs = refs[2 * pieces + 5 :]
    gain, shift = small[LN2_GAIN], small[LN2_SHIFT]
    out_refs = outs[:pieces]
    (mixed_ref, two_ref, active_ref, gh_ref, ga_ref, gmid_ref, gm_ref, gmf_ref, vec_ref, dy_ref) = outs[pieces:]
    band = x_refs[0].shape[0]
    tokens, width = mix_ref.shape
    ff = w_up.shape[1]
    vec_ref[...] = jnp.zeros_like(vec_ref)
    c0 = 0.7978845608028654
    c1 = 0.044715
    row = lax.broadcasted_iota(jnp.int32, (width, width), 0) // 64
    column = lane_index((width, width)) // 64
    opposite = (row == (column + 1 - 2 * (column % 2))).astype(F32).astype(BF16)
    per = rows // band
    for t in range(tokens // rows):
        at = slice(t * rows, (t + 1) * rows)
        x = jnp.concatenate([x_refs[t * per + j][...] for j in range(per)], axis=0).astype(F32)
        dy = jnp.concatenate([dy_refs[t * per + j][...] for j in range(per)], axis=0)
        dy_ref[at, :] = dy
        mix = mix_ref[at, :]
        mixed = mix.astype(BF16)
        mixed_ref[at, :] = mixed
        middle = x + (dot_nn(mixed, w_out[...]) + small[BIAS_OUT])
        unit, scale = norm_parts(middle)
        two = (unit * gain + shift).astype(BF16)
        two_ref[at, :] = two
        out = middle + small[BIAS_DOWN]
        grad_two = jnp.zeros((rows, width), F32)
        step = width
        for f in range(0, ff, step):
            fs = slice(f, f + step)
            hidden = dot_nn(two, w_up[:, fs]) + small[BIAS_UP + f // step : BIAS_UP + f // step + 1]
            square = hidden * hidden
            tanh = jnp.tanh(c0 * hidden * (1.0 + c1 * square))
            half = 0.5 * (1.0 + tanh)
            active = (hidden * half).astype(BF16)
            active_ref[at, fs] = active
            out = out + dot_nn(active, w_down[fs, :])
            slope = half + hidden * (0.5 * (1.0 - tanh * tanh)) * (c0 + (3.0 * c0 * c1) * square)
            grad = dot_nt(dy, w_down[fs, :]) * slope
            grad_low = grad.astype(BF16)
            gh_ref[at, fs] = grad_low
            vec_ref[0:1, fs] += jnp.sum(grad_low.astype(F32), axis=0, keepdims=True)
            grad_two = grad_two + dot_nt(grad_low, w_up[:, fs])
        for j in range(per):
            out_refs[t * per + j][...] = out[j * band : (j + 1) * band].astype(BF16)
        dy_wide = dy.astype(F32)
        grad_middle = dy_wide + norm_back(grad_two, unit, scale, gain)
        gmid_ref[at, :] = grad_middle
        vec_ref[1:2, :width] += jnp.sum(grad_two * unit, axis=0, keepdims=True)
        vec_ref[2:3, :width] += jnp.sum(grad_two, axis=0, keepdims=True)
        vec_ref[3:4, :width] += jnp.sum(dy_wide, axis=0, keepdims=True)
        grad_attn = grad_middle.astype(BF16)
        ga_ref[at, :] = grad_attn
        vec_ref[4:5, :width] += jnp.sum(grad_attn.astype(F32), axis=0, keepdims=True)
        gm = dot_nt(grad_attn, w_out[...]).astype(BF16)
        gm_ref[at, :] = gm
        high, mid, low = split_three(gm.astype(F32) * mix)
        inner = dot_nn(high, opposite) + (dot_nn(mid, opposite) + dot_nn(low, opposite))
        gmf_ref[at, :] = three_lanes(-inner, lane_index((rows, width))).astype(BF16)


def middle_part(xs, dys, mix, small, w_out, w_up, w_down, rows=512):
    tokens, width = mix.shape
    ff = w_up.shape[1]
    shape = jax.ShapeDtypeStruct
    return pl.pallas_call(
        functools.partial(middle_kernel, len(xs), rows),
        out_shape=[shape(x.shape, BF16) for x in xs]
        + [
            shape((tokens, width), BF16),
            shape((tokens, width), BF16),
            shape((tokens, ff), BF16),
            shape((tokens, ff), BF16),
            shape((tokens, width), BF16),
            shape((tokens, width), F32),
            shape((tokens, width), BF16),
            shape((tokens, width), BF16),
            shape((8, ff), F32),
            shape((tokens, width), BF16),
        ],
        compiler_params=pltpu.CompilerParams(vmem_limit_bytes=VMEM_LIMIT),
        name="middle_part",
        cost_estimate=pl.CostEstimate(
            flops=2 * tokens * width * (4 * ff + 5 * width), bytes_accessed=8 * 1024 * 1024,
            transcendentals=tokens * ff,
        ),
    )(*xs, *dys, mix, small, w_out, w_up, w_down)


def split_at(columns):
    return columns // 256 * 128


def place_pieces(marks, total, keep_ref, send_ref):
    piece = total.shape[0] // PIECES
    middle = split_at(total.shape[1])
    for which, target in enumerate((keep_ref, send_ref)):
        for part, columns in enumerate((slice(0, middle), slice(middle, total.shape[1]))):
            for j in range(PIECES // 2):
                source = pl.multiple_of((marks[2 * which + part] ^ j) * piece, piece)
                spot = slice(j * piece, (j + 1) * piece)
                target[spot, columns] = total[pl.ds(source, piece), columns].astype(BF16)


def smem():
    return pl.BlockSpec(memory_space=pltpu.SMEM)


def vmem():
    return pl.BlockSpec(memory_space=pltpu.VMEM)


def weight_grad_kernel(count, marks, *refs):
    pairs = refs[: 2 * count]
    keep_ref, send_ref, total = refs[2 * count :]
    start = 0
    for left, right in zip(pairs[0::2], pairs[1::2]):
        stop = start + right.shape[1]
        for r in range(0, left.shape[1], 256):
            total[r : r + 256, start:stop] = dot_tn(left[:, r : r + 256], right[...])
        start = stop
    place_pieces(marks, total, keep_ref, send_ref)


def weight_grad(marks, pairs, name):
    rows = pairs[0][0].shape[1]
    columns = sum(right.shape[1] for _, right in pairs)
    depth = pairs[0][0].shape[0]
    half = jax.ShapeDtypeStruct((rows // 2, columns), BF16)
    flat = [array for pair in pairs for array in pair]
    return pl.pallas_call(
        functools.partial(weight_grad_kernel, len(pairs)),
        in_specs=[smem()] + [vmem()] * len(flat),
        out_specs=[vmem(), vmem()],
        out_shape=[half, half],
        scratch_shapes=[pltpu.VMEM((rows, columns), F32)],
        compiler_params=pltpu.CompilerParams(vmem_limit_bytes=VMEM_LIMIT),
        name=name,
        cost_estimate=pl.CostEstimate(
            flops=2 * rows * columns * depth, bytes_accessed=6 * rows * columns, transcendentals=0
        ),
    )(marks, *flat)


def qkv_grad_kernel(pairs, *refs):
    marks, normed, small, w_ref, vec_ref = refs[:5]
    dqs, owns, gots = (refs[5 + i * pairs : 5 + (i + 1) * pairs] for i in range(3))
    packed, keep_ref, send_ref, total = refs[5 + 3 * pairs :]
    width = normed.shape[1]
    for h in range(pairs):
        packed[:, 128 * h : 128 * (h + 1)] = dqs[h][...]
        both = (owns[h][...] + gots[h][...].astype(F32)).astype(BF16)
        for i in range(2):
            at = (i + 1) * width + 128 * h
            packed[:, at : at + 128] = both[:, 128 * i : 128 * (i + 1)]
    for r in range(0, width, 256):
        total[r : r + 256, : 3 * width] = dot_tn(normed[:, r : r + 256], packed[...])
    sums = jnp.sum(packed[...].astype(F32), axis=0, keepdims=True)
    terms = jnp.concatenate(split_three(jnp.broadcast_to(sums, (16, 3 * width))), axis=0)
    spread = dot_nt(terms, w_ref[...])
    shift_row = spread[0:1] + (spread[16:17] + spread[32:33])
    rows = jnp.zeros((width, 128), F32)
    for at in range(0, 3 * width, 128):
        rows = rows + total[:, at : at + 128] * w_ref[:, at : at + 128].astype(F32)
    gain_row = jnp.sum(rows.T, axis=0, keepdims=True)
    gain_row = (gain_row - small[LN1_SHIFT] * shift_row) / small[LN1_GAIN]
    vectors = [vec_ref[0:1, :]] + [vec_ref[i : i + 1, :width] for i in range(1, 5)]
    vectors += [sums[:, :width], sums[:, 2 * width :], gain_row, shift_row]
    tiles = [row[:, at : at + VECTOR_LANES] for row in vectors for at in range(0, row.shape[1], VECTOR_LANES)]
    piece = width // PIECES
    per = len(tiles) // PIECES
    total[:, 3 * width :] = jnp.zeros((width, VECTOR_LANES), F32)
    for i, tile in enumerate(tiles):
        at = (i // per) * piece + i % per
        total[at : at + 1, 3 * width :] = tile
    place_pieces(marks, total, keep_ref, send_ref)


def qkv_grad(marks, normed, small, w_qkv, vec, dqs, owns, gots):
    tokens, width = normed.shape
    columns = 3 * width + VECTOR_LANES
    half = jax.ShapeDtypeStruct((width // 2, columns), BF16)
    flat = [normed, small, w_qkv, vec, *dqs, *owns, *gots]
    return pl.pallas_call(
        functools.partial(qkv_grad_kernel, len(dqs)),
        in_specs=[smem()] + [vmem()] * len(flat),
        out_specs=[vmem()] * 3,
        out_shape=[jax.ShapeDtypeStruct((tokens, 3 * width), BF16), half, half],
        scratch_shapes=[pltpu.VMEM((width, columns), F32)],
        compiler_params=pltpu.CompilerParams(vmem_limit_bytes=VMEM_LIMIT),
        name="qkv_grad",
        cost_estimate=pl.CostEstimate(
            flops=6 * tokens * width * width, bytes_accessed=18 * tokens * width, transcendentals=0
        ),
    )(marks, *flat)


def last_kernel(pieces, *refs):
    packed, gmid_ref, small, w_ref = refs[:4]
    x_refs, out_refs = refs[4 : 4 + pieces], refs[4 + pieces :]
    band = x_refs[0].shape[0]
    grad = dot_nt(packed[...], w_ref[...])
    x = jnp.concatenate([ref[...] for ref in x_refs], axis=0).astype(F32)
    unit, scale = norm_parts(x)
    result = (gmid_ref[...] + norm_back(grad, unit, scale, small[LN1_GAIN])).astype(BF16)
    for j in range(pieces):
        out_refs[j][...] = result[j * band : (j + 1) * band]


def last_part(packed, gmid, small, w_qkv, xs):
    tokens, width = gmid.shape
    return pl.pallas_call(
        functools.partial(last_kernel, len(xs)),
        out_shape=[jax.ShapeDtypeStruct(x.shape, BF16) for x in xs],
        compiler_params=pltpu.CompilerParams(vmem_limit_bytes=VMEM_LIMIT),
        name="last_part",
        cost_estimate=pl.CostEstimate(
            flops=6 * tokens * width * width, bytes_accessed=10 * tokens * width, transcendentals=0
        ),
    )(packed, gmid, small, w_qkv, *xs)


def assemble_kernel(segments, per, marks, *refs):
    parts, out_refs = refs[:4], refs[4:]
    half = PIECES // 2
    piece = parts[0].shape[0] // half
    middle = parts[0].shape[1]
    step = pl.program_id(0)
    for i in range(per):
        index = step * per + i

        def fill(which, i=i, index=index):
            for part in range(2):
                source = parts[2 * which + part]
                at = pl.ds(pl.multiple_of(((index ^ marks[2 * which + part]) % half) * piece, piece), piece)
                low, high = part * middle, part * middle + source.shape[1]
                for start, stop, which_out, tall, offset in segments:
                    first, last = max(start, low), min(stop, high)
                    if first < last:
                        spot = slice(i * tall + offset, i * tall + offset + piece)
                        out_refs[which_out][spot, first - start : last - start] = source[
                            at, first - low : last - low
                        ].astype(F32)

        mine = index // half == marks[0] // half
        pl.when(mine)(functools.partial(fill, 0))
        pl.when(jnp.logical_not(mine))(functools.partial(fill, 1))


def assemble(marks, parts, segments, shapes, name):
    steps = 2
    per = PIECES // steps
    size = sum(rows * columns for rows, columns in shapes)
    return pl.pallas_call(
        functools.partial(assemble_kernel, segments, per),
        grid=(steps,),
        in_specs=[smem()] + [vmem()] * 4,
        out_specs=[pl.BlockSpec((rows // steps, w), lambda i: (i, 0)) for rows, w in shapes],
        out_shape=[jax.ShapeDtypeStruct(shape, F32) for shape in shapes],
        compiler_params=pltpu.CompilerParams(vmem_limit_bytes=VMEM_LIMIT),
        name=name,
        cost_estimate=pl.CostEstimate(flops=size, bytes_accessed=6 * size, transcendentals=0),
    )(marks, *parts)


def return_kernel(pieces, row_ref, *refs):
    for j in range(pieces):
        refs[pieces][row_ref[0] ^ j] = refs[j][...]


def return_rows(row, got):
    return pl.pallas_call(
        functools.partial(return_kernel, len(got)),
        in_specs=[smem()] + [vmem()] * len(got),
        out_specs=vmem(),
        out_shape=jax.ShapeDtypeStruct((len(got), *got[0].shape), BF16),
        name="return_rows",
    )(row, *got)


def swap(value, axis, size, mask):
    return lax.ppermute(value, axis, [(i, i ^ mask) for i in range(size)])


class Order:
    def __init__(self):
        self.last = ()

    def enter(self, *values):
        return lax.optimization_barrier((values, self.last))[0]

    def leave(self, *values):
        self.last = values


class Wave:
    def __init__(self, order, keep, send, marks, layout, core, ways, deep, rest):
        self.order, self.core, self.ways, self.deep, self.rest = order, core, ways, deep, rest
        self.marks, self.layout = marks, layout
        self.middle = split_at(keep.shape[1])
        self.value, self.got = keep, core(send)
        order.leave(send)

    def columns(self, value):
        return [value[:, : self.middle], value[:, self.middle :]]

    def plane(self, step):
        if step == 0:
            value, got = self.order.enter(self.value, self.got)
            parts = self.columns(add_low(value, got))
        else:
            parts = self.added()
        half = parts[0].shape[0] // 2
        self.value = [part[:half] for part in parts]
        sent = [part[half:] for part in parts]
        self.got = [self.ways[(step + i) % 2](part) for i, part in enumerate(sent)]
        self.order.leave(*sent)

    def added(self):
        values = self.order.enter(*self.value, *self.got)
        return [add_low(one, two) for one, two in zip(values[:2], values[2:])]

    def line(self):
        parts = self.added()
        half = parts[0].shape[0] // 2
        self.value = jnp.concatenate([part[:half] for part in parts], axis=1)
        sent = jnp.concatenate([part[half:] for part in parts], axis=1)
        self.got = self.deep(sent)
        self.order.leave(sent)

    def exchanges(self):
        for send in self.rest:
            value, got = self.order.enter(self.value, self.got)
            self.value = add_low(value, got)
            self.got = send(self.value)
            self.order.leave(self.value)

    def line_back(self):
        value, got = self.order.enter(self.value, self.got)
        self.value = add_low(value, got)
        self.got = self.deep(self.value)
        self.order.leave(self.value)

    def plane_back(self, step):
        if step == 1:
            value, got = self.order.enter(self.value, self.got)
            self.value = self.columns(jnp.concatenate([value, got], axis=0))
        else:
            self.value = self.joined()
        self.got = [self.ways[(step + i) % 2](part) for i, part in enumerate(self.value)]
        self.order.leave(*self.value)

    def joined(self):
        values = self.order.enter(*self.value, *self.got)
        return [jnp.concatenate(pair, axis=0) for pair in zip(values[:2], values[2:])]

    def core_back(self):
        self.value = self.joined()
        self.got = [self.core(part) for part in self.value]
        self.order.leave(*self.value)

    def wait(self):
        if isinstance(self.got, list):
            self.got = list(self.order.enter(*self.got))
            self.order.leave(*self.got)
        else:
            (self.got,) = self.order.enter(self.got)
            self.order.leave(self.got)

    def finish(self):
        parts = self.order.enter(*self.value, *self.got)
        self.sums = assemble(self.marks, parts, *self.layout)
        self.order.leave(*self.sums)

    def steps(self):
        yield functools.partial(self.plane, 0)
        yield functools.partial(self.plane, 1)
        yield self.line
        yield self.exchanges
        yield self.line_back
        yield functools.partial(self.plane_back, 1)
        yield functools.partial(self.plane_back, 0)
        yield self.core_back
        yield self.finish


def add_low(one, two):
    return (one.astype(F32) + two.astype(F32)).astype(BF16)


def after(value, *others):
    return lax.optimization_barrier((value, others))[0]


def bits_of(axis, size):
    found, mask = [], 1
    while mask < size:
        found.append((axis, size, mask, (lax.axis_index(axis) // mask) % 2))
        mask *= 2
    return found


def per_device(
    seq_size, row_size,
    block_input, segment_ids, ln1_gain, ln1_shift, w_qkv, bias_query, bias_value, w_out, bias_out,
    ln2_gain, ln2_shift, w_up, bias_up, w_down, bias_down, out_grad,
):
    rows, band, width = block_input.shape
    length = segment_ids.shape[1]
    share = seq_size // rows
    tokens = rows * band
    crops = max(length // (4 * band), 1)
    place = lax.axis_index("seq")
    my_row, my_part = place // share, place % share

    def deal(pieces):
        got = [pieces[0]]
        for j in range(1, rows):
            turn = [(s, ((s // share) ^ j) * share + s % share) for s in range(seq_size)]
            got.append(lax.ppermute(pieces[j], "seq", turn))
        return got

    def pick(array):
        return [lax.dynamic_index_in_dim(array, my_row ^ j, 0, False) for j in range(rows)]

    xs = deal(pick(block_input))
    dys = pick(out_grad)

    own_row = lax.dynamic_index_in_dim(segment_ids, my_row, 0, False).reshape(seq_size, band)
    key_ids = jnp.concatenate(
        [
            lax.dynamic_index_in_dim(own_row, (my_row ^ j) * share + (my_part ^ i), 0, False)
            for i in range(share)
            for j in range(rows)
        ]
    )
    spot = jnp.arange(128) % 64
    same = key_ids[:, None] == spot[None, :]
    used = spot[None, :] < crops
    ones = (spot >= LSE_LANE) & (spot < LSE_LANE + 3)
    kf = jnp.where(used, jnp.where(same, 0.0, -1.0), jnp.where(ones, 1.0, 0.0)).astype(BF16)
    qf = jnp.where(used & same, BIG, 0.0).astype(BF16)[:tokens]

    small = jnp.stack(
        [ln1_gain, ln1_shift, bias_query, bias_value, bias_out, ln2_gain, ln2_shift, bias_down]
    )
    small = jnp.concatenate([small, bias_up.reshape(-1, width)], axis=0)
    shape = jax.ShapeDtypeStruct
    normed, q, kv = pl.pallas_call(
        functools.partial(qkv_kernel, rows, width),
        out_shape=[
            shape((tokens, width), BF16),
            shape((tokens, width), BF16),
            shape((tokens, 2 * width), BF16),
        ],
        compiler_params=pltpu.CompilerParams(vmem_limit_bytes=VMEM_LIMIT),
        name="norm_and_project",
    )(*xs, small, w_qkv)

    dys = deal(lax.optimization_barrier((dys, xs))[0])
    seq_bits = bits_of("seq", seq_size)
    row_bits = bits_of("row", row_size)
    part_bits = [bit for bit in seq_bits if bit[2] < share]
    kvs, whole = [kv], kv
    for axis, size, mask, own in part_bits:
        got = swap(whole, axis, size, mask)
        kvs.append(got)
        if mask * 2 < share:
            whole = jnp.concatenate([whole, got], 0)

    mix, qfb = attention_forward(q, kvs, qf, kf)
    *outs, mixed, two, active, grad_hidden, grad_attn, grad_middle, gm, gmf, vec, dy = middle_part(
        xs, dys, mix, small, w_out, w_up, w_down
    )

    def straight(bit):
        return lambda value: swap(value, *bit[:3])

    core, one, two_, deep = seq_bits[0][3], seq_bits[1][3], seq_bits[2][3], row_bits[0][3]
    ways = (straight(seq_bits[1]), straight(seq_bits[2]))
    rest = [straight(bit) for bit in row_bits[1:] + seq_bits[3:]]
    route = (straight(seq_bits[0]), ways, straight(row_bits[0]), rest)
    left, right = one * 4 + two_ * 2 + deep, two_ * 4 + one * 2 + deep
    mine, other = core * 8, 8 - core * 8
    marks = jnp.stack([mine + left, mine + right, other + left, other + right]).astype(jnp.int32)

    pairs = width // 128
    ff = w_up.shape[1]
    tall = width // PIECES
    down_layout = ([(0, width, 0, ff // PIECES, 0)], [(ff, width)], "assemble_down")
    up_segments = [(0, ff, 0, tall, 0), (ff, ff + width, 1, tall, 0)]
    up_layout = (up_segments, [(width, ff), (width, width)], "assemble_up_out")
    qkv_segments = [(0, 3 * width, 0, tall, 0), (3 * width, 3 * width + VECTOR_LANES, 1, tall, 0)]
    qkv_layout = (qkv_segments, [(width, 3 * width), (width, VECTOR_LANES)], "assemble_qkv")
    row = my_row.astype(jnp.int32).reshape(1)

    order = Order()
    terms, gots, steps, done = [], [], {}, {}

    def backward():
        (grad,) = order.enter(gm)
        terms.append(attention_backward(q, grad, qfb, gmf, kvs, kf, len(terms)))
        order.leave(*terms[-1])
        if share == 2:
            gots.append(straight(part_bits[0])(terms[-1][2]))

    def start_wave(letter, pairs_of, name, layout):
        flat = order.enter(*[array for pair in pairs_of for array in pair])
        keep, send = weight_grad(marks, list(zip(flat[0::2], flat[1::2])), name)
        done[letter] = Wave(order, keep, send, marks, layout, *route)
        steps[letter] = done[letter].steps()

    def start_qkv():
        own_terms, far_terms = [term[1] for term in terms], gots
        if share != 2:
            both = jnp.concatenate(
                [jnp.concatenate([part.astype(BF16) for part in term[1:]], 0) for term in terms], axis=1
            )
            for bit in reversed(part_bits):
                half = both.shape[0] // 2
                kept, got = both[:half], straight(bit)(both[half:])
                both = add_low(kept, got)
            own_terms = [kept[:, 256 * h : 256 * (h + 1)].astype(F32) for h in range(pairs)]
            far_terms = [got[:, 256 * h : 256 * (h + 1)] for h in range(pairs)]
        (vec_,) = order.enter(vec)
        dqs = [term[0] for term in terms]
        done["p"], keep, send = qkv_grad(marks, normed, small, w_qkv, vec_, dqs, own_terms, far_terms)
        done["q"] = Wave(order, keep, send, marks, qkv_layout, *route)
        steps["q"] = done["q"].steps()

    def last():
        (packed,) = order.enter(done["p"])
        done["i"] = last_part(packed, grad_middle, small, w_qkv, xs)
        order.leave(*done["i"])

    def send_back(which):
        done[which] = deal(order.enter(*(outs if which == "o" else done["i"])))

    def take_back(which):
        done[which] = return_rows(row, order.enter(*done[which]))
        order.leave(done[which])

    actions = {
        "b": backward,
        "D": lambda: start_wave("d", [(active, dy)], "grad_down", down_layout),
        "U": lambda: start_wave("u", [(two, grad_hidden), (mixed, grad_attn)], "grad_up_out", up_layout),
        "G": start_qkv,
        "L": last,
        "o": lambda: send_back("o"),
        "i": lambda: send_back("i"),
        "O": lambda: take_back("o"),
        "I": lambda: take_back("i"),
        "d": lambda: next(steps["d"])(),
        "u": lambda: next(steps["u"])(),
        "q": lambda: next(steps["q"])(),
    }
    def wait(which):
        if which.isdigit():
            if share == 2:
                (gots[int(which)],) = order.enter(gots[int(which)])
                order.leave(gots[int(which)])
        elif which in "oi":
            done[which] = list(order.enter(*done[which]))
            order.leave(*done[which])
        else:
            done[which].wait()

    for word in SCHEDULE:
        if word[0] == "w":
            wait(word[1])
        else:
            actions[word]()
    result, input_grad = done["o"], done["i"]
    (sum_down,) = done["d"].sums
    sum_up, sum_out = done["u"].sums
    sum_qkv, tiles = done["q"].sums

    count = (ff + 8 * width) // VECTOR_LANES // PIECES
    vectors = tiles.reshape(PIECES, -1, VECTOR_LANES)[:, :count].reshape(-1)
    cuts = [ff + i * width for i in range(9)]
    names = [vectors[a:b] for a, b in zip(cuts[:-1], cuts[1:])]
    ln2_gain_sum, ln2_shift_sum, bias_down_sum, bias_out_sum = names[:4]
    bias_q_sum, bias_v_sum, ln1_gain_sum, ln1_shift_sum = names[4:]
    return (
        result,
        input_grad,
        ln1_gain_sum,
        ln1_shift_sum,
        sum_qkv,
        bias_q_sum,
        bias_v_sum,
        sum_out,
        bias_out_sum,
        ln2_gain_sum,
        ln2_shift_sum,
        sum_up,
        vectors[:ff],
        sum_down,
        bias_down_sum,
    )


def solution(mesh):
    split = P("row", "seq", None)
    placed = (split, P("row", None)) + (P(),) * 13 + (split,)
    return jax.shard_map(
        functools.partial(per_device, mesh.shape["seq"], mesh.shape["row"]),
        mesh=mesh,
        in_specs=placed,
        out_specs=(split, split) + (P(),) * 13,
        check_vma=False,
    )
```

```python
import functools

import jax
import jax.numpy as jnp
from jax import lax
from jax.experimental import pallas as pl
from jax.experimental.pallas import tpu as pltpu
from jax.sharding import PartitionSpec as P

HEADS = 8
EPSILON = 1e-06
BIG = 1e30
LSE_LANE = 16
PIECES = 16
AT_ONCE = 2
SCHEDULE = (
    "U", "o", "b", "wo", "u", "D", "b", "u", "G", "d", "u", "q", "u", "d", "q", "L",
    "d", "u", "wq", "i", "wd", "q", "wu", "d", "wq", "wi", "u", "q", "I", "u", "d", "q",
    "d", "wu", "q", "d", "u", "O", "q", "u", "d", "q", "q", "d",
)
MODES = {"d": "xy", "u": "xy", "q": "xy"}
VECTOR_LANES = 128
F32 = jnp.float32
BF16 = jnp.bfloat16
MIB = 1024 * 1024
LN1_GAIN, LN1_SHIFT, BIAS_Q, BIAS_V, BIAS_OUT, LN2_GAIN, LN2_SHIFT, BIAS_DOWN = (
    slice(i, i + 1) for i in range(8)
)
BIAS_UP = 8


def dot_nn(a, b):
    return lax.dot_general(a, b, (((1,), (0,)), ((), ())), preferred_element_type=F32)


def dot_nt(a, b):
    return lax.dot_general(a, b, (((1,), (1,)), ((), ())), preferred_element_type=F32)


def dot_tn(a, b):
    return lax.dot_general(a, b, (((0,), (0,)), ((), ())), preferred_element_type=F32)


def split_three(value):
    high = value.astype(BF16)
    rest = value - high.astype(F32)
    middle = rest.astype(BF16)
    low = (rest - middle.astype(F32)).astype(BF16)
    return high, middle, low


def lane_index(shape):
    return lax.broadcasted_iota(jnp.int32, shape, len(shape) - 1)


def three_lanes(value, lanes):
    high, middle, low = split_three(value)
    spot = lanes % 64
    out = jnp.where(spot == LSE_LANE, high.astype(F32), 0.0)
    out = jnp.where(spot == LSE_LANE + 1, middle.astype(F32), out)
    return jnp.where(spot == LSE_LANE + 2, low.astype(F32), out)


def norm_parts(value):
    centre = jnp.mean(value, axis=-1, keepdims=True)
    centred = value - centre
    spread = jnp.mean(centred * centred, axis=-1, keepdims=True)
    scale = lax.rsqrt(spread + EPSILON)
    return centred * scale, scale


def norm_back(grad, unit, scale, gain):
    grad_unit = grad * gain
    first = jnp.mean(grad_unit, axis=-1, keepdims=True)
    second = jnp.mean(grad_unit * unit, axis=-1, keepdims=True)
    return scale * (grad_unit - first - unit * second)


def fetch_kernel(source, target, sem):
    copy = pltpu.make_async_copy(source, target, sem)
    copy.start()
    copy.wait()


def fetch(array):
    return pl.pallas_call(
        fetch_kernel,
        in_specs=[pl.BlockSpec(memory_space=pl.ANY)],
        out_specs=vmem(),
        out_shape=jax.ShapeDtypeStruct(array.shape, array.dtype),
        scratch_shapes=[pltpu.SemaphoreType.DMA],
        compiler_params=pltpu.CompilerParams(vmem_limit_bytes=8 * MIB),
        name="fetch",
    )(array)


def qkv_kernel(pieces, width, *refs):
    x_refs = refs[:pieces]
    small, w_ref, x_ref, normed_ref, q_ref, kv_ref = refs[pieces:]
    band = x_refs[0].shape[0]
    for j in range(pieces):
        x_ref[j * band : (j + 1) * band, :] = x_refs[j][...]
        unit, _ = norm_parts(x_refs[j][...].astype(F32))
        normed_ref[j * band : (j + 1) * band, :] = (unit * small[LN1_GAIN] + small[LN1_SHIFT]).astype(BF16)
    normed = normed_ref[...]
    q = dot_nn(normed, w_ref[:, :width])
    q_ref[...] = ((q + small[BIAS_Q]) * (width // HEADS) ** -0.5).astype(BF16)
    kv_ref[:, :width] = dot_nn(normed, w_ref[:, width : 2 * width]).astype(BF16)
    kv_ref[:, width:] = (dot_nn(normed, w_ref[:, 2 * width :]) + small[BIAS_V]).astype(BF16)


def forward_kernel(parts, wide, rows, *refs):
    q_ref = refs[0]
    k_refs = refs[1 : 1 + parts]
    v_refs = refs[1 + parts : 1 + 2 * parts]
    qf_ref, kf_ref, mix_ref, qfb_ref, k_aug, v_aug = refs[1 + 2 * parts :]
    tokens = q_ref.shape[0]
    low_half = (lane_index((1, 128)) < 64).astype(F32)
    halves = (low_half.astype(BF16), (1.0 - low_half).astype(BF16))
    for pair in range(wide):
        at = slice(128 * pair, 128 * (pair + 1))
        for parity in range(2):
            mine, other = halves[parity], halves[1 - parity]
            start = 0
            for k_ref, v_ref in zip(k_refs, v_refs):
                stop = start + k_ref.shape[0]
                k_aug[2 * pair + parity, start:stop, :] = k_ref[:, at] * mine + kf_ref[start:stop, :] * other
                v_aug[2 * pair + parity, start:stop, :] = v_ref[:, at] * mine + other
                start = stop
    lanes = lane_index((rows, 128))
    low = lanes < 64
    held = {}

    def scores_of(pair, block, parity):
        at, heads = slice(block * rows, (block + 1) * rows), slice(128 * pair, 128 * (pair + 1))
        q = q_ref[at, heads] * halves[parity] + qf_ref[at, :] * halves[1 - parity]
        return dot_nt(q, k_aug[2 * pair + parity])

    def use(pair, block, parity, scores):
        top = jnp.max(scores, axis=-1, keepdims=True)
        exps = jnp.exp(scores - top).astype(BF16)
        sums = dot_nn(exps, v_aug[2 * pair + parity])
        if parity == 0:
            held[0] = (sums, top)
            return
        (even, even_top), odd, odd_top = held[0], sums, top
        at, heads = slice(block * rows, (block + 1) * rows), slice(128 * pair, 128 * (pair + 1))
        total = jnp.where(low, odd, even)
        mix_ref[at, heads] = jnp.where(low, even, odd) / pltpu.roll(total, 64, 1)
        log_total = jnp.where(low, odd_top, even_top) + jnp.log(total)
        qfb_ref[at, heads] = (qf_ref[at, :].astype(F32) + three_lanes(-log_total, lanes)).astype(BF16)

    before = None
    for pair in range(wide):
        for block in range(tokens // rows):
            for parity in range(2):
                now = (pair, block, parity, scores_of(pair, block, parity))
                if before is not None:
                    use(*before)
                before = now
    use(*before)


def attention_forward(q, kvs, qf, kf, wide=2, rows=256):
    tokens, width = q.shape
    lanes = 128 * wide
    steps = width // lanes
    length = kf.shape[0]
    parts = len(kvs)
    in_specs = [pl.BlockSpec((tokens, lanes), lambda h: (0, h))]
    in_specs += [pl.BlockSpec((kv.shape[0], lanes), lambda h: (0, h)) for kv in kvs]
    in_specs += [pl.BlockSpec((kv.shape[0], lanes), lambda h: (0, steps + h)) for kv in kvs]
    in_specs += [
        pl.BlockSpec((tokens, 128), lambda h: (0, 0)),
        pl.BlockSpec((length, 128), lambda h: (0, 0)),
    ]
    return pl.pallas_call(
        functools.partial(forward_kernel, parts, wide, rows),
        grid=(steps,),
        in_specs=in_specs,
        out_specs=[
            pl.BlockSpec((tokens, lanes), lambda h: (0, h)),
            pl.BlockSpec((tokens, lanes), lambda h: (0, h)),
        ],
        out_shape=[
            jax.ShapeDtypeStruct((tokens, width), F32),
            jax.ShapeDtypeStruct((tokens, width), BF16),
        ],
        scratch_shapes=[pltpu.VMEM((2 * wide, length, 128), BF16), pltpu.VMEM((2 * wide, length, 128), BF16)],
        compiler_params=pltpu.CompilerParams(vmem_limit_bytes=(8 + 8 * length // 1024) * MIB),
        name="attention_forward",
        cost_estimate=pl.CostEstimate(
            flops=4 * tokens * length * width, bytes_accessed=8 * tokens * width,
            transcendentals=tokens * length * HEADS,
        ),
    )(q, *kvs, *kvs, qf, kf)


def backward_kernel(parts, rows, *refs):
    q_ref, gm_ref, qfb_ref, gmf_ref = refs[:4]
    k_refs = refs[4 : 4 + parts]
    v_refs = refs[4 + parts : 4 + 2 * parts]
    kf_ref = refs[4 + 2 * parts]
    rest = refs[5 + 2 * parts :]
    dq_ref = rest[0]
    pair_refs = rest[1 : 1 + parts]
    q_aug, gm_aug, dqt = rest[1 + parts :]
    low_half = (lane_index((1, 128)) < 64).astype(F32)
    halves = (low_half.astype(BF16), (1.0 - low_half).astype(BF16))
    for parity in range(2):
        mine, other = halves[parity], halves[1 - parity]
        q_aug[parity] = q_ref[...] * mine + qfb_ref[...] * other
        gm_aug[parity] = gm_ref[...] * mine + gmf_ref[...] * other
    dqt[...] = jnp.zeros_like(dqt)
    low = lane_index((rows, 128)) < 64
    start = 0
    for k_ref, v_ref, pair_ref in zip(k_refs, v_refs, pair_refs):

        def block(step, carry, start=start, k_ref=k_ref, v_ref=v_ref, pair_ref=pair_ref):
            at = pl.ds(pl.multiple_of(step * rows, rows), rows)
            at_all = pl.ds(pl.multiple_of(start + step * rows, rows), rows)
            k, v, kf = k_ref[at, :], v_ref[at, :], kf_ref[at_all, :]
            dks, dvs = [], []
            for parity in range(2):
                mine, other = halves[parity], halves[1 - parity]
                k_aug = k * mine + kf * other
                v_aug = v * mine + other
                probs = jnp.exp(dot_nt(k_aug, q_aug[parity]))
                slopes = dot_nt(v_aug, gm_aug[parity])
                grads = (probs * slopes).astype(BF16)
                dvs.append(dot_nn(probs.astype(BF16), gm_ref[...]))
                dks.append(dot_nn(grads, q_ref[...]))
                dqt[parity] += dot_tn(k, grads)
            pair_ref[at, :128] = jnp.where(low, dks[0], dks[1]).astype(pair_ref.dtype)
            pair_ref[at, 128:] = jnp.where(low, dvs[0], dvs[1]).astype(pair_ref.dtype)
            return carry

        lax.fori_loop(0, k_ref.shape[0] // rows, block, 0)
        start += k_ref.shape[0]
    dq_t = jnp.concatenate([dqt[0, :64, :], dqt[1, 64:, :]], axis=0)
    dq_ref[...] = dq_t.T.astype(BF16) * (64.0**-0.5)


def attention_backward(q, gm, qfb, gmf, kvs, kf, first, count, rows=512):
    tokens, width = q.shape
    pairs = width // 128
    length = kf.shape[0]
    parts = len(kvs)
    of_pair = lambda i: (0, first + i)
    in_specs = [pl.BlockSpec((tokens, 128), of_pair)] * 4
    in_specs += [pl.BlockSpec((kv.shape[0], 128), of_pair) for kv in kvs]
    in_specs += [pl.BlockSpec((kv.shape[0], 128), lambda i: (0, pairs + first + i)) for kv in kvs]
    in_specs += [pl.BlockSpec((length, 128), lambda i: (0, 0))]
    kinds = [F32] + [BF16] * (parts - 1)
    outs = [jax.ShapeDtypeStruct((tokens, 128 * count), BF16)]
    outs += [jax.ShapeDtypeStruct((kv.shape[0], 256 * count), kind) for kv, kind in zip(kvs, kinds)]
    return pl.pallas_call(
        functools.partial(backward_kernel, parts, rows),
        grid=(count,),
        in_specs=in_specs,
        out_specs=[pl.BlockSpec((out.shape[0], out.shape[1] // count), lambda i: (0, i)) for out in outs],
        out_shape=outs,
        scratch_shapes=[
            pltpu.VMEM((2, tokens, 128), BF16),
            pltpu.VMEM((2, tokens, 128), BF16),
            pltpu.VMEM((2, 128, tokens), F32),
        ],
        compiler_params=pltpu.CompilerParams(vmem_limit_bytes=(12 + 4 * length // 1024) * MIB),
        name="attention_backward",
        cost_estimate=pl.CostEstimate(
            flops=10 * tokens * length * 128 * count, bytes_accessed=12 * tokens * 128 * count,
            transcendentals=tokens * length * 2 * count,
        ),
    )(q, gm, qfb, gmf, *kvs, *kvs, kf)


def middle_kernel(pieces, rows, *refs):
    dy_refs = refs[:pieces]
    x_ref, mix_ref, small, w_out, w_up, w_down = refs[pieces : pieces + 6]
    outs = refs[pieces + 6 :]
    gain, shift = small[LN2_GAIN], small[LN2_SHIFT]
    out_refs = outs[:pieces]
    (mixed_ref, two_ref, active_ref, gh_ref, ga_ref, gmid_ref, gm_ref, gmf_ref, vec_ref, dy_ref) = outs[pieces:]
    band = dy_refs[0].shape[0]
    tokens, width = mix_ref.shape
    ff = w_up.shape[1]
    vec_ref[...] = jnp.zeros_like(vec_ref)
    c0 = 0.7978845608028654
    c1 = 0.044715
    row = lax.broadcasted_iota(jnp.int32, (width, width), 0) // 64
    column = lane_index((width, width)) // 64
    opposite = (row == (column + 1 - 2 * (column % 2))).astype(F32).astype(BF16)
    per = rows // band
    for t in range(tokens // rows):
        at = slice(t * rows, (t + 1) * rows)
        x = x_ref[at, :].astype(F32)
        dy = jnp.concatenate([dy_refs[t * per + j][...] for j in range(per)], axis=0)
        dy_ref[at, :] = dy
        mix = mix_ref[at, :]
        mixed = mix.astype(BF16)
        mixed_ref[at, :] = mixed
        middle = x + (dot_nn(mixed, w_out[...]) + small[BIAS_OUT])
        unit, scale = norm_parts(middle)
        two = (unit * gain + shift).astype(BF16)
        two_ref[at, :] = two
        out = middle + small[BIAS_DOWN]
        grad_two = jnp.zeros((rows, width), F32)
        step = 2 * width
        before = None
        for f in range(0, ff + step, step):
            if f < ff:
                fs = slice(f, f + step)
                bias = jnp.concatenate(
                    [small[BIAS_UP + i : BIAS_UP + i + 1] for i in range(f // width, (f + step) // width)], axis=1
                )
                now = (fs, dot_nn(two, w_up[:, fs]) + bias, dot_nt(dy, w_down[fs, :]))
            if before is not None:
                fs, hidden, grad = before
                square = hidden * hidden
                tanh = jnp.tanh(c0 * hidden * (1.0 + c1 * square))
                half = 0.5 * (1.0 + tanh)
                active = (hidden * half).astype(BF16)
                active_ref[at, fs] = active
                out = out + dot_nn(active, w_down[fs, :])
                slope = half + hidden * (0.5 * (1.0 - tanh * tanh)) * (c0 + (3.0 * c0 * c1) * square)
                grad_low = (grad * slope).astype(BF16)
                gh_ref[at, fs] = grad_low
                vec_ref[0:1, fs] += jnp.sum(grad_low.astype(F32), axis=0, keepdims=True)
                grad_two = grad_two + dot_nt(grad_low, w_up[:, fs])
            before = now
        for j in range(per):
            out_refs[t * per + j][...] = out[j * band : (j + 1) * band].astype(BF16)
        dy_wide = dy.astype(F32)
        grad_middle = dy_wide + norm_back(grad_two, unit, scale, gain)
        gmid_ref[at, :] = grad_middle
        vec_ref[1:2, :width] += jnp.sum(grad_two * unit, axis=0, keepdims=True)
        vec_ref[2:3, :width] += jnp.sum(grad_two, axis=0, keepdims=True)
        vec_ref[3:4, :width] += jnp.sum(dy_wide, axis=0, keepdims=True)
        grad_attn = grad_middle.astype(BF16)
        ga_ref[at, :] = grad_attn
        vec_ref[4:5, :width] += jnp.sum(grad_attn.astype(F32), axis=0, keepdims=True)
        gm = dot_nt(grad_attn, w_out[...]).astype(BF16)
        gm_ref[at, :] = gm
        high, mid, _ = split_three(gm.astype(F32) * mix)
        inner = dot_nn(high, opposite) + dot_nn(mid, opposite)
        gmf_ref[at, :] = three_lanes(-inner, lane_index((rows, width))).astype(BF16)


def middle_part(dys, x, mix, small, w_out, w_up, w_down, rows=512):
    tokens, width = mix.shape
    ff = w_up.shape[1]
    shape = jax.ShapeDtypeStruct
    return pl.pallas_call(
        functools.partial(middle_kernel, len(dys), rows),
        out_shape=[shape(dy.shape, BF16) for dy in dys]
        + [
            shape((tokens, width), BF16),
            shape((tokens, width), BF16),
            shape((tokens, ff), BF16),
            shape((tokens, ff), BF16),
            shape((tokens, width), BF16),
            shape((tokens, width), F32),
            shape((tokens, width), BF16),
            shape((tokens, width), BF16),
            shape((8, ff), F32),
            shape((tokens, width), BF16),
        ],
        compiler_params=pltpu.CompilerParams(vmem_limit_bytes=24 * MIB),
        name="middle_part",
        cost_estimate=pl.CostEstimate(
            flops=2 * tokens * width * (4 * ff + 5 * width), bytes_accessed=8 * 1024 * 1024,
            transcendentals=tokens * ff,
        ),
    )(*dys, x, mix, small, w_out, w_up, w_down)


def columns_by_way(mode, columns):
    middle = columns // 256 * 128
    return {
        "x": ((0, columns, 0),),
        "y": ((0, columns, 1),),
        "xy": ((0, middle, 0), (middle, columns, 1)),
    }[mode]


def place_pieces(marks, mode, total, keep_ref, send_ref):
    piece = total.shape[0] // PIECES
    for which, target in enumerate((keep_ref, send_ref)):
        for start, stop, way in columns_by_way(mode, total.shape[1]):
            for j in range(PIECES // 2):
                source = pl.multiple_of((marks[2 * which + way] ^ j) * piece, piece)
                spot = slice(j * piece, (j + 1) * piece)
                target[spot, start:stop] = total[pl.ds(source, piece), start:stop].astype(BF16)


def smem():
    return pl.BlockSpec(memory_space=pltpu.SMEM)


def vmem():
    return pl.BlockSpec(memory_space=pltpu.VMEM)


def weight_grad_kernel(count, mode, marks, *refs):
    pairs = refs[: 2 * count]
    keep_ref, send_ref, total = refs[2 * count :]
    start = 0
    for left, right in zip(pairs[0::2], pairs[1::2]):
        stop = start + right.shape[1]
        for r in range(0, left.shape[1], 256):
            total[r : r + 256, start:stop] = dot_tn(left[:, r : r + 256], right[...])
        start = stop
    place_pieces(marks, mode, total, keep_ref, send_ref)


def weight_grad(marks, mode, pairs, name):
    rows = pairs[0][0].shape[1]
    columns = sum(right.shape[1] for _, right in pairs)
    depth = pairs[0][0].shape[0]
    half = jax.ShapeDtypeStruct((rows // 2, columns), BF16)
    flat = [array for pair in pairs for array in pair]
    return pl.pallas_call(
        functools.partial(weight_grad_kernel, len(pairs), mode),
        in_specs=[smem()] + [vmem()] * len(flat),
        out_specs=[vmem(), vmem()],
        out_shape=[half, half],
        scratch_shapes=[pltpu.VMEM((rows, columns), F32)],
        compiler_params=pltpu.CompilerParams(vmem_limit_bytes=16 * MIB),
        name=name,
        cost_estimate=pl.CostEstimate(
            flops=2 * rows * columns * depth, bytes_accessed=6 * rows * columns, transcendentals=0
        ),
    )(marks, *flat)


def qkv_grad_kernel(count, mode, *refs):
    marks, normed, small, w_ref, vec_ref = refs[:5]
    dqs, owns, gots = (refs[5 + i * count : 5 + (i + 1) * count] for i in range(3))
    packed, keep_ref, send_ref, total = refs[5 + 3 * count :]
    width = normed.shape[1]
    share = width // count
    for t in range(count):
        packed[:, share * t : share * (t + 1)] = dqs[t][...]
        both = (owns[t][...] + gots[t][...].astype(F32)).astype(BF16)
        for i in range(2 * share // 128):
            at = (i % 2 + 1) * width + share * t + 128 * (i // 2)
            packed[:, at : at + 128] = both[:, 128 * i : 128 * (i + 1)]
    for r in range(0, width, 256):
        total[r : r + 256, : 3 * width] = dot_tn(normed[:, r : r + 256], packed[...])
    sums = jnp.sum(packed[...].astype(F32), axis=0, keepdims=True)
    terms = jnp.concatenate(split_three(jnp.broadcast_to(sums, (16, 3 * width))), axis=0)
    spread = dot_nt(terms, w_ref[...])
    shift_row = spread[0:1] + (spread[16:17] + spread[32:33])
    rows = jnp.zeros((width, 128), F32)
    for at in range(0, 3 * width, 128):
        rows = rows + total[:, at : at + 128] * w_ref[:, at : at + 128].astype(F32)
    gain_row = jnp.sum(rows.T, axis=0, keepdims=True)
    gain_row = (gain_row - small[LN1_SHIFT] * shift_row) / small[LN1_GAIN]
    vectors = [vec_ref[0:1, :]] + [vec_ref[i : i + 1, :width] for i in range(1, 5)]
    vectors += [sums[:, :width], sums[:, 2 * width :], gain_row, shift_row]
    tiles = [row[:, at : at + VECTOR_LANES] for row in vectors for at in range(0, row.shape[1], VECTOR_LANES)]
    piece = width // PIECES
    per = len(tiles) // PIECES
    total[:, 3 * width :] = jnp.zeros((width, VECTOR_LANES), F32)
    for i, tile in enumerate(tiles):
        at = (i // per) * piece + i % per
        total[at : at + 1, 3 * width :] = tile
    place_pieces(marks, mode, total, keep_ref, send_ref)


def qkv_grad(marks, mode, normed, small, w_qkv, vec, dqs, owns, gots):
    tokens, width = normed.shape
    columns = 3 * width + VECTOR_LANES
    half = jax.ShapeDtypeStruct((width // 2, columns), BF16)
    flat = [normed, small, w_qkv, vec, *dqs, *owns, *gots]
    return pl.pallas_call(
        functools.partial(qkv_grad_kernel, len(dqs), mode),
        in_specs=[smem()] + [vmem()] * len(flat),
        out_specs=[vmem()] * 3,
        out_shape=[jax.ShapeDtypeStruct((tokens, 3 * width), BF16), half, half],
        scratch_shapes=[pltpu.VMEM((width, columns), F32)],
        compiler_params=pltpu.CompilerParams(vmem_limit_bytes=16 * MIB),
        name="qkv_grad",
        cost_estimate=pl.CostEstimate(
            flops=6 * tokens * width * width, bytes_accessed=18 * tokens * width, transcendentals=0
        ),
    )(marks, *flat)


def last_kernel(pieces, packed, gmid_ref, small, w_ref, x_ref, *out_refs):
    band = out_refs[0].shape[0]
    grad = dot_nt(packed[...], w_ref[...])
    unit, scale = norm_parts(x_ref[...].astype(F32))
    result = (gmid_ref[...] + norm_back(grad, unit, scale, small[LN1_GAIN])).astype(BF16)
    for j in range(pieces):
        out_refs[j][...] = result[j * band : (j + 1) * band]


def last_part(packed, gmid, small, w_qkv, x, pieces):
    tokens, width = gmid.shape
    return pl.pallas_call(
        functools.partial(last_kernel, pieces),
        out_shape=[jax.ShapeDtypeStruct((tokens // pieces, width), BF16)] * pieces,
        compiler_params=pltpu.CompilerParams(vmem_limit_bytes=12 * MIB),
        name="last_part",
        cost_estimate=pl.CostEstimate(
            flops=6 * tokens * width * width, bytes_accessed=10 * tokens * width, transcendentals=0
        ),
    )(packed, gmid, small, w_qkv, x)


def assemble_kernel(segments, mode, per, marks, *refs):
    own_far, out_refs = refs[:2], refs[2:]
    half = PIECES // 2
    piece = own_far[0].shape[0] // half
    step = pl.program_id(0)
    for i in range(per):
        index = step * per + i

        def fill(which, i=i, index=index):
            source = own_far[which]
            for low, high, way in columns_by_way(mode, source.shape[1]):
                at = pl.ds(pl.multiple_of(((index ^ marks[2 * which + way]) % half) * piece, piece), piece)
                for start, stop, which_out, tall, offset in segments:
                    first, last = max(start, low), min(stop, high)
                    if first < last:
                        spot = slice(i * tall + offset, i * tall + offset + piece)
                        out_refs[which_out][spot, first - start : last - start] = source[at, first:last].astype(F32)

        mine = index // half == marks[0] // half
        pl.when(mine)(functools.partial(fill, 0))
        pl.when(jnp.logical_not(mine))(functools.partial(fill, 1))


def assemble(marks, mode, parts, segments, shapes, name):
    steps = 2
    per = PIECES // steps
    size = sum(rows * columns for rows, columns in shapes)
    return pl.pallas_call(
        functools.partial(assemble_kernel, segments, mode, per),
        grid=(steps,),
        in_specs=[smem()] + [vmem()] * 2,
        out_specs=[pl.BlockSpec((rows // steps, w), lambda i: (i, 0)) for rows, w in shapes],
        out_shape=[jax.ShapeDtypeStruct(shape, F32) for shape in shapes],
        compiler_params=pltpu.CompilerParams(vmem_limit_bytes=16 * MIB),
        name=name,
        cost_estimate=pl.CostEstimate(flops=size, bytes_accessed=6 * size, transcendentals=0),
    )(marks, *parts)


def return_kernel(pieces, row_ref, *refs):
    out, sems = refs[pieces], refs[pieces + 1]
    copies = [
        pltpu.make_async_copy(refs[j], out.at[row_ref[0] ^ j], sems.at[j]) for j in range(pieces)
    ]
    for copy in copies:
        copy.start()
    for copy in copies:
        copy.wait()


def return_rows(row, got):
    return pl.pallas_call(
        functools.partial(return_kernel, len(got)),
        in_specs=[smem()] + [vmem()] * len(got),
        out_specs=pl.BlockSpec(memory_space=pl.ANY),
        out_shape=jax.ShapeDtypeStruct((len(got), *got[0].shape), BF16),
        scratch_shapes=[pltpu.SemaphoreType.DMA((len(got),))],
        compiler_params=pltpu.CompilerParams(vmem_limit_bytes=4 * MIB),
        name="return_rows",
    )(row, *got)


def swap(value, axis, size, mask):
    return lax.ppermute(value, axis, [(i, i ^ mask) for i in range(size)])


class Order:
    def __init__(self):
        self.last = ()

    def enter(self, *values):
        return lax.optimization_barrier((values, self.last))[0]

    def leave(self, *values):
        self.last = values


class Wave:
    def __init__(self, order, keep, send, marks, mode, layout, core, ways, deep, rest):
        self.order, self.core, self.ways, self.deep, self.rest = order, core, ways, deep, rest
        self.marks, self.mode, self.layout = marks, mode, layout
        self.parts = columns_by_way(mode, keep.shape[1])
        self.value, self.got = [keep], [core(send)]
        order.leave(send)

    def arrived(self):
        count = len(self.value)
        values = self.order.enter(*self.value, *self.got)
        return list(zip(values[:count], values[count:]))

    def added(self):
        return [add_low(one, two) for one, two in self.arrived()]

    def split(self, value):
        return [value[:, start:stop] for start, stop, _ in self.parts]

    def travel(self, step, values):
        self.got = [self.ways[(step + way) % 2](value) for (_, _, way), value in zip(self.parts, values)]
        self.order.leave(*values)

    def plane(self, step):
        values = self.added()
        if step == 0:
            values = self.split(values[0])
        half = values[0].shape[0] // 2
        self.value = [value[:half] for value in values]
        self.travel(step, [value[half:] for value in values])

    def line(self):
        values = self.added()
        half = values[0].shape[0] // 2
        self.value = [jnp.concatenate([value[:half] for value in values], axis=1)]
        sent = jnp.concatenate([value[half:] for value in values], axis=1)
        self.got = [self.deep(sent)]
        self.order.leave(sent)

    def exchanges(self):
        for send in self.rest:
            self.value = self.added()
            self.got = [send(self.value[0])]
            self.order.leave(*self.value)

    def line_back(self):
        self.value = self.added()
        self.got = [self.deep(self.value[0])]
        self.order.leave(*self.value)

    def joined(self):
        return [jnp.concatenate(pair, axis=0) for pair in self.arrived()]

    def plane_back(self, step):
        values = self.joined()
        self.value = self.split(values[0]) if step == 1 else values
        self.travel(step, self.value)

    def core_back(self):
        self.value = [jnp.concatenate(self.joined(), axis=1)]
        self.got = [self.core(self.value[0])]
        self.order.leave(*self.value)

    def wait(self):
        self.got = list(self.order.enter(*self.got))
        self.order.leave(*self.got)

    def finish(self):
        ((own, far),) = self.arrived()
        self.sums = assemble(self.marks, self.mode, (own, far), *self.layout)
        self.order.leave(*self.sums)

    def steps(self):
        yield functools.partial(self.plane, 0)
        yield functools.partial(self.plane, 1)
        yield self.line
        yield self.exchanges
        yield self.line_back
        yield functools.partial(self.plane_back, 1)
        yield functools.partial(self.plane_back, 0)
        yield self.core_back
        yield self.finish


def add_low(one, two):
    return (one.astype(F32) + two.astype(F32)).astype(BF16)


def after(value, *others):
    return lax.optimization_barrier((value, others))[0]


def bits_of(axis, size):
    found, mask = [], 1
    while mask < size:
        found.append((axis, size, mask, (lax.axis_index(axis) // mask) % 2))
        mask *= 2
    return found


def per_device(
    seq_size, row_size,
    block_input, segment_ids, ln1_gain, ln1_shift, w_qkv, bias_query, bias_value, w_out, bias_out,
    ln2_gain, ln2_shift, w_up, bias_up, w_down, bias_down, out_grad,
):
    rows, band, width = block_input.shape
    length = segment_ids.shape[1]
    share = seq_size // rows
    tokens = rows * band
    crops = max(length // (4 * band), 1)
    place = lax.axis_index("seq")
    my_row, my_part = place // share, place % share

    def deal(pieces):
        got = [pieces[0]]
        for j in range(1, rows):
            turn = [(s, ((s // share) ^ j) * share + s % share) for s in range(seq_size)]
            got.append(lax.ppermute(pieces[j], "seq", turn))
        return got

    def pick(array):
        return [lax.dynamic_index_in_dim(array, my_row ^ j, 0, False) for j in range(rows)]

    xs = deal(pick(block_input))
    dys = pick(out_grad)

    own_row = lax.dynamic_index_in_dim(segment_ids, my_row, 0, False).reshape(seq_size, band)
    key_ids = jnp.concatenate(
        [
            lax.dynamic_index_in_dim(own_row, (my_row ^ j) * share + (my_part ^ i), 0, False)
            for i in range(share)
            for j in range(rows)
        ]
    )
    spot = jnp.arange(128) % 64
    same = key_ids[:, None] == spot[None, :]
    used = spot[None, :] < crops
    ones = (spot >= LSE_LANE) & (spot < LSE_LANE + 3)
    kf = jnp.where(used, jnp.where(same, 0.0, -1.0), jnp.where(ones, 1.0, 0.0)).astype(BF16)
    qf = jnp.where(used & same, BIG, 0.0).astype(BF16)[:tokens]

    small = jnp.stack(
        [ln1_gain, ln1_shift, bias_query, bias_value, bias_out, ln2_gain, ln2_shift, bias_down]
    )
    small = jnp.concatenate([small, bias_up.reshape(-1, width)], axis=0)
    shape = jax.ShapeDtypeStruct
    x, normed, q, kv = pl.pallas_call(
        functools.partial(qkv_kernel, rows, width),
        out_shape=[
            shape((tokens, width), BF16),
            shape((tokens, width), BF16),
            shape((tokens, width), BF16),
            shape((tokens, 2 * width), BF16),
        ],
        compiler_params=pltpu.CompilerParams(vmem_limit_bytes=12 * MIB),
        name="norm_and_project",
    )(*xs, small, w_qkv)


    dys = list(lax.optimization_barrier((dys, kv))[0])
    dys = deal(dys)
    seq_bits = bits_of("seq", seq_size)
    row_bits = bits_of("row", row_size)
    part_bits = [bit for bit in seq_bits if bit[2] < share]
    kvs, whole = [kv], kv
    for axis, size, mask, own in part_bits:
        got = swap(whole, axis, size, mask)
        kvs.append(got)
        if mask * 2 < share:
            whole = jnp.concatenate([whole, got], 0)

    mix, qfb = attention_forward(q, kvs, qf, kf)
    *outs, mixed, two, active, grad_hidden, grad_attn, grad_middle, gm, gmf, vec, dy = middle_part(
        dys, x, mix, small, w_out, w_up, w_down
    )

    def straight(bit):
        return lambda value: swap(value, *bit[:3])

    core, one, two_, deep = seq_bits[0][3], seq_bits[1][3], seq_bits[2][3], row_bits[0][3]
    ways = (straight(seq_bits[1]), straight(seq_bits[2]))
    rest = [straight(bit) for bit in row_bits[1:] + seq_bits[3:]]
    route = (straight(seq_bits[0]), ways, straight(row_bits[0]), rest)
    left, right = one * 4 + two_ * 2 + deep, two_ * 4 + one * 2 + deep
    mine, other = core * 8, 8 - core * 8
    marks = jnp.stack([mine + left, mine + right, other + left, other + right]).astype(jnp.int32)

    pairs = width // 128
    ff = w_up.shape[1]
    tall = width // PIECES
    down_layout = ([(0, width, 0, ff // PIECES, 0)], [(ff, width)], "assemble_down")
    up_segments = [(0, ff, 0, tall, 0), (ff, ff + width, 1, tall, 0)]
    up_layout = (up_segments, [(width, ff), (width, width)], "assemble_up_out")
    qkv_segments = [(0, 3 * width, 0, tall, 0), (3 * width, 3 * width + VECTOR_LANES, 1, tall, 0)]
    qkv_layout = (qkv_segments, [(width, 3 * width), (width, VECTOR_LANES)], "assemble_qkv")
    row = my_row.astype(jnp.int32).reshape(1)

    order = Order()
    terms, gots, steps, done = [], [], {}, {}

    def backward():
        (grad,) = order.enter(gm)
        terms.append(attention_backward(q, grad, qfb, gmf, kvs, kf, AT_ONCE * len(terms), AT_ONCE))
        order.leave(*terms[-1])
        if share == 2:
            gots.append(straight(part_bits[0])(terms[-1][2]))

    def start_wave(letter, pairs_of, name, layout):
        flat = order.enter(*[array for pair in pairs_of for array in pair])
        keep, send = weight_grad(marks, MODES[letter], list(zip(flat[0::2], flat[1::2])), name)
        done[letter] = Wave(order, keep, send, marks, MODES[letter], layout, *route)
        steps[letter] = done[letter].steps()

    def start_qkv():
        own_terms, far_terms = [term[1] for term in terms], gots
        if share != 2:
            both = jnp.concatenate(
                [jnp.concatenate([part.astype(BF16) for part in term[1:]], 0) for term in terms], axis=1
            )
            for bit in reversed(part_bits):
                half = both.shape[0] // 2
                kept, got = both[:half], straight(bit)(both[half:])
                both = add_low(kept, got)
            cuts = [slice(256 * AT_ONCE * t, 256 * AT_ONCE * (t + 1)) for t in range(len(terms))]
            own_terms = [kept[:, cut].astype(F32) for cut in cuts]
            far_terms = [got[:, cut] for cut in cuts]
        (vec_,) = order.enter(vec)
        dqs = [term[0] for term in terms]
        done["p"], keep, send = qkv_grad(marks, MODES["q"], normed, small, w_qkv, vec_, dqs, own_terms, far_terms)
        done["q"] = Wave(order, keep, send, marks, MODES["q"], qkv_layout, *route)
        steps["q"] = done["q"].steps()

    def last():
        (packed,) = order.enter(done["p"])
        done["i"] = last_part(packed, grad_middle, small, w_qkv, x, rows)
        order.leave(*done["i"])

    def send_back(which):
        done[which] = deal(order.enter(*(outs if which == "o" else done["i"])))

    def take_back(which):
        done[which] = return_rows(row, order.enter(*done[which]))
        order.leave(done[which])

    actions = {
        "b": backward,
        "D": lambda: start_wave("d", [(active, dy)], "grad_down", down_layout),
        "U": lambda: start_wave("u", [(two, grad_hidden), (mixed, grad_attn)], "grad_up_out", up_layout),
        "G": start_qkv,
        "L": last,
        "o": lambda: send_back("o"),
        "i": lambda: send_back("i"),
        "O": lambda: take_back("o"),
        "I": lambda: take_back("i"),
        "d": lambda: next(steps["d"])(),
        "u": lambda: next(steps["u"])(),
        "q": lambda: next(steps["q"])(),
    }
    def wait(which):
        if which.isdigit():
            if share == 2:
                (gots[int(which)],) = order.enter(gots[int(which)])
                order.leave(gots[int(which)])
        elif which in "oi":
            done[which] = list(order.enter(*done[which]))
            order.leave(*done[which])
        else:
            done[which].wait()

    for word in SCHEDULE:
        if word[0] == "w":
            wait(word[1])
        else:
            actions[word]()
    result, input_grad = done["o"], done["i"]
    (sum_down,) = done["d"].sums
    sum_up, sum_out = done["u"].sums
    sum_qkv, tiles = done["q"].sums

    count = (ff + 8 * width) // VECTOR_LANES // PIECES
    vectors = tiles.reshape(PIECES, -1, VECTOR_LANES)[:, :count].reshape(-1)
    cuts = [ff + i * width for i in range(9)]
    names = [vectors[a:b] for a, b in zip(cuts[:-1], cuts[1:])]
    ln2_gain_sum, ln2_shift_sum, bias_down_sum, bias_out_sum = names[:4]
    bias_q_sum, bias_v_sum, ln1_gain_sum, ln1_shift_sum = names[4:]
    return (
        result,
        input_grad,
        ln1_gain_sum,
        ln1_shift_sum,
        sum_qkv,
        bias_q_sum,
        bias_v_sum,
        sum_out,
        bias_out_sum,
        ln2_gain_sum,
        ln2_shift_sum,
        sum_up,
        vectors[:ff],
        sum_down,
        bias_down_sum,
    )


def solution(mesh):
    split = P("row", "seq", None)
    placed = (split, P("row", None)) + (P(),) * 13 + (split,)
    return jax.shard_map(
        functools.partial(per_device, mesh.shape["seq"], mesh.shape["row"]),
        mesh=mesh,
        in_specs=placed,
        out_specs=(split, split) + (P(),) * 13,
        check_vma=False,
    )
```

```python
import functools

import jax
import jax.numpy as jnp
from jax import lax
from jax.experimental import pallas as pl
from jax.experimental.pallas import tpu as pltpu
from jax.sharding import PartitionSpec as P

HEADS = 8
EPSILON = 1e-06
BIG = 1e30
LSE_LANE = 16
PIECES = 16
AT_ONCE = 2
SCHEDULE = (
    "U", "D", "u", "b", "u", "b", "u", "d", "G", "u", "q", "d", "u", "L", "q", "d",
    "u", "q", "d", "q", "u", "d", "O", "q", "d", "u", "q", "d", "q", "I", "u", "d",
    "q", "d", "q",
)
MODES = {"d": "xy", "u": "xy", "q": "xy"}
VECTOR_LANES = 128
F32 = jnp.float32
BF16 = jnp.bfloat16
MIB = 1024 * 1024
LN1_GAIN, LN1_SHIFT, BIAS_Q, BIAS_V, BIAS_OUT, LN2_GAIN, LN2_SHIFT, BIAS_DOWN = (
    slice(i, i + 1) for i in range(8)
)
BIAS_UP = 8


def dot_nn(a, b):
    return lax.dot_general(a, b, (((1,), (0,)), ((), ())), preferred_element_type=F32)


def dot_nt(a, b):
    return lax.dot_general(a, b, (((1,), (1,)), ((), ())), preferred_element_type=F32)


def dot_tn(a, b):
    return lax.dot_general(a, b, (((0,), (0,)), ((), ())), preferred_element_type=F32)


def split_three(value):
    high = value.astype(BF16)
    rest = value - high.astype(F32)
    middle = rest.astype(BF16)
    low = (rest - middle.astype(F32)).astype(BF16)
    return high, middle, low


def lane_index(shape):
    return lax.broadcasted_iota(jnp.int32, shape, len(shape) - 1)


def three_lanes(value, lanes):
    high, middle, low = split_three(value)
    spot = lanes % 64
    out = jnp.where(spot == LSE_LANE, high.astype(F32), 0.0)
    out = jnp.where(spot == LSE_LANE + 1, middle.astype(F32), out)
    return jnp.where(spot == LSE_LANE + 2, low.astype(F32), out)


def norm_parts(value):
    centre = jnp.mean(value, axis=-1, keepdims=True)
    centred = value - centre
    spread = jnp.mean(centred * centred, axis=-1, keepdims=True)
    scale = lax.rsqrt(spread + EPSILON)
    return centred * scale, scale


def norm_back(grad, unit, scale, gain):
    grad_unit = grad * gain
    first = jnp.mean(grad_unit, axis=-1, keepdims=True)
    second = jnp.mean(grad_unit * unit, axis=-1, keepdims=True)
    return scale * (grad_unit - first - unit * second)


def fetch_kernel(source, target, sem):
    copy = pltpu.make_async_copy(source, target, sem)
    copy.start()
    copy.wait()


def fetch(array):
    return pl.pallas_call(
        fetch_kernel,
        in_specs=[pl.BlockSpec(memory_space=pl.ANY)],
        out_specs=vmem(),
        out_shape=jax.ShapeDtypeStruct(array.shape, array.dtype),
        scratch_shapes=[pltpu.SemaphoreType.DMA],
        compiler_params=pltpu.CompilerParams(vmem_limit_bytes=8 * MIB),
        name="fetch",
    )(array)


def qkv_kernel(pieces, width, *refs):
    x_refs = refs[:pieces]
    small, w_ref, x_ref, normed_ref, q_ref, kv_ref = refs[pieces:]
    band = x_refs[0].shape[0]
    for j in range(pieces):
        x_ref[j * band : (j + 1) * band, :] = x_refs[j][...]
        unit, _ = norm_parts(x_refs[j][...].astype(F32))
        normed_ref[j * band : (j + 1) * band, :] = (unit * small[LN1_GAIN] + small[LN1_SHIFT]).astype(BF16)
    normed = normed_ref[...]
    q = dot_nn(normed, w_ref[:, :width])
    q_ref[...] = ((q + small[BIAS_Q]) * (width // HEADS) ** -0.5).astype(BF16)
    kv_ref[:, :width] = dot_nn(normed, w_ref[:, width : 2 * width]).astype(BF16)
    kv_ref[:, width:] = (dot_nn(normed, w_ref[:, 2 * width :]) + small[BIAS_V]).astype(BF16)


def forward_kernel(parts, wide, rows, *refs):
    q_ref = refs[0]
    k_refs = refs[1 : 1 + parts]
    v_refs = refs[1 + parts : 1 + 2 * parts]
    qf_ref, kf_ref, mix_ref, qfb_ref, k_aug, v_aug = refs[1 + 2 * parts :]
    tokens = q_ref.shape[0]
    low_half = (lane_index((1, 128)) < 64).astype(F32)
    halves = (low_half.astype(BF16), (1.0 - low_half).astype(BF16))
    for pair in range(wide):
        at = slice(128 * pair, 128 * (pair + 1))
        for parity in range(2):
            mine, other = halves[parity], halves[1 - parity]
            start = 0
            for k_ref, v_ref in zip(k_refs, v_refs):
                stop = start + k_ref.shape[0]
                k_aug[2 * pair + parity, start:stop, :] = k_ref[:, at] * mine + kf_ref[start:stop, :] * other
                v_aug[2 * pair + parity, start:stop, :] = v_ref[:, at] * mine + other
                start = stop
    lanes = lane_index((rows, 128))
    low = lanes < 64
    held = {}

    def scores_of(pair, block, parity):
        at, heads = slice(block * rows, (block + 1) * rows), slice(128 * pair, 128 * (pair + 1))
        q = q_ref[at, heads] * halves[parity] + qf_ref[at, :] * halves[1 - parity]
        return dot_nt(q, k_aug[2 * pair + parity])

    def use(pair, block, parity, scores):
        top = jnp.max(scores, axis=-1, keepdims=True)
        exps = jnp.exp(scores - top).astype(BF16)
        sums = dot_nn(exps, v_aug[2 * pair + parity])
        if parity == 0:
            held[0] = (sums, top)
            return
        (even, even_top), odd, odd_top = held[0], sums, top
        at, heads = slice(block * rows, (block + 1) * rows), slice(128 * pair, 128 * (pair + 1))
        total = jnp.where(low, odd, even)
        mix_ref[at, heads] = jnp.where(low, even, odd) / pltpu.roll(total, 64, 1)
        log_total = jnp.where(low, odd_top, even_top) + jnp.log(total)
        qfb_ref[at, heads] = (qf_ref[at, :].astype(F32) + three_lanes(-log_total, lanes)).astype(BF16)

    before = None
    for pair in range(wide):
        for block in range(tokens // rows):
            for parity in range(2):
                now = (pair, block, parity, scores_of(pair, block, parity))
                if before is not None:
                    use(*before)
                before = now
    use(*before)


def attention_forward(q, kvs, qf, kf, wide=2, rows=256):
    tokens, width = q.shape
    lanes = 128 * wide
    steps = width // lanes
    length = kf.shape[0]
    parts = len(kvs)
    in_specs = [pl.BlockSpec((tokens, lanes), lambda h: (0, h))]
    in_specs += [pl.BlockSpec((kv.shape[0], lanes), lambda h: (0, h)) for kv in kvs]
    in_specs += [pl.BlockSpec((kv.shape[0], lanes), lambda h: (0, steps + h)) for kv in kvs]
    in_specs += [
        pl.BlockSpec((tokens, 128), lambda h: (0, 0)),
        pl.BlockSpec((length, 128), lambda h: (0, 0)),
    ]
    return pl.pallas_call(
        functools.partial(forward_kernel, parts, wide, rows),
        grid=(steps,),
        in_specs=in_specs,
        out_specs=[
            pl.BlockSpec((tokens, lanes), lambda h: (0, h)),
            pl.BlockSpec((tokens, lanes), lambda h: (0, h)),
        ],
        out_shape=[
            jax.ShapeDtypeStruct((tokens, width), F32),
            jax.ShapeDtypeStruct((tokens, width), BF16),
        ],
        scratch_shapes=[pltpu.VMEM((2 * wide, length, 128), BF16), pltpu.VMEM((2 * wide, length, 128), BF16)],
        compiler_params=pltpu.CompilerParams(vmem_limit_bytes=(8 + 8 * length // 1024) * MIB),
        name="attention_forward",
        cost_estimate=pl.CostEstimate(
            flops=4 * tokens * length * width, bytes_accessed=8 * tokens * width,
            transcendentals=tokens * length * HEADS,
        ),
    )(q, *kvs, *kvs, qf, kf)


def backward_kernel(parts, count, rows, *refs):
    q_ref, gm_ref, qfb_ref, gmf_ref = refs[:4]
    k_refs = refs[4 : 4 + parts]
    v_refs = refs[4 + parts : 4 + 2 * parts]
    kf_ref = refs[4 + 2 * parts]
    rest = refs[5 + 2 * parts :]
    dq_ref = rest[0]
    pair_refs = rest[1 : 1 + parts]
    q_aug, gm_aug, dqt = rest[1 + parts :]
    low_half = (lane_index((1, 128)) < 64).astype(F32)
    halves = (low_half.astype(BF16), (1.0 - low_half).astype(BF16))
    low = lane_index((rows, 128)) < 64
    for pair in range(count):
        heads = slice(128 * pair, 128 * (pair + 1))
        for parity in range(2):
            mine, other = halves[parity], halves[1 - parity]
            q_aug[2 * pair + parity] = q_ref[:, heads] * mine + qfb_ref[:, heads] * other
            gm_aug[2 * pair + parity] = gm_ref[:, heads] * mine + gmf_ref[:, heads] * other
        start = 0
        for k_ref, v_ref, pair_ref in zip(k_refs, v_refs, pair_refs):
            for block in range(k_ref.shape[0] // rows):
                at = slice(block * rows, (block + 1) * rows)
                k, v = k_ref[at, heads], v_ref[at, heads]
                kf = kf_ref[start + block * rows : start + (block + 1) * rows, :]
                dks, dvs = [], []
                for parity in range(2):
                    mine, other = halves[parity], halves[1 - parity]
                    probs = jnp.exp(dot_nt(k * mine + kf * other, q_aug[2 * pair + parity]))
                    slopes = dot_nt(v * mine + other, gm_aug[2 * pair + parity])
                    grads = (probs * slopes).astype(BF16)
                    dvs.append(dot_nn(probs.astype(BF16), gm_ref[:, heads]))
                    dks.append(dot_nn(grads, q_ref[:, heads]))
                    term = dot_tn(k, grads)
                    if start + block == 0:
                        dqt[2 * pair + parity] = term
                    else:
                        dqt[2 * pair + parity] += term
                left, right = 256 * pair, 256 * pair + 128
                pair_ref[at, left:right] = jnp.where(low, dks[0], dks[1]).astype(pair_ref.dtype)
                pair_ref[at, right : right + 128] = jnp.where(low, dvs[0], dvs[1]).astype(pair_ref.dtype)
            start += k_ref.shape[0]
        dq_t = jnp.concatenate([dqt[2 * pair, :64, :], dqt[2 * pair + 1, 64:, :]], axis=0)
        dq_ref[:, heads] = dq_t.T.astype(BF16) * (64.0**-0.5)


def attention_backward(q, gm, qfb, gmf, kvs, kf, first, count, rows=512):
    tokens, width = q.shape
    length = kf.shape[0]
    parts = len(kvs)
    lanes = 128 * count
    steps = width // lanes
    own = lambda i: (0, first // count)
    in_specs = [pl.BlockSpec((tokens, lanes), own)] * 4
    in_specs += [pl.BlockSpec((kv.shape[0], lanes), own) for kv in kvs]
    in_specs += [pl.BlockSpec((kv.shape[0], lanes), lambda i: (0, steps + first // count)) for kv in kvs]
    in_specs += [pl.BlockSpec((length, 128), lambda i: (0, 0))]
    kinds = [F32] + [BF16] * (parts - 1)
    outs = [jax.ShapeDtypeStruct((tokens, 128 * count), BF16)]
    outs += [jax.ShapeDtypeStruct((kv.shape[0], 256 * count), kind) for kv, kind in zip(kvs, kinds)]
    return pl.pallas_call(
        functools.partial(backward_kernel, parts, count, rows),
        grid=(1,),
        in_specs=in_specs,
        out_specs=[pl.BlockSpec(out.shape, lambda i: (0, 0)) for out in outs],
        out_shape=outs,
        scratch_shapes=[
            pltpu.VMEM((2 * count, tokens, 128), BF16),
            pltpu.VMEM((2 * count, tokens, 128), BF16),
            pltpu.VMEM((2 * count, 128, tokens), F32),
        ],
        compiler_params=pltpu.CompilerParams(vmem_limit_bytes=(12 + 4 * length // 1024) * MIB),
        name="attention_backward",
        cost_estimate=pl.CostEstimate(
            flops=10 * tokens * length * 128 * count, bytes_accessed=12 * tokens * 128 * count,
            transcendentals=tokens * length * 2 * count,
        ),
    )(q, gm, qfb, gmf, *kvs, *kvs, kf)


def middle_kernel(pieces, rows, *refs):
    dy_refs = refs[:pieces]
    x_ref, mix_ref, small, w_out, w_up, w_down = refs[pieces : pieces + 6]
    outs = refs[pieces + 6 :]
    gain, shift = small[LN2_GAIN], small[LN2_SHIFT]
    out_refs = outs[:pieces]
    (mixed_ref, two_ref, active_ref, gh_ref, ga_ref, gmid_ref, gm_ref, gmf_ref, vec_ref, dy_ref) = outs[pieces:]
    band = dy_refs[0].shape[0]
    tokens, width = mix_ref.shape
    ff = w_up.shape[1]
    vec_ref[...] = jnp.zeros_like(vec_ref)
    c0 = 0.7978845608028654
    c1 = 0.044715
    row = lax.broadcasted_iota(jnp.int32, (width, width), 0) // 64
    column = lane_index((width, width)) // 64
    opposite = (row == (column + 1 - 2 * (column % 2))).astype(F32).astype(BF16)
    per = rows // band
    for t in range(tokens // rows):
        at = slice(t * rows, (t + 1) * rows)
        x = x_ref[at, :].astype(F32)
        dy = jnp.concatenate([dy_refs[t * per + j][...] for j in range(per)], axis=0)
        dy_ref[at, :] = dy
        mix = mix_ref[at, :]
        mixed = mix.astype(BF16)
        mixed_ref[at, :] = mixed
        middle = x + (dot_nn(mixed, w_out[...]) + small[BIAS_OUT])
        unit, scale = norm_parts(middle)
        two = (unit * gain + shift).astype(BF16)
        two_ref[at, :] = two
        out = middle + small[BIAS_DOWN]
        grad_two = jnp.zeros((rows, width), F32)
        step = 2 * width
        before = None
        for f in range(0, ff + step, step):
            if f < ff:
                fs = slice(f, f + step)
                bias = jnp.concatenate(
                    [small[BIAS_UP + i : BIAS_UP + i + 1] for i in range(f // width, (f + step) // width)], axis=1
                )
                now = (fs, dot_nn(two, w_up[:, fs]) + bias, dot_nt(dy, w_down[fs, :]))
            if before is not None:
                fs, hidden, grad = before
                square = hidden * hidden
                tanh = jnp.tanh(c0 * hidden * (1.0 + c1 * square))
                half = 0.5 * (1.0 + tanh)
                active = (hidden * half).astype(BF16)
                active_ref[at, fs] = active
                out = out + dot_nn(active, w_down[fs, :])
                slope = half + hidden * (0.5 * (1.0 - tanh * tanh)) * (c0 + (3.0 * c0 * c1) * square)
                grad_low = (grad * slope).astype(BF16)
                gh_ref[at, fs] = grad_low
                vec_ref[0:1, fs] += jnp.sum(grad_low.astype(F32), axis=0, keepdims=True)
                grad_two = grad_two + dot_nt(grad_low, w_up[:, fs])
            before = now
        for j in range(per):
            out_refs[t * per + j][...] = out[j * band : (j + 1) * band].astype(BF16)
        dy_wide = dy.astype(F32)
        grad_middle = dy_wide + norm_back(grad_two, unit, scale, gain)
        gmid_ref[at, :] = grad_middle
        vec_ref[1:2, :width] += jnp.sum(grad_two * unit, axis=0, keepdims=True)
        vec_ref[2:3, :width] += jnp.sum(grad_two, axis=0, keepdims=True)
        vec_ref[3:4, :width] += jnp.sum(dy_wide, axis=0, keepdims=True)
        grad_attn = grad_middle.astype(BF16)
        ga_ref[at, :] = grad_attn
        vec_ref[4:5, :width] += jnp.sum(grad_attn.astype(F32), axis=0, keepdims=True)
        gm = dot_nt(grad_attn, w_out[...]).astype(BF16)
        gm_ref[at, :] = gm
        high, mid, _ = split_three(gm.astype(F32) * mix)
        inner = dot_nn(high, opposite) + dot_nn(mid, opposite)
        gmf_ref[at, :] = three_lanes(-inner, lane_index((rows, width))).astype(BF16)


def middle_part(dys, x, mix, small, w_out, w_up, w_down, rows=512):
    tokens, width = mix.shape
    ff = w_up.shape[1]
    shape = jax.ShapeDtypeStruct
    return pl.pallas_call(
        functools.partial(middle_kernel, len(dys), rows),
        out_shape=[shape(dy.shape, BF16) for dy in dys]
        + [
            shape((tokens, width), BF16),
            shape((tokens, width), BF16),
            shape((tokens, ff), BF16),
            shape((tokens, ff), BF16),
            shape((tokens, width), BF16),
            shape((tokens, width), F32),
            shape((tokens, width), BF16),
            shape((tokens, width), BF16),
            shape((8, ff), F32),
            shape((tokens, width), BF16),
        ],
        compiler_params=pltpu.CompilerParams(vmem_limit_bytes=24 * MIB),
        name="middle_part",
        cost_estimate=pl.CostEstimate(
            flops=2 * tokens * width * (4 * ff + 5 * width), bytes_accessed=8 * 1024 * 1024,
            transcendentals=tokens * ff,
        ),
    )(*dys, x, mix, small, w_out, w_up, w_down)


def columns_by_way(mode, columns):
    middle = columns // 256 * 128
    return {
        "x": ((0, columns, 0),),
        "y": ((0, columns, 1),),
        "xy": ((0, middle, 0), (middle, columns, 1)),
    }[mode]


def place_pieces(marks, mode, total, keep_ref, send_ref):
    piece = total.shape[0] // PIECES
    for which, target in enumerate((keep_ref, send_ref)):
        for start, stop, way in columns_by_way(mode, total.shape[1]):
            for j in range(PIECES // 2):
                source = pl.multiple_of((marks[2 * which + way] ^ j) * piece, piece)
                spot = slice(j * piece, (j + 1) * piece)
                target[spot, start:stop] = total[pl.ds(source, piece), start:stop].astype(BF16)


def smem():
    return pl.BlockSpec(memory_space=pltpu.SMEM)


def vmem():
    return pl.BlockSpec(memory_space=pltpu.VMEM)


def weight_grad_kernel(count, mode, marks, *refs):
    pairs = refs[: 2 * count]
    keep_ref, send_ref, total = refs[2 * count :]
    start = 0
    for left, right in zip(pairs[0::2], pairs[1::2]):
        stop = start + right.shape[1]
        for r in range(0, left.shape[1], 256):
            total[r : r + 256, start:stop] = dot_tn(left[:, r : r + 256], right[...])
        start = stop
    place_pieces(marks, mode, total, keep_ref, send_ref)


def weight_grad(marks, mode, pairs, name):
    rows = pairs[0][0].shape[1]
    columns = sum(right.shape[1] for _, right in pairs)
    depth = pairs[0][0].shape[0]
    half = jax.ShapeDtypeStruct((rows // 2, columns), BF16)
    flat = [array for pair in pairs for array in pair]
    return pl.pallas_call(
        functools.partial(weight_grad_kernel, len(pairs), mode),
        in_specs=[smem()] + [vmem()] * len(flat),
        out_specs=[vmem(), vmem()],
        out_shape=[half, half],
        scratch_shapes=[pltpu.VMEM((rows, columns), F32)],
        compiler_params=pltpu.CompilerParams(vmem_limit_bytes=16 * MIB),
        name=name,
        cost_estimate=pl.CostEstimate(
            flops=2 * rows * columns * depth, bytes_accessed=6 * rows * columns, transcendentals=0
        ),
    )(marks, *flat)


def qkv_grad_kernel(count, mode, *refs):
    marks, normed, small, w_ref, vec_ref = refs[:5]
    dqs, owns, gots = (refs[5 + i * count : 5 + (i + 1) * count] for i in range(3))
    packed, keep_ref, send_ref, total = refs[5 + 3 * count :]
    width = normed.shape[1]
    share = width // count
    for t in range(count):
        packed[:, share * t : share * (t + 1)] = dqs[t][...]
        both = (owns[t][...] + gots[t][...].astype(F32)).astype(BF16)
        for i in range(2 * share // 128):
            at = (i % 2 + 1) * width + share * t + 128 * (i // 2)
            packed[:, at : at + 128] = both[:, 128 * i : 128 * (i + 1)]
    for r in range(0, width, 256):
        total[r : r + 256, : 3 * width] = dot_tn(normed[:, r : r + 256], packed[...])
    sums = jnp.sum(packed[...].astype(F32), axis=0, keepdims=True)
    terms = jnp.concatenate(split_three(jnp.broadcast_to(sums, (16, 3 * width))), axis=0)
    spread = dot_nt(terms, w_ref[...])
    shift_row = spread[0:1] + (spread[16:17] + spread[32:33])
    rows = jnp.zeros((width, 128), F32)
    for at in range(0, 3 * width, 128):
        rows = rows + total[:, at : at + 128] * w_ref[:, at : at + 128].astype(F32)
    gain_row = jnp.sum(rows.T, axis=0, keepdims=True)
    gain_row = (gain_row - small[LN1_SHIFT] * shift_row) / small[LN1_GAIN]
    vectors = [vec_ref[0:1, :]] + [vec_ref[i : i + 1, :width] for i in range(1, 5)]
    vectors += [sums[:, :width], sums[:, 2 * width :], gain_row, shift_row]
    tiles = [row[:, at : at + VECTOR_LANES] for row in vectors for at in range(0, row.shape[1], VECTOR_LANES)]
    piece = width // PIECES
    per = len(tiles) // PIECES
    total[:, 3 * width :] = jnp.zeros((width, VECTOR_LANES), F32)
    for i, tile in enumerate(tiles):
        at = (i // per) * piece + i % per
        total[at : at + 1, 3 * width :] = tile
    place_pieces(marks, mode, total, keep_ref, send_ref)


def qkv_grad(marks, mode, normed, small, w_qkv, vec, dqs, owns, gots):
    tokens, width = normed.shape
    columns = 3 * width + VECTOR_LANES
    half = jax.ShapeDtypeStruct((width // 2, columns), BF16)
    flat = [normed, small, w_qkv, vec, *dqs, *owns, *gots]
    return pl.pallas_call(
        functools.partial(qkv_grad_kernel, len(dqs), mode),
        in_specs=[smem()] + [vmem()] * len(flat),
        out_specs=[vmem()] * 3,
        out_shape=[jax.ShapeDtypeStruct((tokens, 3 * width), BF16), half, half],
        scratch_shapes=[pltpu.VMEM((width, columns), F32)],
        compiler_params=pltpu.CompilerParams(vmem_limit_bytes=16 * MIB),
        name="qkv_grad",
        cost_estimate=pl.CostEstimate(
            flops=6 * tokens * width * width, bytes_accessed=18 * tokens * width, transcendentals=0
        ),
    )(marks, *flat)


def last_kernel(pieces, packed, gmid_ref, small, w_ref, x_ref, *out_refs):
    band = out_refs[0].shape[0]
    grad = dot_nt(packed[...], w_ref[...])
    unit, scale = norm_parts(x_ref[...].astype(F32))
    result = (gmid_ref[...] + norm_back(grad, unit, scale, small[LN1_GAIN])).astype(BF16)
    for j in range(pieces):
        out_refs[j][...] = result[j * band : (j + 1) * band]


def last_part(packed, gmid, small, w_qkv, x, pieces):
    tokens, width = gmid.shape
    return pl.pallas_call(
        functools.partial(last_kernel, pieces),
        out_shape=[jax.ShapeDtypeStruct((tokens // pieces, width), BF16)] * pieces,
        compiler_params=pltpu.CompilerParams(vmem_limit_bytes=12 * MIB),
        name="last_part",
        cost_estimate=pl.CostEstimate(
            flops=6 * tokens * width * width, bytes_accessed=10 * tokens * width, transcendentals=0
        ),
    )(packed, gmid, small, w_qkv, x)


def assemble_kernel(segments, mode, per, marks, *refs):
    own_far, out_refs = refs[:2], refs[2:]
    half = PIECES // 2
    piece = own_far[0].shape[0] // half
    step = pl.program_id(0)
    for i in range(per):
        index = step * per + i

        def fill(which, i=i, index=index):
            source = own_far[which]
            for low, high, way in columns_by_way(mode, source.shape[1]):
                at = pl.ds(pl.multiple_of(((index ^ marks[2 * which + way]) % half) * piece, piece), piece)
                for start, stop, which_out, tall, offset in segments:
                    first, last = max(start, low), min(stop, high)
                    if first < last:
                        spot = slice(i * tall + offset, i * tall + offset + piece)
                        out_refs[which_out][spot, first - start : last - start] = source[at, first:last].astype(F32)

        mine = index // half == marks[0] // half
        pl.when(mine)(functools.partial(fill, 0))
        pl.when(jnp.logical_not(mine))(functools.partial(fill, 1))


def assemble(marks, mode, parts, segments, shapes, name):
    steps = 2
    per = PIECES // steps
    size = sum(rows * columns for rows, columns in shapes)
    return pl.pallas_call(
        functools.partial(assemble_kernel, segments, mode, per),
        grid=(steps,),
        in_specs=[smem()] + [vmem()] * 2,
        out_specs=[pl.BlockSpec((rows // steps, w), lambda i: (i, 0)) for rows, w in shapes],
        out_shape=[jax.ShapeDtypeStruct(shape, F32) for shape in shapes],
        compiler_params=pltpu.CompilerParams(vmem_limit_bytes=16 * MIB),
        name=name,
        cost_estimate=pl.CostEstimate(flops=size, bytes_accessed=6 * size, transcendentals=0),
    )(marks, *parts)


def return_kernel(halves, row_ref, *refs):
    out, sems = refs[-2], refs[-1]
    copies = []
    for i, (ref, (j, half)) in enumerate(zip(refs, halves)):
        width = ref.shape[1]
        at = 0 if half is None else half * width
        copies.append(pltpu.make_async_copy(ref, out.at[row_ref[0] ^ j, :, at : at + width], sems.at[i]))
    for copy in copies:
        copy.start()
    for copy in copies:
        copy.wait()


def return_rows(row, own, halves, name):
    flat = [own] + [piece for half in halves for piece in half]
    places = [(0, None)] + [(j + 1, h) for h, half in enumerate(halves) for j in range(len(half))]
    pieces = len(halves[0]) + 1
    return pl.pallas_call(
        functools.partial(return_kernel, places),
        in_specs=[smem()] + [vmem()] * len(flat),
        out_specs=pl.BlockSpec(memory_space=pl.ANY),
        out_shape=jax.ShapeDtypeStruct((pieces, *own.shape), BF16),
        scratch_shapes=[pltpu.SemaphoreType.DMA((len(flat),))],
        compiler_params=pltpu.CompilerParams(vmem_limit_bytes=4 * MIB),
        name=name,
    )(row, *flat)


def swap(value, axis, size, mask):
    return lax.ppermute(value, axis, [(i, i ^ mask) for i in range(size)])


class Order:
    def __init__(self):
        self.last = ()

    def enter(self, *values):
        return lax.optimization_barrier((values, self.last))[0]

    def leave(self, *values):
        self.last = values


class Cargo:
    def __init__(self, pieces):
        self.pieces = pieces
        width = pieces[0].shape[1] // 2
        self.columns = [slice(0, width), slice(width, 2 * width)]
        self.came = [[None] * len(pieces) for _ in range(2)]
        self.onward = [None, None]

    def load(self, half, way, first):
        columns = self.columns[half]
        far = self.pieces[3][:, columns] if first else self.onward[half]
        return jnp.concatenate([self.pieces[way + 1][:, columns], far], axis=0)

    def land(self, half, way, first, got):
        band = got.shape[0] // 2
        self.came[half][way + 1] = got[:band]
        if first:
            self.onward[half] = got[band:]
        else:
            self.came[half][3] = got[band:]


def fold(value, rows):
    if rows < value.shape[0]:
        return jnp.concatenate([value[at : at + rows] for at in range(0, value.shape[0], rows)], axis=1)
    wide = value.shape[1] * value.shape[0] // rows
    return jnp.concatenate([value[:, at : at + wide] for at in range(0, value.shape[1], wide)], axis=0)


class Wave:
    def __init__(self, order, keep, send, marks, mode, layout, core, ways, deep, rest):
        self.order, self.core, self.ways, self.deep, self.rest = order, core, ways, deep, rest
        self.marks, self.mode, self.layout = marks, mode, layout
        self.parts = columns_by_way(mode, keep.shape[1])
        self.value, self.got = [keep], [core(send)]
        self.cargo, self.aboard = {}, None
        order.leave(send)

    def arrived(self):
        count = len(self.value)
        values = self.order.enter(*self.value, *self.got)
        kept, came = values[:count], list(values[count:])
        if self.aboard is not None:
            cargo, first, ways, shape = self.aboard
            for i, way in enumerate(ways):
                own = self.parts[i][1] - self.parts[i][0]
                cargo.land(i, way, first, fold(came[i][:, own:], shape[0]))
                came[i] = came[i][:, :own]
            self.aboard = None
        return list(zip(kept, came))

    def added(self):
        return [add_low(one, two) for one, two in self.arrived()]

    def split(self, value):
        return [value[:, start:stop] for start, stop, _ in self.parts]

    def travel(self, step, values, key):
        ways = [(step + way) % 2 for _, _, way in self.parts]
        if key in self.cargo:
            cargo, first = self.cargo[key]
            loads = [cargo.load(i, way, first) for i, way in enumerate(ways)]
            self.aboard = (cargo, first, ways, loads[0].shape)
            values = [
                jnp.concatenate([value, fold(load, value.shape[0])], axis=1) for value, load in zip(values, loads)
            ]
        self.got = [self.ways[way](value) for way, value in zip(ways, values)]
        self.order.leave(*values)

    def plane(self, step):
        values = self.added()
        if step == 0:
            values = self.split(values[0])
        half = values[0].shape[0] // 2
        self.value = [value[:half] for value in values]
        self.travel(step, [value[half:] for value in values], ("out", step))

    def line(self):
        values = self.added()
        half = values[0].shape[0] // 2
        self.value = [jnp.concatenate([value[:half] for value in values], axis=1)]
        sent = jnp.concatenate([value[half:] for value in values], axis=1)
        self.got = [self.deep(sent)]
        self.order.leave(sent)

    def exchanges(self):
        for send in self.rest:
            self.value = self.added()
            self.got = [send(self.value[0])]
            self.order.leave(*self.value)

    def line_back(self):
        self.value = self.added()
        self.got = [self.deep(self.value[0])]
        self.order.leave(*self.value)

    def joined(self):
        return [jnp.concatenate(pair, axis=0) for pair in self.arrived()]

    def plane_back(self, step):
        values = self.joined()
        self.value = self.split(values[0]) if step == 1 else values
        self.travel(step, self.value, ("back", step))

    def core_back(self):
        self.value = [jnp.concatenate(self.joined(), axis=1)]
        self.got = [self.core(self.value[0])]
        self.order.leave(*self.value)

    def wait(self):
        self.got = list(self.order.enter(*self.got))
        self.order.leave(*self.got)

    def finish(self):
        ((own, far),) = self.arrived()
        self.sums = assemble(self.marks, self.mode, (own, far), *self.layout)
        self.order.leave(*self.sums)

    def steps(self):
        yield functools.partial(self.plane, 0)
        yield functools.partial(self.plane, 1)
        yield self.line
        yield self.exchanges
        yield self.line_back
        yield functools.partial(self.plane_back, 1)
        yield functools.partial(self.plane_back, 0)
        yield self.core_back
        yield self.finish


def add_low(one, two):
    return (one.astype(F32) + two.astype(F32)).astype(BF16)


def after(value, *others):
    return lax.optimization_barrier((value, others))[0]


def bits_of(axis, size):
    found, mask = [], 1
    while mask < size:
        found.append((axis, size, mask, (lax.axis_index(axis) // mask) % 2))
        mask *= 2
    return found


def per_device(
    seq_size, row_size,
    block_input, segment_ids, ln1_gain, ln1_shift, w_qkv, bias_query, bias_value, w_out, bias_out,
    ln2_gain, ln2_shift, w_up, bias_up, w_down, bias_down, out_grad,
):
    rows, band, width = block_input.shape
    length = segment_ids.shape[1]
    share = seq_size // rows
    tokens = rows * band
    crops = max(length // (4 * band), 1)
    place = lax.axis_index("seq")
    my_row, my_part = place // share, place % share

    def deal(pieces):
        got = [pieces[0]]
        for j in range(1, rows):
            turn = [(s, ((s // share) ^ j) * share + s % share) for s in range(seq_size)]
            got.append(lax.ppermute(pieces[j], "seq", turn))
        return got

    def pick(array):
        return [lax.dynamic_index_in_dim(array, my_row ^ j, 0, False) for j in range(rows)]

    xs = deal(pick(block_input))
    dys = pick(out_grad)

    own_row = lax.dynamic_index_in_dim(segment_ids, my_row, 0, False).reshape(seq_size, band)
    key_ids = jnp.concatenate(
        [
            lax.dynamic_index_in_dim(own_row, (my_row ^ j) * share + (my_part ^ i), 0, False)
            for i in range(share)
            for j in range(rows)
        ]
    )
    spot = jnp.arange(128) % 64
    same = key_ids[:, None] == spot[None, :]
    used = spot[None, :] < crops
    ones = (spot >= LSE_LANE) & (spot < LSE_LANE + 3)
    kf = jnp.where(used, jnp.where(same, 0.0, -1.0), jnp.where(ones, 1.0, 0.0)).astype(BF16)
    qf = jnp.where(used & same, BIG, 0.0).astype(BF16)[:tokens]

    small = jnp.stack(
        [ln1_gain, ln1_shift, bias_query, bias_value, bias_out, ln2_gain, ln2_shift, bias_down]
    )
    small = jnp.concatenate([small, bias_up.reshape(-1, width)], axis=0)
    shape = jax.ShapeDtypeStruct
    x, normed, q, kv = pl.pallas_call(
        functools.partial(qkv_kernel, rows, width),
        out_shape=[
            shape((tokens, width), BF16),
            shape((tokens, width), BF16),
            shape((tokens, width), BF16),
            shape((tokens, 2 * width), BF16),
        ],
        compiler_params=pltpu.CompilerParams(vmem_limit_bytes=12 * MIB),
        name="norm_and_project",
    )(*xs, small, w_qkv)


    dys = list(lax.optimization_barrier((dys, kv))[0])
    dys = deal(dys)
    seq_bits = bits_of("seq", seq_size)
    row_bits = bits_of("row", row_size)
    part_bits = [bit for bit in seq_bits if bit[2] < share]
    kvs, whole = [kv], kv
    for axis, size, mask, own in part_bits:
        got = swap(whole, axis, size, mask)
        kvs.append(got)
        if mask * 2 < share:
            whole = jnp.concatenate([whole, got], 0)

    mix, qfb = attention_forward(q, kvs, qf, kf)
    *outs, mixed, two, active, grad_hidden, grad_attn, grad_middle, gm, gmf, vec, dy = middle_part(
        dys, x, mix, small, w_out, w_up, w_down
    )

    def straight(bit):
        return lambda value: swap(value, *bit[:3])

    plane = [bit for bit in seq_bits if bit[2] >= share]
    core, one, two_, deep = seq_bits[0][3], plane[0][3], plane[1][3], row_bits[0][3]
    ways = (straight(plane[0]), straight(plane[1]))
    rest = [straight(bit) for bit in row_bits[1:] + plane[2:] + part_bits[1:]]
    route = (straight(seq_bits[0]), ways, straight(row_bits[0]), rest)
    left, right = one * 4 + two_ * 2 + deep, two_ * 4 + one * 2 + deep
    mine, other = core * 8, 8 - core * 8
    marks = jnp.stack([mine + left, mine + right, other + left, other + right]).astype(jnp.int32)

    pairs = width // 128
    ff = w_up.shape[1]
    tall = width // PIECES
    down_layout = ([(0, width, 0, ff // PIECES, 0)], [(ff, width)], "assemble_down")
    up_segments = [(0, ff, 0, tall, 0), (ff, ff + width, 1, tall, 0)]
    up_layout = (up_segments, [(width, ff), (width, width)], "assemble_up_out")
    qkv_segments = [(0, 3 * width, 0, tall, 0), (3 * width, 3 * width + VECTOR_LANES, 1, tall, 0)]
    qkv_layout = (qkv_segments, [(width, 3 * width), (width, VECTOR_LANES)], "assemble_qkv")
    row = my_row.astype(jnp.int32).reshape(1)

    order = Order()
    terms, gots, steps, done = [], [], {}, {}

    def backward():
        (grad,) = order.enter(gm)
        terms.append(attention_backward(q, grad, qfb, gmf, kvs, kf, AT_ONCE * len(terms), AT_ONCE))
        order.leave(*terms[-1])
        if share == 2:
            gots.append(straight(part_bits[0])(terms[-1][2]))

    def start_wave(letter, pairs_of, name, layout):
        flat = order.enter(*[array for pair in pairs_of for array in pair])
        keep, send = weight_grad(marks, MODES[letter], list(zip(flat[0::2], flat[1::2])), name)
        done[letter] = Wave(order, keep, send, marks, MODES[letter], layout, *route)
        steps[letter] = done[letter].steps()
        if letter == "d":
            ride("d", outs, "out", "o")

    def start_qkv():
        own_terms, far_terms = [term[1] for term in terms], gots
        if share != 2:
            both = jnp.concatenate(
                [jnp.concatenate([part.astype(BF16) for part in term[1:]], 0) for term in terms], axis=1
            )
            for bit in reversed(part_bits):
                half = both.shape[0] // 2
                kept, got = both[:half], straight(bit)(both[half:])
                both = add_low(kept, got)
            cuts = [slice(256 * AT_ONCE * t, 256 * AT_ONCE * (t + 1)) for t in range(len(terms))]
            own_terms = [kept[:, cut].astype(F32) for cut in cuts]
            far_terms = [got[:, cut] for cut in cuts]
        (vec_,) = order.enter(vec)
        dqs = [term[0] for term in terms]
        done["p"], keep, send = qkv_grad(marks, MODES["q"], normed, small, w_qkv, vec_, dqs, own_terms, far_terms)
        done["q"] = Wave(order, keep, send, marks, MODES["q"], qkv_layout, *route)
        steps["q"] = done["q"].steps()

    def last():
        (packed,) = order.enter(done["p"])
        pieces = last_part(packed, grad_middle, small, w_qkv, x, rows)
        order.leave(*pieces)
        ride("u", pieces, "back", "i")

    def ride(letter, pieces, stage, name):
        done[name] = Cargo(pieces)
        steps_ = (0, 1) if stage == "out" else (1, 0)
        for i, step in enumerate(steps_):
            done[letter].cargo[(stage, step)] = (done[name], i == 0)

    def take_back(name):
        cargo = done[name]
        halves = [list(order.enter(*half[1:])) for half in cargo.came]
        done[name] = return_rows(row, cargo.pieces[0], halves, "return_rows")
        order.leave(done[name])

    actions = {
        "b": backward,
        "D": lambda: start_wave("d", [(active, dy)], "grad_down", down_layout),
        "U": lambda: start_wave("u", [(two, grad_hidden), (mixed, grad_attn)], "grad_up_out", up_layout),
        "G": start_qkv,
        "L": last,
        "O": lambda: take_back("o"),
        "I": lambda: take_back("i"),
        "d": lambda: next(steps["d"])(),
        "u": lambda: next(steps["u"])(),
        "q": lambda: next(steps["q"])(),
    }
    def wait(which):
        if which.isdigit():
            if share == 2:
                (gots[int(which)],) = order.enter(gots[int(which)])
                order.leave(gots[int(which)])
        else:
            done[which].wait()

    for word in SCHEDULE:
        if word[0] == "w":
            wait(word[1])
        else:
            actions[word]()
    result, input_grad = done["o"], done["i"]
    (sum_down,) = done["d"].sums
    sum_up, sum_out = done["u"].sums
    sum_qkv, tiles = done["q"].sums

    count = (ff + 8 * width) // VECTOR_LANES // PIECES
    vectors = tiles.reshape(PIECES, -1, VECTOR_LANES)[:, :count].reshape(-1)
    cuts = [ff + i * width for i in range(9)]
    names = [vectors[a:b] for a, b in zip(cuts[:-1], cuts[1:])]
    ln2_gain_sum, ln2_shift_sum, bias_down_sum, bias_out_sum = names[:4]
    bias_q_sum, bias_v_sum, ln1_gain_sum, ln1_shift_sum = names[4:]
    return (
        result,
        input_grad,
        ln1_gain_sum,
        ln1_shift_sum,
        sum_qkv,
        bias_q_sum,
        bias_v_sum,
        sum_out,
        bias_out_sum,
        ln2_gain_sum,
        ln2_shift_sum,
        sum_up,
        vectors[:ff],
        sum_down,
        bias_down_sum,
    )


def solution(mesh):
    split = P("row", "seq", None)
    placed = (split, P("row", None)) + (P(),) * 13 + (split,)
    return jax.shard_map(
        functools.partial(per_device, mesh.shape["seq"], mesh.shape["row"]),
        mesh=mesh,
        in_specs=placed,
        out_specs=(split, split) + (P(),) * 13,
        check_vma=False,
    )
```

```python
import functools

import jax
import jax.numpy as jnp
from jax import lax
from jax.experimental import pallas as pl
from jax.experimental.pallas import tpu as pltpu
from jax.sharding import PartitionSpec as P

HEADS = 8
EPSILON = 1e-06
BIG = 1e30
LSE_LANE = 16
PIECES = 16
AT_ONCE = 2
SCHEDULE = (
    "U", "D", "u", "b", "u", "b", "u", "d", "G", "u", "q", "d", "u", "L", "q", "d",
    "u", "q", "d", "q", "u", "d", "O", "q", "d", "u", "q", "d", "q", "I", "u", "d",
    "q", "q", "d",
)
MODES = {"d": "xy", "u": "xy", "q": "xy"}
VECTOR_LANES = 128
F32 = jnp.float32
BF16 = jnp.bfloat16
MIB = 1024 * 1024
LN1_GAIN, LN1_SHIFT, BIAS_Q, BIAS_V, BIAS_OUT, LN2_GAIN, LN2_SHIFT, BIAS_DOWN = (
    slice(i, i + 1) for i in range(8)
)
BIAS_UP = 8


def dot_nn(a, b):
    return lax.dot_general(a, b, (((1,), (0,)), ((), ())), preferred_element_type=F32)


def dot_nt(a, b):
    return lax.dot_general(a, b, (((1,), (1,)), ((), ())), preferred_element_type=F32)


def dot_tn(a, b):
    return lax.dot_general(a, b, (((0,), (0,)), ((), ())), preferred_element_type=F32)


def split_three(value):
    high = value.astype(BF16)
    rest = value - high.astype(F32)
    middle = rest.astype(BF16)
    low = (rest - middle.astype(F32)).astype(BF16)
    return high, middle, low


def lane_index(shape):
    return lax.broadcasted_iota(jnp.int32, shape, len(shape) - 1)


def three_lanes(value, lanes):
    high, middle, low = split_three(value)
    spot = lanes % 64
    out = jnp.where(spot == LSE_LANE, high.astype(F32), 0.0)
    out = jnp.where(spot == LSE_LANE + 1, middle.astype(F32), out)
    return jnp.where(spot == LSE_LANE + 2, low.astype(F32), out)


def norm_parts(value):
    centre = jnp.mean(value, axis=-1, keepdims=True)
    centred = value - centre
    spread = jnp.mean(centred * centred, axis=-1, keepdims=True)
    scale = lax.rsqrt(spread + EPSILON)
    return centred * scale, scale


def norm_back(grad, unit, scale, gain):
    grad_unit = grad * gain
    first = jnp.mean(grad_unit, axis=-1, keepdims=True)
    second = jnp.mean(grad_unit * unit, axis=-1, keepdims=True)
    return scale * (grad_unit - first - unit * second)


def fetch_kernel(source, target, sem):
    copy = pltpu.make_async_copy(source, target, sem)
    copy.start()
    copy.wait()


def fetch(array):
    return pl.pallas_call(
        fetch_kernel,
        in_specs=[pl.BlockSpec(memory_space=pl.ANY)],
        out_specs=vmem(),
        out_shape=jax.ShapeDtypeStruct(array.shape, array.dtype),
        scratch_shapes=[pltpu.SemaphoreType.DMA],
        compiler_params=pltpu.CompilerParams(vmem_limit_bytes=8 * MIB),
        name="fetch",
    )(array)


def qkv_kernel(pieces, width, *refs):
    x_refs = refs[:pieces]
    small, w_ref, x_ref, normed_ref, q_ref, kv_ref = refs[pieces:]
    band = x_refs[0].shape[0]
    for j in range(pieces):
        x_ref[j * band : (j + 1) * band, :] = x_refs[j][...]
        unit, _ = norm_parts(x_refs[j][...].astype(F32))
        normed_ref[j * band : (j + 1) * band, :] = (unit * small[LN1_GAIN] + small[LN1_SHIFT]).astype(BF16)
    normed = normed_ref[...]
    q = dot_nn(normed, w_ref[:, :width])
    q_ref[...] = ((q + small[BIAS_Q]) * (width // HEADS) ** -0.5).astype(BF16)
    kv_ref[:, :width] = dot_nn(normed, w_ref[:, width : 2 * width]).astype(BF16)
    kv_ref[:, width:] = (dot_nn(normed, w_ref[:, 2 * width :]) + small[BIAS_V]).astype(BF16)


def forward_kernel(parts, wide, rows, *refs):
    q_ref = refs[0]
    k_refs = refs[1 : 1 + parts]
    v_refs = refs[1 + parts : 1 + 2 * parts]
    qf_ref, kf_ref, mix_ref, qfb_ref, k_aug, v_aug = refs[1 + 2 * parts :]
    tokens = q_ref.shape[0]
    low_half = (lane_index((1, 128)) < 64).astype(F32)
    halves = (low_half.astype(BF16), (1.0 - low_half).astype(BF16))
    for pair in range(wide):
        at = slice(128 * pair, 128 * (pair + 1))
        for parity in range(2):
            mine, other = halves[parity], halves[1 - parity]
            start = 0
            for k_ref, v_ref in zip(k_refs, v_refs):
                stop = start + k_ref.shape[0]
                k_aug[2 * pair + parity, start:stop, :] = k_ref[:, at] * mine + kf_ref[start:stop, :] * other
                v_aug[2 * pair + parity, start:stop, :] = v_ref[:, at] * mine + other
                start = stop
    lanes = lane_index((rows, 128))
    low = lanes < 64
    held = {}

    def scores_of(pair, block, parity):
        at, heads = slice(block * rows, (block + 1) * rows), slice(128 * pair, 128 * (pair + 1))
        q = q_ref[at, heads] * halves[parity] + qf_ref[at, :] * halves[1 - parity]
        return dot_nt(q, k_aug[2 * pair + parity])

    def use(pair, block, parity, scores):
        top = jnp.max(scores, axis=-1, keepdims=True)
        exps = jnp.exp(scores - top).astype(BF16)
        sums = dot_nn(exps, v_aug[2 * pair + parity])
        if parity == 0:
            held[0] = (sums, top)
            return
        (even, even_top), odd, odd_top = held[0], sums, top
        at, heads = slice(block * rows, (block + 1) * rows), slice(128 * pair, 128 * (pair + 1))
        total = jnp.where(low, odd, even)
        mix_ref[at, heads] = jnp.where(low, even, odd) / pltpu.roll(total, 64, 1)
        log_total = jnp.where(low, odd_top, even_top) + jnp.log(total)
        qfb_ref[at, heads] = (qf_ref[at, :].astype(F32) + three_lanes(-log_total, lanes)).astype(BF16)

    before = None
    for pair in range(wide):
        for block in range(tokens // rows):
            for parity in range(2):
                now = (pair, block, parity, scores_of(pair, block, parity))
                if before is not None:
                    use(*before)
                before = now
    use(*before)


def attention_forward(q, kvs, qf, kf, wide=2, rows=256):
    tokens, width = q.shape
    lanes = 128 * wide
    steps = width // lanes
    length = kf.shape[0]
    parts = len(kvs)
    in_specs = [pl.BlockSpec((tokens, lanes), lambda h: (0, h))]
    in_specs += [pl.BlockSpec((kv.shape[0], lanes), lambda h: (0, h)) for kv in kvs]
    in_specs += [pl.BlockSpec((kv.shape[0], lanes), lambda h: (0, steps + h)) for kv in kvs]
    in_specs += [
        pl.BlockSpec((tokens, 128), lambda h: (0, 0)),
        pl.BlockSpec((length, 128), lambda h: (0, 0)),
    ]
    return pl.pallas_call(
        functools.partial(forward_kernel, parts, wide, rows),
        grid=(steps,),
        in_specs=in_specs,
        out_specs=[
            pl.BlockSpec((tokens, lanes), lambda h: (0, h)),
            pl.BlockSpec((tokens, lanes), lambda h: (0, h)),
        ],
        out_shape=[
            jax.ShapeDtypeStruct((tokens, width), F32),
            jax.ShapeDtypeStruct((tokens, width), BF16),
        ],
        scratch_shapes=[pltpu.VMEM((2 * wide, length, 128), BF16), pltpu.VMEM((2 * wide, length, 128), BF16)],
        compiler_params=pltpu.CompilerParams(vmem_limit_bytes=(8 + 8 * length // 1024) * MIB),
        name="attention_forward",
        cost_estimate=pl.CostEstimate(
            flops=4 * tokens * length * width, bytes_accessed=8 * tokens * width,
            transcendentals=tokens * length * HEADS,
        ),
    )(q, *kvs, *kvs, qf, kf)


def backward_kernel(parts, count, rows, *refs):
    q_ref, gm_ref, qfb_ref, gmf_ref = refs[:4]
    k_refs = refs[4 : 4 + parts]
    v_refs = refs[4 + parts : 4 + 2 * parts]
    kf_ref = refs[4 + 2 * parts]
    rest = refs[5 + 2 * parts :]
    dq_ref = rest[0]
    pair_refs = rest[1 : 1 + parts]
    q_aug, gm_aug, dqt = rest[1 + parts :]
    low_half = (lane_index((1, 128)) < 64).astype(F32)
    halves = (low_half.astype(BF16), (1.0 - low_half).astype(BF16))
    low = lane_index((rows, 128)) < 64
    for pair in range(count):
        heads = slice(128 * pair, 128 * (pair + 1))
        for parity in range(2):
            mine, other = halves[parity], halves[1 - parity]
            q_aug[2 * pair + parity] = q_ref[:, heads] * mine + qfb_ref[:, heads] * other
            gm_aug[2 * pair + parity] = gm_ref[:, heads] * mine + gmf_ref[:, heads] * other
        start = 0
        for k_ref, v_ref, pair_ref in zip(k_refs, v_refs, pair_refs):
            for block in range(k_ref.shape[0] // rows):
                at = slice(block * rows, (block + 1) * rows)
                k, v = k_ref[at, heads], v_ref[at, heads]
                kf = kf_ref[start + block * rows : start + (block + 1) * rows, :]
                dks, dvs = [], []
                for parity in range(2):
                    mine, other = halves[parity], halves[1 - parity]
                    probs = jnp.exp(dot_nt(k * mine + kf * other, q_aug[2 * pair + parity]))
                    slopes = dot_nt(v * mine + other, gm_aug[2 * pair + parity])
                    grads = (probs * slopes).astype(BF16)
                    dvs.append(dot_nn(probs.astype(BF16), gm_ref[:, heads]))
                    dks.append(dot_nn(grads, q_ref[:, heads]))
                    term = dot_tn(k, grads)
                    if start + block == 0:
                        dqt[2 * pair + parity] = term
                    else:
                        dqt[2 * pair + parity] += term
                left, right = 256 * pair, 256 * pair + 128
                pair_ref[at, left:right] = jnp.where(low, dks[0], dks[1]).astype(pair_ref.dtype)
                pair_ref[at, right : right + 128] = jnp.where(low, dvs[0], dvs[1]).astype(pair_ref.dtype)
            start += k_ref.shape[0]
        dq_t = jnp.concatenate([dqt[2 * pair, :64, :], dqt[2 * pair + 1, 64:, :]], axis=0)
        dq_ref[:, heads] = dq_t.T.astype(BF16) * (64.0**-0.5)


def attention_backward(q, gm, qfb, gmf, kvs, kf, first, count, rows=512):
    tokens, width = q.shape
    length = kf.shape[0]
    parts = len(kvs)
    lanes = 128 * count
    steps = width // lanes
    own = lambda i: (0, first // count)
    in_specs = [pl.BlockSpec((tokens, lanes), own)] * 4
    in_specs += [pl.BlockSpec((kv.shape[0], lanes), own) for kv in kvs]
    in_specs += [pl.BlockSpec((kv.shape[0], lanes), lambda i: (0, steps + first // count)) for kv in kvs]
    in_specs += [pl.BlockSpec((length, 128), lambda i: (0, 0))]
    kinds = [F32] + [BF16] * (parts - 1)
    outs = [jax.ShapeDtypeStruct((tokens, 128 * count), BF16)]
    outs += [jax.ShapeDtypeStruct((kv.shape[0], 256 * count), kind) for kv, kind in zip(kvs, kinds)]
    return pl.pallas_call(
        functools.partial(backward_kernel, parts, count, rows),
        grid=(1,),
        in_specs=in_specs,
        out_specs=[pl.BlockSpec(out.shape, lambda i: (0, 0)) for out in outs],
        out_shape=outs,
        scratch_shapes=[
            pltpu.VMEM((2 * count, tokens, 128), BF16),
            pltpu.VMEM((2 * count, tokens, 128), BF16),
            pltpu.VMEM((2 * count, 128, tokens), F32),
        ],
        compiler_params=pltpu.CompilerParams(vmem_limit_bytes=(12 + 4 * length // 1024) * MIB),
        name="attention_backward",
        cost_estimate=pl.CostEstimate(
            flops=10 * tokens * length * 128 * count, bytes_accessed=12 * tokens * 128 * count,
            transcendentals=tokens * length * 2 * count,
        ),
    )(q, gm, qfb, gmf, *kvs, *kvs, kf)


def middle_kernel(pieces, rows, *refs):
    dy_refs = refs[:pieces]
    x_ref, mix_ref, small, w_out, w_up, w_down = refs[pieces : pieces + 6]
    outs = refs[pieces + 6 :]
    gain, shift = small[LN2_GAIN], small[LN2_SHIFT]
    out_refs = outs[:pieces]
    (mixed_ref, two_ref, active_ref, gh_ref, ga_ref, gmid_ref, gm_ref, gmf_ref, vec_ref, dy_ref) = outs[pieces:]
    band = dy_refs[0].shape[0]
    tokens, width = mix_ref.shape
    ff = w_up.shape[1]
    vec_ref[...] = jnp.zeros_like(vec_ref)
    c0 = 0.7978845608028654
    c1 = 0.044715
    row = lax.broadcasted_iota(jnp.int32, (width, width), 0) // 64
    column = lane_index((width, width)) // 64
    opposite = (row == (column + 1 - 2 * (column % 2))).astype(F32).astype(BF16)
    per = rows // band
    for t in range(tokens // rows):
        at = slice(t * rows, (t + 1) * rows)
        x = x_ref[at, :].astype(F32)
        dy = jnp.concatenate([dy_refs[t * per + j][...] for j in range(per)], axis=0)
        dy_ref[at, :] = dy
        mix = mix_ref[at, :]
        mixed = mix.astype(BF16)
        mixed_ref[at, :] = mixed
        middle = x + (dot_nn(mixed, w_out[...]) + small[BIAS_OUT])
        unit, scale = norm_parts(middle)
        two = (unit * gain + shift).astype(BF16)
        two_ref[at, :] = two
        out = middle + small[BIAS_DOWN]
        grad_two = jnp.zeros((rows, width), F32)
        step = 2 * width
        before = None
        for f in range(0, ff + step, step):
            if f < ff:
                fs = slice(f, f + step)
                bias = jnp.concatenate(
                    [small[BIAS_UP + i : BIAS_UP + i + 1] for i in range(f // width, (f + step) // width)], axis=1
                )
                now = (fs, dot_nn(two, w_up[:, fs]) + bias, dot_nt(dy, w_down[fs, :]))
            if before is not None:
                fs, hidden, grad = before
                square = hidden * hidden
                tanh = jnp.tanh(c0 * hidden * (1.0 + c1 * square))
                half = 0.5 * (1.0 + tanh)
                active = (hidden * half).astype(BF16)
                active_ref[at, fs] = active
                out = out + dot_nn(active, w_down[fs, :])
                slope = half + hidden * (0.5 * (1.0 - tanh * tanh)) * (c0 + (3.0 * c0 * c1) * square)
                grad_low = (grad * slope).astype(BF16)
                gh_ref[at, fs] = grad_low
                vec_ref[0:1, fs] += jnp.sum(grad_low.astype(F32), axis=0, keepdims=True)
                grad_two = grad_two + dot_nt(grad_low, w_up[:, fs])
            before = now
        for j in range(per):
            out_refs[t * per + j][...] = out[j * band : (j + 1) * band].astype(BF16)
        dy_wide = dy.astype(F32)
        grad_middle = dy_wide + norm_back(grad_two, unit, scale, gain)
        gmid_ref[at, :] = grad_middle
        vec_ref[1:2, :width] += jnp.sum(grad_two * unit, axis=0, keepdims=True)
        vec_ref[2:3, :width] += jnp.sum(grad_two, axis=0, keepdims=True)
        vec_ref[3:4, :width] += jnp.sum(dy_wide, axis=0, keepdims=True)
        grad_attn = grad_middle.astype(BF16)
        ga_ref[at, :] = grad_attn
        vec_ref[4:5, :width] += jnp.sum(grad_attn.astype(F32), axis=0, keepdims=True)
        gm = dot_nt(grad_attn, w_out[...]).astype(BF16)
        gm_ref[at, :] = gm
        high, mid, _ = split_three(gm.astype(F32) * mix)
        inner = dot_nn(high, opposite) + dot_nn(mid, opposite)
        gmf_ref[at, :] = three_lanes(-inner, lane_index((rows, width))).astype(BF16)


def middle_part(dys, x, mix, small, w_out, w_up, w_down, rows=512):
    tokens, width = mix.shape
    ff = w_up.shape[1]
    shape = jax.ShapeDtypeStruct
    return pl.pallas_call(
        functools.partial(middle_kernel, len(dys), rows),
        out_shape=[shape(dy.shape, BF16) for dy in dys]
        + [
            shape((tokens, width), BF16),
            shape((tokens, width), BF16),
            shape((tokens, ff), BF16),
            shape((tokens, ff), BF16),
            shape((tokens, width), BF16),
            shape((tokens, width), F32),
            shape((tokens, width), BF16),
            shape((tokens, width), BF16),
            shape((8, ff), F32),
            shape((tokens, width), BF16),
        ],
        compiler_params=pltpu.CompilerParams(vmem_limit_bytes=24 * MIB),
        name="middle_part",
        cost_estimate=pl.CostEstimate(
            flops=2 * tokens * width * (4 * ff + 5 * width), bytes_accessed=8 * 1024 * 1024,
            transcendentals=tokens * ff,
        ),
    )(*dys, x, mix, small, w_out, w_up, w_down)


def columns_by_way(mode, columns):
    middle = columns // 256 * 128
    return {
        "x": ((0, columns, 0),),
        "y": ((0, columns, 1),),
        "xy": ((0, middle, 0), (middle, columns, 1)),
    }[mode]


def place_pieces(marks, mode, total, keep_ref, send_ref):
    piece = total.shape[0] // PIECES
    for which, target in enumerate((keep_ref, send_ref)):
        for start, stop, way in columns_by_way(mode, total.shape[1]):
            for j in range(PIECES // 2):
                source = pl.multiple_of((marks[2 * which + way] ^ j) * piece, piece)
                spot = slice(j * piece, (j + 1) * piece)
                target[spot, start:stop] = total[pl.ds(source, piece), start:stop].astype(BF16)


def smem():
    return pl.BlockSpec(memory_space=pltpu.SMEM)


def vmem():
    return pl.BlockSpec(memory_space=pltpu.VMEM)


def weight_grad_kernel(count, mode, marks, *refs):
    pairs = refs[: 2 * count]
    keep_ref, send_ref, total = refs[2 * count :]
    start = 0
    for left, right in zip(pairs[0::2], pairs[1::2]):
        stop = start + right.shape[1]
        for r in range(0, left.shape[1], 256):
            total[r : r + 256, start:stop] = dot_tn(left[:, r : r + 256], right[...])
        start = stop
    place_pieces(marks, mode, total, keep_ref, send_ref)


def weight_grad(marks, mode, pairs, name):
    rows = pairs[0][0].shape[1]
    columns = sum(right.shape[1] for _, right in pairs)
    depth = pairs[0][0].shape[0]
    half = jax.ShapeDtypeStruct((rows // 2, columns), BF16)
    flat = [array for pair in pairs for array in pair]
    return pl.pallas_call(
        functools.partial(weight_grad_kernel, len(pairs), mode),
        in_specs=[smem()] + [vmem()] * len(flat),
        out_specs=[vmem(), vmem()],
        out_shape=[half, half],
        scratch_shapes=[pltpu.VMEM((rows, columns), F32)],
        compiler_params=pltpu.CompilerParams(vmem_limit_bytes=16 * MIB),
        name=name,
        cost_estimate=pl.CostEstimate(
            flops=2 * rows * columns * depth, bytes_accessed=6 * rows * columns, transcendentals=0
        ),
    )(marks, *flat)


def qkv_grad_kernel(count, mode, *refs):
    marks, normed, small, w_ref, vec_ref = refs[:5]
    dqs, owns, gots = (refs[5 + i * count : 5 + (i + 1) * count] for i in range(3))
    packed, keep_ref, send_ref, total = refs[5 + 3 * count :]
    width = normed.shape[1]
    share = width // count
    for t in range(count):
        packed[:, share * t : share * (t + 1)] = dqs[t][...]
        both = (owns[t][...] + gots[t][...].astype(F32)).astype(BF16)
        for i in range(2 * share // 128):
            at = (i % 2 + 1) * width + share * t + 128 * (i // 2)
            packed[:, at : at + 128] = both[:, 128 * i : 128 * (i + 1)]
    for r in range(0, width, 256):
        total[r : r + 256, : 3 * width] = dot_tn(normed[:, r : r + 256], packed[...])
    sums = jnp.sum(packed[...].astype(F32), axis=0, keepdims=True)
    terms = jnp.concatenate(split_three(jnp.broadcast_to(sums, (16, 3 * width))), axis=0)
    spread = dot_nt(terms, w_ref[...])
    shift_row = spread[0:1] + (spread[16:17] + spread[32:33])
    rows = jnp.zeros((width, 128), F32)
    for at in range(0, 3 * width, 128):
        rows = rows + total[:, at : at + 128] * w_ref[:, at : at + 128].astype(F32)
    gain_row = jnp.sum(rows.T, axis=0, keepdims=True)
    gain_row = (gain_row - small[LN1_SHIFT] * shift_row) / small[LN1_GAIN]
    vectors = [vec_ref[0:1, :]] + [vec_ref[i : i + 1, :width] for i in range(1, 5)]
    vectors += [sums[:, :width], sums[:, 2 * width :], gain_row, shift_row]
    tiles = [row[:, at : at + VECTOR_LANES] for row in vectors for at in range(0, row.shape[1], VECTOR_LANES)]
    piece = width // PIECES
    per = len(tiles) // PIECES
    total[:, 3 * width :] = jnp.zeros((width, VECTOR_LANES), F32)
    for i, tile in enumerate(tiles):
        at = (i // per) * piece + i % per
        total[at : at + 1, 3 * width :] = tile
    place_pieces(marks, mode, total, keep_ref, send_ref)


def qkv_grad(marks, mode, normed, small, w_qkv, vec, dqs, owns, gots):
    tokens, width = normed.shape
    columns = 3 * width + VECTOR_LANES
    half = jax.ShapeDtypeStruct((width // 2, columns), BF16)
    flat = [normed, small, w_qkv, vec, *dqs, *owns, *gots]
    return pl.pallas_call(
        functools.partial(qkv_grad_kernel, len(dqs), mode),
        in_specs=[smem()] + [vmem()] * len(flat),
        out_specs=[vmem()] * 3,
        out_shape=[jax.ShapeDtypeStruct((tokens, 3 * width), BF16), half, half],
        scratch_shapes=[pltpu.VMEM((width, columns), F32)],
        compiler_params=pltpu.CompilerParams(vmem_limit_bytes=16 * MIB),
        name="qkv_grad",
        cost_estimate=pl.CostEstimate(
            flops=6 * tokens * width * width, bytes_accessed=18 * tokens * width, transcendentals=0
        ),
    )(marks, *flat)


def last_kernel(pieces, packed, gmid_ref, small, w_ref, x_ref, *out_refs):
    band = out_refs[0].shape[0]
    grad = dot_nt(packed[...], w_ref[...])
    unit, scale = norm_parts(x_ref[...].astype(F32))
    result = (gmid_ref[...] + norm_back(grad, unit, scale, small[LN1_GAIN])).astype(BF16)
    for j in range(pieces):
        out_refs[j][...] = result[j * band : (j + 1) * band]


def last_part(packed, gmid, small, w_qkv, x, pieces):
    tokens, width = gmid.shape
    return pl.pallas_call(
        functools.partial(last_kernel, pieces),
        out_shape=[jax.ShapeDtypeStruct((tokens // pieces, width), BF16)] * pieces,
        compiler_params=pltpu.CompilerParams(vmem_limit_bytes=12 * MIB),
        name="last_part",
        cost_estimate=pl.CostEstimate(
            flops=6 * tokens * width * width, bytes_accessed=10 * tokens * width, transcendentals=0
        ),
    )(packed, gmid, small, w_qkv, x)


def assemble_kernel(segments, mode, per, marks, *refs):
    own_far, out_refs = refs[:2], refs[2:]
    half = PIECES // 2
    piece = own_far[0].shape[0] // half
    step = pl.program_id(0)
    for i in range(per):
        index = step * per + i

        def fill(which, i=i, index=index):
            source = own_far[which]
            for low, high, way in columns_by_way(mode, source.shape[1]):
                at = pl.ds(pl.multiple_of(((index ^ marks[2 * which + way]) % half) * piece, piece), piece)
                for start, stop, which_out, tall, offset in segments:
                    first, last = max(start, low), min(stop, high)
                    if first < last:
                        spot = slice(i * tall + offset, i * tall + offset + piece)
                        out_refs[which_out][spot, first - start : last - start] = source[at, first:last].astype(F32)

        mine = index // half == marks[0] // half
        pl.when(mine)(functools.partial(fill, 0))
        pl.when(jnp.logical_not(mine))(functools.partial(fill, 1))


def assemble(marks, mode, parts, segments, shapes, name):
    steps = 2
    per = PIECES // steps
    size = sum(rows * columns for rows, columns in shapes)
    return pl.pallas_call(
        functools.partial(assemble_kernel, segments, mode, per),
        grid=(steps,),
        in_specs=[smem()] + [vmem()] * 2,
        out_specs=[pl.BlockSpec((rows // steps, w), lambda i: (i, 0)) for rows, w in shapes],
        out_shape=[jax.ShapeDtypeStruct(shape, F32) for shape in shapes],
        compiler_params=pltpu.CompilerParams(vmem_limit_bytes=16 * MIB),
        name=name,
        cost_estimate=pl.CostEstimate(flops=size, bytes_accessed=6 * size, transcendentals=0),
    )(marks, *parts)


def return_kernel(halves, row_ref, *refs):
    out, sems = refs[-2], refs[-1]
    copies = []
    for i, (ref, (j, half)) in enumerate(zip(refs, halves)):
        width = ref.shape[1]
        at = 0 if half is None else half * width
        copies.append(pltpu.make_async_copy(ref, out.at[row_ref[0] ^ j, :, at : at + width], sems.at[i]))
    for copy in copies:
        copy.start()
    for copy in copies:
        copy.wait()


def return_rows(row, own, halves, name):
    flat = [own] + [piece for half in halves for piece in half]
    places = [(0, None)] + [(j + 1, h) for h, half in enumerate(halves) for j in range(len(half))]
    pieces = len(halves[0]) + 1
    return pl.pallas_call(
        functools.partial(return_kernel, places),
        in_specs=[smem()] + [vmem()] * len(flat),
        out_specs=pl.BlockSpec(memory_space=pl.ANY),
        out_shape=jax.ShapeDtypeStruct((pieces, *own.shape), BF16),
        scratch_shapes=[pltpu.SemaphoreType.DMA((len(flat),))],
        compiler_params=pltpu.CompilerParams(vmem_limit_bytes=4 * MIB),
        name=name,
    )(row, *flat)


def swap(value, axis, size, mask):
    return lax.ppermute(value, axis, [(i, i ^ mask) for i in range(size)])


class Order:
    def __init__(self):
        self.last = ()

    def enter(self, *values):
        return lax.optimization_barrier((values, self.last))[0]

    def leave(self, *values):
        self.last = values


class Cargo:
    def __init__(self, pieces):
        self.pieces = pieces
        width = pieces[0].shape[1] // 2
        self.columns = [slice(0, width), slice(width, 2 * width)]
        self.came = [[None] * len(pieces) for _ in range(2)]
        self.onward = [None, None]

    def load(self, half, way, first):
        columns = self.columns[half]
        far = self.pieces[3][:, columns] if first else self.onward[half]
        return jnp.concatenate([self.pieces[way + 1][:, columns], far], axis=0)

    def land(self, half, way, first, got):
        band = got.shape[0] // 2
        self.came[half][way + 1] = got[:band]
        if first:
            self.onward[half] = got[band:]
        else:
            self.came[half][3] = got[band:]


def fold(value, rows):
    if rows < value.shape[0]:
        return jnp.concatenate([value[at : at + rows] for at in range(0, value.shape[0], rows)], axis=1)
    wide = value.shape[1] * value.shape[0] // rows
    return jnp.concatenate([value[:, at : at + wide] for at in range(0, value.shape[1], wide)], axis=0)


class Wave:
    def __init__(self, order, keep, send, marks, mode, layout, core, ways, deep, rest):
        self.order, self.core, self.ways, self.deep, self.rest = order, core, ways, deep, rest
        self.marks, self.mode, self.layout = marks, mode, layout
        self.parts = columns_by_way(mode, keep.shape[1])
        self.value, self.got = [keep], [core(send)]
        self.cargo, self.aboard = {}, None
        order.leave(send)

    def arrived(self):
        count = len(self.value)
        values = self.order.enter(*self.value, *self.got)
        kept, came = values[:count], list(values[count:])
        if self.aboard is not None:
            cargo, first, ways, shape = self.aboard
            for i, way in enumerate(ways):
                own = self.parts[i][1] - self.parts[i][0]
                cargo.land(i, way, first, fold(came[i][:, own:], shape[0]))
                came[i] = came[i][:, :own]
            self.aboard = None
        return list(zip(kept, came))

    def added(self):
        return [add_low(one, two) for one, two in self.arrived()]

    def split(self, value):
        return [value[:, start:stop] for start, stop, _ in self.parts]

    def travel(self, step, values, key):
        ways = [(step + way) % 2 for _, _, way in self.parts]
        if key in self.cargo:
            cargo, first = self.cargo[key]
            loads = [cargo.load(i, way, first) for i, way in enumerate(ways)]
            self.aboard = (cargo, first, ways, loads[0].shape)
            values = [
                jnp.concatenate([value, fold(load, value.shape[0])], axis=1) for value, load in zip(values, loads)
            ]
        self.got = [self.ways[way](value) for way, value in zip(ways, values)]
        self.order.leave(*values)

    def plane(self, step):
        values = self.added()
        if step == 0:
            values = self.split(values[0])
        half = values[0].shape[0] // 2
        self.value = [value[:half] for value in values]
        self.travel(step, [value[half:] for value in values], ("out", step))

    def line(self):
        values = self.added()
        half = values[0].shape[0] // 2
        self.value = [jnp.concatenate([value[:half] for value in values], axis=1)]
        sent = jnp.concatenate([value[half:] for value in values], axis=1)
        self.got = [self.deep(sent)]
        self.order.leave(sent)

    def exchanges(self):
        for send in self.rest:
            self.value = self.added()
            self.got = [send(self.value[0])]
            self.order.leave(*self.value)

    def line_back(self):
        self.value = self.added()
        self.got = [self.deep(self.value[0])]
        self.order.leave(*self.value)

    def joined(self):
        return [jnp.concatenate(pair, axis=0) for pair in self.arrived()]

    def plane_back(self, step):
        values = self.joined()
        self.value = self.split(values[0]) if step == 1 else values
        self.travel(step, self.value, ("back", step))

    def core_back(self):
        self.value = [jnp.concatenate(self.joined(), axis=1)]
        self.got = [self.core(self.value[0])]
        self.order.leave(*self.value)

    def wait(self):
        self.got = list(self.order.enter(*self.got))
        self.order.leave(*self.got)

    def finish(self):
        ((own, far),) = self.arrived()
        self.sums = assemble(self.marks, self.mode, (own, far), *self.layout)
        self.order.leave(*self.sums)

    def steps(self):
        yield functools.partial(self.plane, 0)
        yield functools.partial(self.plane, 1)
        yield self.line
        yield self.exchanges
        yield self.line_back
        yield functools.partial(self.plane_back, 1)
        yield functools.partial(self.plane_back, 0)
        yield self.core_back
        yield self.finish


def add_low(one, two):
    return (one.astype(F32) + two.astype(F32)).astype(BF16)


def after(value, *others):
    return lax.optimization_barrier((value, others))[0]


def bits_of(axis, size):
    found, mask = [], 1
    while mask < size:
        found.append((axis, size, mask, (lax.axis_index(axis) // mask) % 2))
        mask *= 2
    return found


def per_device(
    seq_size, row_size,
    block_input, segment_ids, ln1_gain, ln1_shift, w_qkv, bias_query, bias_value, w_out, bias_out,
    ln2_gain, ln2_shift, w_up, bias_up, w_down, bias_down, out_grad,
):
    rows, band, width = block_input.shape
    length = segment_ids.shape[1]
    share = seq_size // rows
    tokens = rows * band
    crops = max(length // (4 * band), 1)
    place = lax.axis_index("seq")
    my_row, my_part = place // share, place % share

    def deal(pieces):
        got = [pieces[0]]
        for j in range(1, rows):
            turn = [(s, ((s // share) ^ j) * share + s % share) for s in range(seq_size)]
            got.append(lax.ppermute(pieces[j], "seq", turn))
        return got

    def pick(array):
        return [lax.dynamic_index_in_dim(array, my_row ^ j, 0, False) for j in range(rows)]

    xs = deal(pick(block_input))
    dys = pick(out_grad)

    own_row = lax.dynamic_index_in_dim(segment_ids, my_row, 0, False).reshape(seq_size, band)
    key_ids = jnp.concatenate(
        [
            lax.dynamic_index_in_dim(own_row, (my_row ^ j) * share + (my_part ^ i), 0, False)
            for i in range(share)
            for j in range(rows)
        ]
    )
    spot = jnp.arange(128) % 64
    same = key_ids[:, None] == spot[None, :]
    used = spot[None, :] < crops
    ones = (spot >= LSE_LANE) & (spot < LSE_LANE + 3)
    kf = jnp.where(used, jnp.where(same, 0.0, -1.0), jnp.where(ones, 1.0, 0.0)).astype(BF16)
    qf = jnp.where(used & same, BIG, 0.0).astype(BF16)[:tokens]

    small = jnp.stack(
        [ln1_gain, ln1_shift, bias_query, bias_value, bias_out, ln2_gain, ln2_shift, bias_down]
    )
    small = jnp.concatenate([small, bias_up.reshape(-1, width)], axis=0)
    shape = jax.ShapeDtypeStruct
    x, normed, q, kv = pl.pallas_call(
        functools.partial(qkv_kernel, rows, width),
        out_shape=[
            shape((tokens, width), BF16),
            shape((tokens, width), BF16),
            shape((tokens, width), BF16),
            shape((tokens, 2 * width), BF16),
        ],
        compiler_params=pltpu.CompilerParams(vmem_limit_bytes=12 * MIB),
        name="norm_and_project",
    )(*xs, small, w_qkv)


    dys = list(lax.optimization_barrier((dys, kv))[0])
    dys = deal(dys)
    seq_bits = bits_of("seq", seq_size)
    row_bits = bits_of("row", row_size)
    part_bits = [bit for bit in seq_bits if bit[2] < share]
    kvs, whole = [kv], kv
    for axis, size, mask, own in part_bits:
        got = swap(whole, axis, size, mask)
        kvs.append(got)
        if mask * 2 < share:
            whole = jnp.concatenate([whole, got], 0)

    mix, qfb = attention_forward(q, kvs, qf, kf)
    *outs, mixed, two, active, grad_hidden, grad_attn, grad_middle, gm, gmf, vec, dy = middle_part(
        dys, x, mix, small, w_out, w_up, w_down
    )

    def straight(bit):
        return lambda value: swap(value, *bit[:3])

    plane = [bit for bit in seq_bits if bit[2] >= share]
    core, one, two_, deep = seq_bits[0][3], plane[0][3], plane[1][3], row_bits[0][3]
    ways = (straight(plane[0]), straight(plane[1]))
    rest = [straight(bit) for bit in row_bits[1:] + plane[2:] + part_bits[1:]]
    route = (straight(seq_bits[0]), ways, straight(row_bits[0]), rest)
    left, right = one * 4 + two_ * 2 + deep, two_ * 4 + one * 2 + deep
    mine, other = core * 8, 8 - core * 8
    marks = jnp.stack([mine + left, mine + right, other + left, other + right]).astype(jnp.int32)

    pairs = width // 128
    ff = w_up.shape[1]
    tall = width // PIECES
    down_layout = ([(0, width, 0, ff // PIECES, 0)], [(ff, width)], "assemble_down")
    up_segments = [(0, ff, 0, tall, 0), (ff, ff + width, 1, tall, 0)]
    up_layout = (up_segments, [(width, ff), (width, width)], "assemble_up_out")
    qkv_segments = [(0, 3 * width, 0, tall, 0), (3 * width, 3 * width + VECTOR_LANES, 1, tall, 0)]
    qkv_layout = (qkv_segments, [(width, 3 * width), (width, VECTOR_LANES)], "assemble_qkv")
    row = my_row.astype(jnp.int32).reshape(1)

    order = Order()
    terms, gots, steps, done = [], [], {}, {}

    def backward():
        (grad,) = order.enter(gm)
        terms.append(attention_backward(q, grad, qfb, gmf, kvs, kf, AT_ONCE * len(terms), AT_ONCE))
        order.leave(*terms[-1])
        if share == 2:
            gots.append(straight(part_bits[0])(terms[-1][2]))

    def start_wave(letter, pairs_of, name, layout):
        flat = order.enter(*[array for pair in pairs_of for array in pair])
        keep, send = weight_grad(marks, MODES[letter], list(zip(flat[0::2], flat[1::2])), name)
        done[letter] = Wave(order, keep, send, marks, MODES[letter], layout, *route)
        steps[letter] = done[letter].steps()
        if letter == "d":
            ride("d", outs, "out", "o")

    def start_qkv():
        own_terms, far_terms = [term[1] for term in terms], gots
        if share != 2:
            both = jnp.concatenate(
                [jnp.concatenate([part.astype(BF16) for part in term[1:]], 0) for term in terms], axis=1
            )
            for bit in reversed(part_bits):
                half = both.shape[0] // 2
                kept, got = both[:half], straight(bit)(both[half:])
                both = add_low(kept, got)
            cuts = [slice(256 * AT_ONCE * t, 256 * AT_ONCE * (t + 1)) for t in range(len(terms))]
            own_terms = [kept[:, cut].astype(F32) for cut in cuts]
            far_terms = [got[:, cut] for cut in cuts]
        (vec_,) = order.enter(vec)
        dqs = [term[0] for term in terms]
        done["p"], keep, send = qkv_grad(marks, MODES["q"], normed, small, w_qkv, vec_, dqs, own_terms, far_terms)
        done["q"] = Wave(order, keep, send, marks, MODES["q"], qkv_layout, *route)
        steps["q"] = done["q"].steps()

    def last():
        (packed,) = order.enter(done["p"])
        pieces = last_part(packed, grad_middle, small, w_qkv, x, rows)
        order.leave(*pieces)
        ride("u", pieces, "back", "i")

    def ride(letter, pieces, stage, name):
        done[name] = Cargo(pieces)
        steps_ = (0, 1) if stage == "out" else (1, 0)
        for i, step in enumerate(steps_):
            done[letter].cargo[(stage, step)] = (done[name], i == 0)

    def take_back(name):
        cargo = done[name]
        halves = [list(order.enter(*half[1:])) for half in cargo.came]
        done[name] = return_rows(row, cargo.pieces[0], halves, "return_rows")
        order.leave(done[name])

    actions = {
        "b": backward,
        "D": lambda: start_wave("d", [(active, dy)], "grad_down", down_layout),
        "U": lambda: start_wave("u", [(two, grad_hidden), (mixed, grad_attn)], "grad_up_out", up_layout),
        "G": start_qkv,
        "L": last,
        "O": lambda: take_back("o"),
        "I": lambda: take_back("i"),
        "d": lambda: next(steps["d"])(),
        "u": lambda: next(steps["u"])(),
        "q": lambda: next(steps["q"])(),
    }
    def wait(which):
        if which.isdigit():
            if share == 2:
                (gots[int(which)],) = order.enter(gots[int(which)])
                order.leave(gots[int(which)])
        else:
            done[which].wait()

    for word in SCHEDULE:
        if word[0] == "w":
            wait(word[1])
        else:
            actions[word]()
    result, input_grad = done["o"], done["i"]
    (sum_down,) = done["d"].sums
    sum_up, sum_out = done["u"].sums
    sum_qkv, tiles = done["q"].sums

    count = (ff + 8 * width) // VECTOR_LANES // PIECES
    vectors = tiles.reshape(PIECES, -1, VECTOR_LANES)[:, :count].reshape(-1)
    cuts = [ff + i * width for i in range(9)]
    names = [vectors[a:b] for a, b in zip(cuts[:-1], cuts[1:])]
    ln2_gain_sum, ln2_shift_sum, bias_down_sum, bias_out_sum = names[:4]
    bias_q_sum, bias_v_sum, ln1_gain_sum, ln1_shift_sum = names[4:]
    return (
        result,
        input_grad,
        ln1_gain_sum,
        ln1_shift_sum,
        sum_qkv,
        bias_q_sum,
        bias_v_sum,
        sum_out,
        bias_out_sum,
        ln2_gain_sum,
        ln2_shift_sum,
        sum_up,
        vectors[:ff],
        sum_down,
        bias_down_sum,
    )


def solution(mesh):
    split = P("row", "seq", None)
    placed = (split, P("row", None)) + (P(),) * 13 + (split,)
    return jax.shard_map(
        functools.partial(per_device, mesh.shape["seq"], mesh.shape["row"]),
        mesh=mesh,
        in_specs=placed,
        out_specs=(split, split) + (P(),) * 13,
        check_vma=False,
    )
```

```python
import functools

import jax
import jax.numpy as jnp
from jax import lax
from jax.experimental import pallas as pl
from jax.experimental.pallas import tpu as pltpu
from jax.sharding import PartitionSpec as P

HEADS = 8
EPSILON = 1e-06
BIG = 1e30
LSE_LANE = 16
PIECES = 16
AT_ONCE = 2
SCHEDULE = (
    "U", "D", "u", "b", "u", "b", "u", "d", "G", "u", "q", "d", "u", "L", "q", "d",
    "u", "q", "d", "q", "u", "d", "O", "q", "d", "u", "q", "d", "q", "I", "u", "d",
    "q", "d", "q",
)
MODES = {"d": "xy", "u": "xy", "q": "xy"}
VECTOR_LANES = 128
F32 = jnp.float32
BF16 = jnp.bfloat16
MIB = 1024 * 1024
LN1_GAIN, LN1_SHIFT, BIAS_Q, BIAS_V, BIAS_OUT, LN2_GAIN, LN2_SHIFT, BIAS_DOWN = (
    slice(i, i + 1) for i in range(8)
)
BIAS_UP = 8


def dot_nn(a, b):
    return lax.dot_general(a, b, (((1,), (0,)), ((), ())), preferred_element_type=F32)


def dot_nt(a, b):
    return lax.dot_general(a, b, (((1,), (1,)), ((), ())), preferred_element_type=F32)


def dot_tn(a, b):
    return lax.dot_general(a, b, (((0,), (0,)), ((), ())), preferred_element_type=F32)


def split_three(value):
    high = value.astype(BF16)
    rest = value - high.astype(F32)
    middle = rest.astype(BF16)
    low = (rest - middle.astype(F32)).astype(BF16)
    return high, middle, low


def lane_index(shape):
    return lax.broadcasted_iota(jnp.int32, shape, len(shape) - 1)


def three_lanes(value, lanes):
    high, middle, low = split_three(value)
    spot = lanes % 64
    out = jnp.where(spot == LSE_LANE, high.astype(F32), 0.0)
    out = jnp.where(spot == LSE_LANE + 1, middle.astype(F32), out)
    return jnp.where(spot == LSE_LANE + 2, low.astype(F32), out)


def norm_parts(value):
    centre = jnp.mean(value, axis=-1, keepdims=True)
    centred = value - centre
    spread = jnp.mean(centred * centred, axis=-1, keepdims=True)
    scale = lax.rsqrt(spread + EPSILON)
    return centred * scale, scale


def norm_back(grad, unit, scale, gain):
    grad_unit = grad * gain
    first = jnp.mean(grad_unit, axis=-1, keepdims=True)
    second = jnp.mean(grad_unit * unit, axis=-1, keepdims=True)
    return scale * (grad_unit - first - unit * second)


def fetch_kernel(source, target, sem):
    copy = pltpu.make_async_copy(source, target, sem)
    copy.start()
    copy.wait()


def fetch(array):
    return pl.pallas_call(
        fetch_kernel,
        in_specs=[pl.BlockSpec(memory_space=pl.ANY)],
        out_specs=vmem(),
        out_shape=jax.ShapeDtypeStruct(array.shape, array.dtype),
        scratch_shapes=[pltpu.SemaphoreType.DMA],
        compiler_params=pltpu.CompilerParams(vmem_limit_bytes=8 * MIB),
        name="fetch",
    )(array)


def qkv_kernel(pieces, width, *refs):
    x_refs = refs[:pieces]
    small, w_ref, x_ref, normed_ref, q_ref, kv_ref = refs[pieces:]
    band = x_refs[0].shape[0]
    for j in range(pieces):
        x_ref[j * band : (j + 1) * band, :] = x_refs[j][...]
        unit, _ = norm_parts(x_refs[j][...].astype(F32))
        normed_ref[j * band : (j + 1) * band, :] = (unit * small[LN1_GAIN] + small[LN1_SHIFT]).astype(BF16)
    normed = normed_ref[...]
    q = dot_nn(normed, w_ref[:, :width])
    q_ref[...] = ((q + small[BIAS_Q]) * (width // HEADS) ** -0.5).astype(BF16)
    kv_ref[:, :width] = dot_nn(normed, w_ref[:, width : 2 * width]).astype(BF16)
    kv_ref[:, width:] = (dot_nn(normed, w_ref[:, 2 * width :]) + small[BIAS_V]).astype(BF16)


def forward_kernel(parts, wide, rows, *refs):
    q_ref = refs[0]
    k_refs = refs[1 : 1 + parts]
    v_refs = refs[1 + parts : 1 + 2 * parts]
    qf_ref, kf_ref, mix_ref, qfb_ref, k_aug, v_aug = refs[1 + 2 * parts :]
    tokens = q_ref.shape[0]
    low_half = (lane_index((1, 128)) < 64).astype(F32)
    halves = (low_half.astype(BF16), (1.0 - low_half).astype(BF16))
    for pair in range(wide):
        at = slice(128 * pair, 128 * (pair + 1))
        for parity in range(2):
            mine, other = halves[parity], halves[1 - parity]
            start = 0
            for k_ref, v_ref in zip(k_refs, v_refs):
                stop = start + k_ref.shape[0]
                k_aug[2 * pair + parity, start:stop, :] = k_ref[:, at] * mine + kf_ref[start:stop, :] * other
                v_aug[2 * pair + parity, start:stop, :] = v_ref[:, at] * mine + other
                start = stop
    lanes = lane_index((rows, 128))
    low = lanes < 64
    held = {}

    def scores_of(pair, block, parity):
        at, heads = slice(block * rows, (block + 1) * rows), slice(128 * pair, 128 * (pair + 1))
        q = q_ref[at, heads] * halves[parity] + qf_ref[at, :] * halves[1 - parity]
        return dot_nt(q, k_aug[2 * pair + parity])

    def use(pair, block, parity, scores):
        top = jnp.max(scores, axis=-1, keepdims=True)
        exps = jnp.exp(scores - top).astype(BF16)
        sums = dot_nn(exps, v_aug[2 * pair + parity])
        if parity == 0:
            held[0] = (sums, top)
            return
        (even, even_top), odd, odd_top = held[0], sums, top
        at, heads = slice(block * rows, (block + 1) * rows), slice(128 * pair, 128 * (pair + 1))
        total = jnp.where(low, odd, even)
        mix_ref[at, heads] = jnp.where(low, even, odd) / pltpu.roll(total, 64, 1)
        log_total = jnp.where(low, odd_top, even_top) + jnp.log(total)
        qfb_ref[at, heads] = (qf_ref[at, :].astype(F32) + three_lanes(-log_total, lanes)).astype(BF16)

    before = None
    for pair in range(wide):
        for block in range(tokens // rows):
            for parity in range(2):
                now = (pair, block, parity, scores_of(pair, block, parity))
                if before is not None:
                    use(*before)
                before = now
    use(*before)


def attention_forward(q, kvs, qf, kf, wide=2, rows=256):
    tokens, width = q.shape
    lanes = 128 * wide
    steps = width // lanes
    length = kf.shape[0]
    parts = len(kvs)
    in_specs = [pl.BlockSpec((tokens, lanes), lambda h: (0, h))]
    in_specs += [pl.BlockSpec((kv.shape[0], lanes), lambda h: (0, h)) for kv in kvs]
    in_specs += [pl.BlockSpec((kv.shape[0], lanes), lambda h: (0, steps + h)) for kv in kvs]
    in_specs += [
        pl.BlockSpec((tokens, 128), lambda h: (0, 0)),
        pl.BlockSpec((length, 128), lambda h: (0, 0)),
    ]
    return pl.pallas_call(
        functools.partial(forward_kernel, parts, wide, rows),
        grid=(steps,),
        in_specs=in_specs,
        out_specs=[
            pl.BlockSpec((tokens, lanes), lambda h: (0, h)),
            pl.BlockSpec((tokens, lanes), lambda h: (0, h)),
        ],
        out_shape=[
            jax.ShapeDtypeStruct((tokens, width), F32),
            jax.ShapeDtypeStruct((tokens, width), BF16),
        ],
        scratch_shapes=[pltpu.VMEM((2 * wide, length, 128), BF16), pltpu.VMEM((2 * wide, length, 128), BF16)],
        compiler_params=pltpu.CompilerParams(vmem_limit_bytes=(8 + 8 * length // 1024) * MIB),
        name="attention_forward",
        cost_estimate=pl.CostEstimate(
            flops=4 * tokens * length * width, bytes_accessed=8 * tokens * width,
            transcendentals=tokens * length * HEADS,
        ),
    )(q, *kvs, *kvs, qf, kf)


def backward_kernel(parts, count, rows, *refs):
    q_ref, gm_ref, qfb_ref, gmf_ref = refs[:4]
    k_refs = refs[4 : 4 + parts]
    v_refs = refs[4 + parts : 4 + 2 * parts]
    kf_ref = refs[4 + 2 * parts]
    rest = refs[5 + 2 * parts :]
    dq_ref = rest[0]
    pair_refs = rest[1 : 1 + parts]
    q_aug, gm_aug, dqt = rest[1 + parts :]
    low_half = (lane_index((1, 128)) < 64).astype(F32)
    halves = (low_half.astype(BF16), (1.0 - low_half).astype(BF16))
    low = lane_index((rows, 128)) < 64
    for pair in range(count):
        heads = slice(128 * pair, 128 * (pair + 1))
        for parity in range(2):
            mine, other = halves[parity], halves[1 - parity]
            q_aug[2 * pair + parity] = q_ref[:, heads] * mine + qfb_ref[:, heads] * other
            gm_aug[2 * pair + parity] = gm_ref[:, heads] * mine + gmf_ref[:, heads] * other
        start = 0
        for k_ref, v_ref, pair_ref in zip(k_refs, v_refs, pair_refs):
            for block in range(k_ref.shape[0] // rows):
                at = slice(block * rows, (block + 1) * rows)
                k, v = k_ref[at, heads], v_ref[at, heads]
                kf = kf_ref[start + block * rows : start + (block + 1) * rows, :]
                dks, dvs = [], []
                for parity in range(2):
                    mine, other = halves[parity], halves[1 - parity]
                    probs = jnp.exp(dot_nt(k * mine + kf * other, q_aug[2 * pair + parity]))
                    slopes = dot_nt(v * mine + other, gm_aug[2 * pair + parity])
                    grads = (probs * slopes).astype(BF16)
                    dvs.append(dot_nn(probs.astype(BF16), gm_ref[:, heads]))
                    dks.append(dot_nn(grads, q_ref[:, heads]))
                    term = dot_tn(k, grads)
                    if start + block == 0:
                        dqt[2 * pair + parity] = term
                    else:
                        dqt[2 * pair + parity] += term
                left, right = 256 * pair, 256 * pair + 128
                pair_ref[at, left:right] = jnp.where(low, dks[0], dks[1]).astype(pair_ref.dtype)
                pair_ref[at, right : right + 128] = jnp.where(low, dvs[0], dvs[1]).astype(pair_ref.dtype)
            start += k_ref.shape[0]
        dq_t = jnp.concatenate([dqt[2 * pair, :64, :], dqt[2 * pair + 1, 64:, :]], axis=0)
        dq_ref[:, heads] = dq_t.T.astype(BF16) * (64.0**-0.5)


def attention_backward(q, gm, qfb, gmf, kvs, kf, first, count, rows=512):
    tokens, width = q.shape
    length = kf.shape[0]
    parts = len(kvs)
    lanes = 128 * count
    steps = width // lanes
    own = lambda i: (0, first // count)
    in_specs = [pl.BlockSpec((tokens, lanes), own)] * 4
    in_specs += [pl.BlockSpec((kv.shape[0], lanes), own) for kv in kvs]
    in_specs += [pl.BlockSpec((kv.shape[0], lanes), lambda i: (0, steps + first // count)) for kv in kvs]
    in_specs += [pl.BlockSpec((length, 128), lambda i: (0, 0))]
    kinds = [F32] + [BF16] * (parts - 1)
    outs = [jax.ShapeDtypeStruct((tokens, 128 * count), BF16)]
    outs += [jax.ShapeDtypeStruct((kv.shape[0], 256 * count), kind) for kv, kind in zip(kvs, kinds)]
    return pl.pallas_call(
        functools.partial(backward_kernel, parts, count, rows),
        grid=(1,),
        in_specs=in_specs,
        out_specs=[pl.BlockSpec(out.shape, lambda i: (0, 0)) for out in outs],
        out_shape=outs,
        scratch_shapes=[
            pltpu.VMEM((2 * count, tokens, 128), BF16),
            pltpu.VMEM((2 * count, tokens, 128), BF16),
            pltpu.VMEM((2 * count, 128, tokens), F32),
        ],
        compiler_params=pltpu.CompilerParams(vmem_limit_bytes=(12 + 4 * length // 1024) * MIB),
        name="attention_backward",
        cost_estimate=pl.CostEstimate(
            flops=10 * tokens * length * 128 * count, bytes_accessed=12 * tokens * 128 * count,
            transcendentals=tokens * length * 2 * count,
        ),
    )(q, gm, qfb, gmf, *kvs, *kvs, kf)


def middle_kernel(pieces, rows, *refs):
    dy_refs = refs[:pieces]
    x_ref, mix_ref, small, w_out, w_up, w_down = refs[pieces : pieces + 6]
    outs = refs[pieces + 6 :]
    gain, shift = small[LN2_GAIN], small[LN2_SHIFT]
    out_refs = outs[:pieces]
    (mixed_ref, two_ref, active_ref, gh_ref, ga_ref, gmid_ref, gm_ref, gmf_ref, vec_ref, dy_ref) = outs[pieces:]
    band = dy_refs[0].shape[0]
    tokens, width = mix_ref.shape
    ff = w_up.shape[1]
    vec_ref[...] = jnp.zeros_like(vec_ref)
    c0 = 0.7978845608028654
    c1 = 0.044715
    row = lax.broadcasted_iota(jnp.int32, (width, width), 0) // 64
    column = lane_index((width, width)) // 64
    opposite = (row == (column + 1 - 2 * (column % 2))).astype(F32).astype(BF16)
    per = rows // band
    for t in range(tokens // rows):
        at = slice(t * rows, (t + 1) * rows)
        x = x_ref[at, :].astype(F32)
        dy = jnp.concatenate([dy_refs[t * per + j][...] for j in range(per)], axis=0)
        dy_ref[at, :] = dy
        mix = mix_ref[at, :]
        mixed = mix.astype(BF16)
        mixed_ref[at, :] = mixed
        middle = x + (dot_nn(mixed, w_out[...]) + small[BIAS_OUT])
        unit, scale = norm_parts(middle)
        two = (unit * gain + shift).astype(BF16)
        two_ref[at, :] = two
        out = middle + small[BIAS_DOWN]
        grad_two = jnp.zeros((rows, width), F32)
        step = 2 * width
        before = None
        for f in range(0, ff + step, step):
            if f < ff:
                fs = slice(f, f + step)
                bias = jnp.concatenate(
                    [small[BIAS_UP + i : BIAS_UP + i + 1] for i in range(f // width, (f + step) // width)], axis=1
                )
                now = (fs, dot_nn(two, w_up[:, fs]) + bias, dot_nt(dy, w_down[fs, :]))
            if before is not None:
                fs, hidden, grad = before
                square = hidden * hidden
                tanh = jnp.tanh(c0 * hidden * (1.0 + c1 * square))
                half = 0.5 * (1.0 + tanh)
                active = (hidden * half).astype(BF16)
                active_ref[at, fs] = active
                out = out + dot_nn(active, w_down[fs, :])
                slope = half + hidden * (0.5 * (1.0 - tanh * tanh)) * (c0 + (3.0 * c0 * c1) * square)
                grad_low = (grad * slope).astype(BF16)
                gh_ref[at, fs] = grad_low
                vec_ref[0:1, fs] += jnp.sum(grad_low.astype(F32), axis=0, keepdims=True)
                grad_two = grad_two + dot_nt(grad_low, w_up[:, fs])
            before = now
        for j in range(per):
            out_refs[t * per + j][...] = out[j * band : (j + 1) * band].astype(BF16)
        dy_wide = dy.astype(F32)
        grad_middle = dy_wide + norm_back(grad_two, unit, scale, gain)
        gmid_ref[at, :] = grad_middle
        vec_ref[1:2, :width] += jnp.sum(grad_two * unit, axis=0, keepdims=True)
        vec_ref[2:3, :width] += jnp.sum(grad_two, axis=0, keepdims=True)
        vec_ref[3:4, :width] += jnp.sum(dy_wide, axis=0, keepdims=True)
        grad_attn = grad_middle.astype(BF16)
        ga_ref[at, :] = grad_attn
        vec_ref[4:5, :width] += jnp.sum(grad_attn.astype(F32), axis=0, keepdims=True)
        gm = dot_nt(grad_attn, w_out[...]).astype(BF16)
        gm_ref[at, :] = gm
        high, mid, _ = split_three(gm.astype(F32) * mix)
        inner = dot_nn(high, opposite) + dot_nn(mid, opposite)
        gmf_ref[at, :] = three_lanes(-inner, lane_index((rows, width))).astype(BF16)


def middle_part(dys, x, mix, small, w_out, w_up, w_down, rows=512):
    tokens, width = mix.shape
    ff = w_up.shape[1]
    shape = jax.ShapeDtypeStruct
    return pl.pallas_call(
        functools.partial(middle_kernel, len(dys), rows),
        out_shape=[shape(dy.shape, BF16) for dy in dys]
        + [
            shape((tokens, width), BF16),
            shape((tokens, width), BF16),
            shape((tokens, ff), BF16),
            shape((tokens, ff), BF16),
            shape((tokens, width), BF16),
            shape((tokens, width), F32),
            shape((tokens, width), BF16),
            shape((tokens, width), BF16),
            shape((8, ff), F32),
            shape((tokens, width), BF16),
        ],
        compiler_params=pltpu.CompilerParams(vmem_limit_bytes=24 * MIB),
        name="middle_part",
        cost_estimate=pl.CostEstimate(
            flops=2 * tokens * width * (4 * ff + 5 * width), bytes_accessed=8 * 1024 * 1024,
            transcendentals=tokens * ff,
        ),
    )(*dys, x, mix, small, w_out, w_up, w_down)


def columns_by_way(mode, columns):
    middle = columns // 256 * 128
    return {
        "x": ((0, columns, 0),),
        "y": ((0, columns, 1),),
        "xy": ((0, middle, 0), (middle, columns, 1)),
    }[mode]


def place_pieces(marks, mode, total, keep_ref, send_ref):
    piece = total.shape[0] // PIECES
    for which, target in enumerate((keep_ref, send_ref)):
        for start, stop, way in columns_by_way(mode, total.shape[1]):

            def move(j, carry, which=which, target=target, start=start, stop=stop, way=way):
                source = pl.ds(pl.multiple_of((marks[2 * which + way] ^ j) * piece, piece), piece)
                spot = pl.ds(pl.multiple_of(j * piece, piece), piece)
                target[spot, start:stop] = total[source, start:stop].astype(BF16)
                return carry

            lax.fori_loop(0, PIECES // 2, move, 0)


def smem():
    return pl.BlockSpec(memory_space=pltpu.SMEM)


def vmem():
    return pl.BlockSpec(memory_space=pltpu.VMEM)


def weight_grad_kernel(count, mode, marks, *refs):
    pairs = refs[: 2 * count]
    keep_ref, send_ref, total = refs[2 * count :]
    start = 0
    for left, right in zip(pairs[0::2], pairs[1::2]):
        stop = start + right.shape[1]
        for r in range(0, left.shape[1], 256):
            total[r : r + 256, start:stop] = dot_tn(left[:, r : r + 256], right[...])
        start = stop
    place_pieces(marks, mode, total, keep_ref, send_ref)


def weight_grad(marks, mode, pairs, name):
    rows = pairs[0][0].shape[1]
    columns = sum(right.shape[1] for _, right in pairs)
    depth = pairs[0][0].shape[0]
    half = jax.ShapeDtypeStruct((rows // 2, columns), BF16)
    flat = [array for pair in pairs for array in pair]
    return pl.pallas_call(
        functools.partial(weight_grad_kernel, len(pairs), mode),
        in_specs=[smem()] + [vmem()] * len(flat),
        out_specs=[vmem(), vmem()],
        out_shape=[half, half],
        scratch_shapes=[pltpu.VMEM((rows, columns), F32)],
        compiler_params=pltpu.CompilerParams(vmem_limit_bytes=16 * MIB),
        name=name,
        cost_estimate=pl.CostEstimate(
            flops=2 * rows * columns * depth, bytes_accessed=6 * rows * columns, transcendentals=0
        ),
    )(marks, *flat)


def qkv_grad_kernel(count, mode, *refs):
    marks, normed, small, w_ref, vec_ref = refs[:5]
    dqs, owns, gots = (refs[5 + i * count : 5 + (i + 1) * count] for i in range(3))
    packed, keep_ref, send_ref, total = refs[5 + 3 * count :]
    width = normed.shape[1]
    share = width // count
    for t in range(count):
        packed[:, share * t : share * (t + 1)] = dqs[t][...]
        both = (owns[t][...] + gots[t][...].astype(F32)).astype(BF16)
        for i in range(2 * share // 128):
            at = (i % 2 + 1) * width + share * t + 128 * (i // 2)
            packed[:, at : at + 128] = both[:, 128 * i : 128 * (i + 1)]
    for r in range(0, width, 256):
        total[r : r + 256, : 3 * width] = dot_tn(normed[:, r : r + 256], packed[...])
    sums = jnp.sum(packed[...].astype(F32), axis=0, keepdims=True)
    terms = jnp.concatenate(split_three(jnp.broadcast_to(sums, (16, 3 * width))), axis=0)
    spread = dot_nt(terms, w_ref[...])
    shift_row = spread[0:1] + (spread[16:17] + spread[32:33])
    rows = jnp.zeros((width, 128), F32)
    for at in range(0, 3 * width, 128):
        rows = rows + total[:, at : at + 128] * w_ref[:, at : at + 128].astype(F32)
    gain_row = jnp.sum(rows.T, axis=0, keepdims=True)
    gain_row = (gain_row - small[LN1_SHIFT] * shift_row) / small[LN1_GAIN]
    vectors = [vec_ref[0:1, :]] + [vec_ref[i : i + 1, :width] for i in range(1, 5)]
    vectors += [sums[:, :width], sums[:, 2 * width :], gain_row, shift_row]
    tiles = [row[:, at : at + VECTOR_LANES] for row in vectors for at in range(0, row.shape[1], VECTOR_LANES)]
    piece = width // PIECES
    per = len(tiles) // PIECES
    total[:, 3 * width :] = jnp.zeros((width, VECTOR_LANES), F32)
    for i, tile in enumerate(tiles):
        at = (i // per) * piece + i % per
        total[at : at + 1, 3 * width :] = tile
    place_pieces(marks, mode, total, keep_ref, send_ref)


def qkv_grad(marks, mode, normed, small, w_qkv, vec, dqs, owns, gots):
    tokens, width = normed.shape
    columns = 3 * width + VECTOR_LANES
    half = jax.ShapeDtypeStruct((width // 2, columns), BF16)
    flat = [normed, small, w_qkv, vec, *dqs, *owns, *gots]
    return pl.pallas_call(
        functools.partial(qkv_grad_kernel, len(dqs), mode),
        in_specs=[smem()] + [vmem()] * len(flat),
        out_specs=[vmem()] * 3,
        out_shape=[jax.ShapeDtypeStruct((tokens, 3 * width), BF16), half, half],
        scratch_shapes=[pltpu.VMEM((width, columns), F32)],
        compiler_params=pltpu.CompilerParams(vmem_limit_bytes=16 * MIB),
        name="qkv_grad",
        cost_estimate=pl.CostEstimate(
            flops=6 * tokens * width * width, bytes_accessed=18 * tokens * width, transcendentals=0
        ),
    )(marks, *flat)


def last_kernel(pieces, packed, gmid_ref, small, w_ref, x_ref, *out_refs):
    band = out_refs[0].shape[0]
    grad = dot_nt(packed[...], w_ref[...])
    unit, scale = norm_parts(x_ref[...].astype(F32))
    result = (gmid_ref[...] + norm_back(grad, unit, scale, small[LN1_GAIN])).astype(BF16)
    for j in range(pieces):
        out_refs[j][...] = result[j * band : (j + 1) * band]


def last_part(packed, gmid, small, w_qkv, x, pieces):
    tokens, width = gmid.shape
    return pl.pallas_call(
        functools.partial(last_kernel, pieces),
        out_shape=[jax.ShapeDtypeStruct((tokens // pieces, width), BF16)] * pieces,
        compiler_params=pltpu.CompilerParams(vmem_limit_bytes=12 * MIB),
        name="last_part",
        cost_estimate=pl.CostEstimate(
            flops=6 * tokens * width * width, bytes_accessed=10 * tokens * width, transcendentals=0
        ),
    )(packed, gmid, small, w_qkv, x)


def assemble_kernel(segments, mode, per, marks, *refs):
    own_far, out_refs = refs[:2], refs[2:]
    half = PIECES // 2
    piece = own_far[0].shape[0] // half
    step = pl.program_id(0)

    def one(i, carry):
        index = step * per + i

        def fill(which):
            source = own_far[which]
            for low, high, way in columns_by_way(mode, source.shape[1]):
                at = pl.ds(pl.multiple_of(((index ^ marks[2 * which + way]) % half) * piece, piece), piece)
                for start, stop, which_out, tall, offset in segments:
                    first, last = max(start, low), min(stop, high)
                    if first < last:
                        spot = pl.ds(pl.multiple_of(i * tall + offset, piece), piece)
                        out_refs[which_out][spot, first - start : last - start] = source[at, first:last].astype(F32)

        mine = index // half == marks[0] // half
        pl.when(mine)(functools.partial(fill, 0))
        pl.when(jnp.logical_not(mine))(functools.partial(fill, 1))
        return carry

    lax.fori_loop(0, per, one, 0)


def assemble(marks, mode, parts, segments, shapes, name):
    steps = 2
    per = PIECES // steps
    size = sum(rows * columns for rows, columns in shapes)
    return pl.pallas_call(
        functools.partial(assemble_kernel, segments, mode, per),
        grid=(steps,),
        in_specs=[smem()] + [vmem()] * 2,
        out_specs=[pl.BlockSpec((rows // steps, w), lambda i: (i, 0)) for rows, w in shapes],
        out_shape=[jax.ShapeDtypeStruct(shape, F32) for shape in shapes],
        compiler_params=pltpu.CompilerParams(vmem_limit_bytes=16 * MIB),
        name=name,
        cost_estimate=pl.CostEstimate(flops=size, bytes_accessed=6 * size, transcendentals=0),
    )(marks, *parts)


def return_kernel(halves, row_ref, *refs):
    out, sems = refs[-2], refs[-1]
    copies = []
    for i, (ref, (j, half)) in enumerate(zip(refs, halves)):
        width = ref.shape[1]
        at = 0 if half is None else half * width
        copies.append(pltpu.make_async_copy(ref, out.at[row_ref[0] ^ j, :, at : at + width], sems.at[i]))
    for copy in copies:
        copy.start()
    for copy in copies:
        copy.wait()


def return_rows(row, own, halves, name):
    flat = [own] + [piece for half in halves for piece in half]
    places = [(0, None)] + [(j + 1, h) for h, half in enumerate(halves) for j in range(len(half))]
    pieces = len(halves[0]) + 1
    return pl.pallas_call(
        functools.partial(return_kernel, places),
        in_specs=[smem()] + [vmem()] * len(flat),
        out_specs=pl.BlockSpec(memory_space=pl.ANY),
        out_shape=jax.ShapeDtypeStruct((pieces, *own.shape), BF16),
        scratch_shapes=[pltpu.SemaphoreType.DMA((len(flat),))],
        compiler_params=pltpu.CompilerParams(vmem_limit_bytes=4 * MIB),
        name=name,
    )(row, *flat)


def swap(value, axis, size, mask):
    return lax.ppermute(value, axis, [(i, i ^ mask) for i in range(size)])


class Order:
    def __init__(self):
        self.last = ()

    def enter(self, *values):
        return lax.optimization_barrier((values, self.last))[0]

    def leave(self, *values):
        self.last = values


class Cargo:
    def __init__(self, pieces):
        self.pieces = pieces
        width = pieces[0].shape[1] // 2
        self.columns = [slice(0, width), slice(width, 2 * width)]
        self.came = [[None] * len(pieces) for _ in range(2)]
        self.onward = [None, None]

    def load(self, half, way, first):
        columns = self.columns[half]
        far = self.pieces[3][:, columns] if first else self.onward[half]
        return jnp.concatenate([self.pieces[way + 1][:, columns], far], axis=0)

    def land(self, half, way, first, got):
        band = got.shape[0] // 2
        self.came[half][way + 1] = got[:band]
        if first:
            self.onward[half] = got[band:]
        else:
            self.came[half][3] = got[band:]


def fold(value, rows):
    if rows < value.shape[0]:
        return jnp.concatenate([value[at : at + rows] for at in range(0, value.shape[0], rows)], axis=1)
    wide = value.shape[1] * value.shape[0] // rows
    return jnp.concatenate([value[:, at : at + wide] for at in range(0, value.shape[1], wide)], axis=0)


class Wave:
    def __init__(self, order, keep, send, marks, mode, layout, core, ways, deep, rest):
        self.order, self.core, self.ways, self.deep, self.rest = order, core, ways, deep, rest
        self.marks, self.mode, self.layout = marks, mode, layout
        self.parts = columns_by_way(mode, keep.shape[1])
        self.value, self.got = [keep], [core(send)]
        self.cargo, self.aboard = {}, None
        order.leave(send)

    def arrived(self):
        count = len(self.value)
        values = self.order.enter(*self.value, *self.got)
        kept, came = values[:count], list(values[count:])
        if self.aboard is not None:
            cargo, first, ways, shape = self.aboard
            for i, way in enumerate(ways):
                own = self.parts[i][1] - self.parts[i][0]
                cargo.land(i, way, first, fold(came[i][:, own:], shape[0]))
                came[i] = came[i][:, :own]
            self.aboard = None
        return list(zip(kept, came))

    def added(self):
        return [add_low(one, two) for one, two in self.arrived()]

    def split(self, value):
        return [value[:, start:stop] for start, stop, _ in self.parts]

    def travel(self, step, values, key):
        ways = [(step + way) % 2 for _, _, way in self.parts]
        if key in self.cargo:
            cargo, first = self.cargo[key]
            loads = [cargo.load(i, way, first) for i, way in enumerate(ways)]
            self.aboard = (cargo, first, ways, loads[0].shape)
            values = [
                jnp.concatenate([value, fold(load, value.shape[0])], axis=1) for value, load in zip(values, loads)
            ]
        self.got = [self.ways[way](value) for way, value in zip(ways, values)]
        self.order.leave(*values)

    def plane(self, step):
        values = self.added()
        if step == 0:
            values = self.split(values[0])
        half = values[0].shape[0] // 2
        self.value = [value[:half] for value in values]
        self.travel(step, [value[half:] for value in values], ("out", step))

    def line(self):
        values = self.added()
        half = values[0].shape[0] // 2
        self.value = [jnp.concatenate([value[:half] for value in values], axis=1)]
        sent = jnp.concatenate([value[half:] for value in values], axis=1)
        self.got = [self.deep(sent)]
        self.order.leave(sent)

    def exchanges(self):
        for send in self.rest:
            self.value = self.added()
            self.got = [send(self.value[0])]
            self.order.leave(*self.value)

    def line_back(self):
        self.value = self.added()
        self.got = [self.deep(self.value[0])]
        self.order.leave(*self.value)

    def joined(self):
        return [jnp.concatenate(pair, axis=0) for pair in self.arrived()]

    def plane_back(self, step):
        values = self.joined()
        self.value = self.split(values[0]) if step == 1 else values
        self.travel(step, self.value, ("back", step))

    def core_back(self):
        self.value = [jnp.concatenate(self.joined(), axis=1)]
        self.got = [self.core(self.value[0])]
        self.order.leave(*self.value)

    def wait(self):
        self.got = list(self.order.enter(*self.got))
        self.order.leave(*self.got)

    def finish(self):
        ((own, far),) = self.arrived()
        self.sums = assemble(self.marks, self.mode, (own, far), *self.layout)
        self.order.leave(*self.sums)

    def steps(self):
        yield functools.partial(self.plane, 0)
        yield functools.partial(self.plane, 1)
        yield self.line
        yield self.exchanges
        yield self.line_back
        yield functools.partial(self.plane_back, 1)
        yield functools.partial(self.plane_back, 0)
        yield self.core_back
        yield self.finish


def add_low(one, two):
    return (one.astype(F32) + two.astype(F32)).astype(BF16)


def after(value, *others):
    return lax.optimization_barrier((value, others))[0]


def bits_of(axis, size):
    found, mask = [], 1
    while mask < size:
        found.append((axis, size, mask, (lax.axis_index(axis) // mask) % 2))
        mask *= 2
    return found


def per_device(
    seq_size, row_size,
    block_input, segment_ids, ln1_gain, ln1_shift, w_qkv, bias_query, bias_value, w_out, bias_out,
    ln2_gain, ln2_shift, w_up, bias_up, w_down, bias_down, out_grad,
):
    rows, band, width = block_input.shape
    length = segment_ids.shape[1]
    share = seq_size // rows
    tokens = rows * band
    crops = max(length // (4 * band), 1)
    place = lax.axis_index("seq")
    my_row, my_part = place // share, place % share

    def deal(pieces):
        got = [pieces[0]]
        for j in range(1, rows):
            turn = [(s, ((s // share) ^ j) * share + s % share) for s in range(seq_size)]
            got.append(lax.ppermute(pieces[j], "seq", turn))
        return got

    def pick(array):
        return [lax.dynamic_index_in_dim(array, my_row ^ j, 0, False) for j in range(rows)]

    xs = deal(pick(block_input))
    dys = pick(out_grad)

    own_row = lax.dynamic_index_in_dim(segment_ids, my_row, 0, False).reshape(seq_size, band)
    key_ids = jnp.concatenate(
        [
            lax.dynamic_index_in_dim(own_row, (my_row ^ j) * share + (my_part ^ i), 0, False)
            for i in range(share)
            for j in range(rows)
        ]
    )
    spot = jnp.arange(128) % 64
    same = key_ids[:, None] == spot[None, :]
    used = spot[None, :] < crops
    ones = (spot >= LSE_LANE) & (spot < LSE_LANE + 3)
    kf = jnp.where(used, jnp.where(same, 0.0, -1.0), jnp.where(ones, 1.0, 0.0)).astype(BF16)
    qf = jnp.where(used & same, BIG, 0.0).astype(BF16)[:tokens]

    small = jnp.stack(
        [ln1_gain, ln1_shift, bias_query, bias_value, bias_out, ln2_gain, ln2_shift, bias_down]
    )
    small = jnp.concatenate([small, bias_up.reshape(-1, width)], axis=0)
    shape = jax.ShapeDtypeStruct
    x, normed, q, kv = pl.pallas_call(
        functools.partial(qkv_kernel, rows, width),
        out_shape=[
            shape((tokens, width), BF16),
            shape((tokens, width), BF16),
            shape((tokens, width), BF16),
            shape((tokens, 2 * width), BF16),
        ],
        compiler_params=pltpu.CompilerParams(vmem_limit_bytes=12 * MIB),
        name="norm_and_project",
    )(*xs, small, w_qkv)


    dys = list(lax.optimization_barrier((dys, kv))[0])
    dys = deal(dys)
    seq_bits = bits_of("seq", seq_size)
    row_bits = bits_of("row", row_size)
    part_bits = [bit for bit in seq_bits if bit[2] < share]
    kvs, whole = [kv], kv
    for axis, size, mask, own in part_bits:
        got = swap(whole, axis, size, mask)
        kvs.append(got)
        if mask * 2 < share:
            whole = jnp.concatenate([whole, got], 0)

    mix, qfb = attention_forward(q, kvs, qf, kf)
    *outs, mixed, two, active, grad_hidden, grad_attn, grad_middle, gm, gmf, vec, dy = middle_part(
        dys, x, mix, small, w_out, w_up, w_down
    )

    def straight(bit):
        return lambda value: swap(value, *bit[:3])

    plane = [bit for bit in seq_bits if bit[2] >= share]
    core, one, two_, deep = seq_bits[0][3], plane[0][3], plane[1][3], row_bits[0][3]
    ways = (straight(plane[0]), straight(plane[1]))
    rest = [straight(bit) for bit in row_bits[1:] + plane[2:] + part_bits[1:]]
    route = (straight(seq_bits[0]), ways, straight(row_bits[0]), rest)
    left, right = one * 4 + two_ * 2 + deep, two_ * 4 + one * 2 + deep
    mine, other = core * 8, 8 - core * 8
    marks = jnp.stack([mine + left, mine + right, other + left, other + right]).astype(jnp.int32)

    pairs = width // 128
    ff = w_up.shape[1]
    tall = width // PIECES
    down_layout = ([(0, width, 0, ff // PIECES, 0)], [(ff, width)], "assemble_down")
    up_segments = [(0, ff, 0, tall, 0), (ff, ff + width, 1, tall, 0)]
    up_layout = (up_segments, [(width, ff), (width, width)], "assemble_up_out")
    qkv_segments = [(0, 3 * width, 0, tall, 0), (3 * width, 3 * width + VECTOR_LANES, 1, tall, 0)]
    qkv_layout = (qkv_segments, [(width, 3 * width), (width, VECTOR_LANES)], "assemble_qkv")
    row = my_row.astype(jnp.int32).reshape(1)

    order = Order()
    terms, gots, steps, done = [], [], {}, {}

    def backward():
        (grad,) = order.enter(gm)
        terms.append(attention_backward(q, grad, qfb, gmf, kvs, kf, AT_ONCE * len(terms), AT_ONCE))
        order.leave(*terms[-1])
        if share == 2:
            gots.append(straight(part_bits[0])(terms[-1][2]))

    def start_wave(letter, pairs_of, name, layout):
        flat = order.enter(*[array for pair in pairs_of for array in pair])
        keep, send = weight_grad(marks, MODES[letter], list(zip(flat[0::2], flat[1::2])), name)
        done[letter] = Wave(order, keep, send, marks, MODES[letter], layout, *route)
        steps[letter] = done[letter].steps()
        if letter == "d":
            ride("d", outs, "out", "o")

    def start_qkv():
        own_terms, far_terms = [term[1] for term in terms], gots
        if share != 2:
            both = jnp.concatenate(
                [jnp.concatenate([part.astype(BF16) for part in term[1:]], 0) for term in terms], axis=1
            )
            for bit in reversed(part_bits):
                half = both.shape[0] // 2
                kept, got = both[:half], straight(bit)(both[half:])
                both = add_low(kept, got)
            cuts = [slice(256 * AT_ONCE * t, 256 * AT_ONCE * (t + 1)) for t in range(len(terms))]
            own_terms = [kept[:, cut].astype(F32) for cut in cuts]
            far_terms = [got[:, cut] for cut in cuts]
        (vec_,) = order.enter(vec)
        dqs = [term[0] for term in terms]
        done["p"], keep, send = qkv_grad(marks, MODES["q"], normed, small, w_qkv, vec_, dqs, own_terms, far_terms)
        done["q"] = Wave(order, keep, send, marks, MODES["q"], qkv_layout, *route)
        steps["q"] = done["q"].steps()

    def last():
        (packed,) = order.enter(done["p"])
        pieces = last_part(packed, grad_middle, small, w_qkv, x, rows)
        order.leave(*pieces)
        ride("u", pieces, "back", "i")

    def ride(letter, pieces, stage, name):
        done[name] = Cargo(pieces)
        steps_ = (0, 1) if stage == "out" else (1, 0)
        for i, step in enumerate(steps_):
            done[letter].cargo[(stage, step)] = (done[name], i == 0)

    def take_back(name):
        cargo = done[name]
        halves = [list(order.enter(*half[1:])) for half in cargo.came]
        done[name] = return_rows(row, cargo.pieces[0], halves, "return_rows")
        order.leave(done[name])

    actions = {
        "b": backward,
        "D": lambda: start_wave("d", [(active, dy)], "grad_down", down_layout),
        "U": lambda: start_wave("u", [(two, grad_hidden), (mixed, grad_attn)], "grad_up_out", up_layout),
        "G": start_qkv,
        "L": last,
        "O": lambda: take_back("o"),
        "I": lambda: take_back("i"),
        "d": lambda: next(steps["d"])(),
        "u": lambda: next(steps["u"])(),
        "q": lambda: next(steps["q"])(),
    }
    def wait(which):
        if which.isdigit():
            if share == 2:
                (gots[int(which)],) = order.enter(gots[int(which)])
                order.leave(gots[int(which)])
        else:
            done[which].wait()

    for word in SCHEDULE:
        if word[0] == "w":
            wait(word[1])
        else:
            actions[word]()
    result, input_grad = done["o"], done["i"]
    (sum_down,) = done["d"].sums
    sum_up, sum_out = done["u"].sums
    sum_qkv, tiles = done["q"].sums

    count = (ff + 8 * width) // VECTOR_LANES // PIECES
    vectors = tiles.reshape(PIECES, -1, VECTOR_LANES)[:, :count].reshape(-1)
    cuts = [ff + i * width for i in range(9)]
    names = [vectors[a:b] for a, b in zip(cuts[:-1], cuts[1:])]
    ln2_gain_sum, ln2_shift_sum, bias_down_sum, bias_out_sum = names[:4]
    bias_q_sum, bias_v_sum, ln1_gain_sum, ln1_shift_sum = names[4:]
    return (
        result,
        input_grad,
        ln1_gain_sum,
        ln1_shift_sum,
        sum_qkv,
        bias_q_sum,
        bias_v_sum,
        sum_out,
        bias_out_sum,
        ln2_gain_sum,
        ln2_shift_sum,
        sum_up,
        vectors[:ff],
        sum_down,
        bias_down_sum,
    )


def solution(mesh):
    split = P("row", "seq", None)
    placed = (split, P("row", None)) + (P(),) * 13 + (split,)
    return jax.shard_map(
        functools.partial(per_device, mesh.shape["seq"], mesh.shape["row"]),
        mesh=mesh,
        in_specs=placed,
        out_specs=(split, split) + (P(),) * 13,
        check_vma=False,
    )
```

```python
import functools

import jax
import jax.numpy as jnp
from jax import lax
from jax.experimental import pallas as pl
from jax.experimental.pallas import tpu as pltpu
from jax.sharding import PartitionSpec as P

HEADS = 8
EPSILON = 1e-06
BIG = 1e30
LSE_LANE = 16
PIECES = 16
AT_ONCE = 2
SCHEDULE = (
    "U", "D", "u", "b", "u", "b", "u", "d", "G", "u", "q", "d", "L", "u", "q", "d",
    "u", "q", "d", "q", "u", "d", "q", "O", "d", "u", "q", "d", "I", "q", "u", "d",
    "q", "d", "q",
)
MODES = {"d": "xy", "u": "xy", "q": "xy"}
VECTOR_LANES = 128
F32 = jnp.float32
BF16 = jnp.bfloat16
MIB = 1024 * 1024
LN1_GAIN, LN1_SHIFT, BIAS_Q, BIAS_V, BIAS_OUT, LN2_GAIN, LN2_SHIFT, BIAS_DOWN = (
    slice(i, i + 1) for i in range(8)
)
BIAS_UP = 8


def dot_nn(a, b):
    return lax.dot_general(a, b, (((1,), (0,)), ((), ())), preferred_element_type=F32)


def dot_nt(a, b):
    return lax.dot_general(a, b, (((1,), (1,)), ((), ())), preferred_element_type=F32)


def dot_tn(a, b):
    return lax.dot_general(a, b, (((0,), (0,)), ((), ())), preferred_element_type=F32)


def split_three(value):
    high = value.astype(BF16)
    rest = value - high.astype(F32)
    middle = rest.astype(BF16)
    low = (rest - middle.astype(F32)).astype(BF16)
    return high, middle, low


def lane_index(shape):
    return lax.broadcasted_iota(jnp.int32, shape, len(shape) - 1)


def three_lanes(value, lanes):
    high, middle, low = split_three(value)
    spot = lanes % 64
    out = jnp.where(spot == LSE_LANE, high.astype(F32), 0.0)
    out = jnp.where(spot == LSE_LANE + 1, middle.astype(F32), out)
    return jnp.where(spot == LSE_LANE + 2, low.astype(F32), out)


def norm_parts(value):
    centre = jnp.mean(value, axis=-1, keepdims=True)
    centred = value - centre
    spread = jnp.mean(centred * centred, axis=-1, keepdims=True)
    scale = lax.rsqrt(spread + EPSILON)
    return centred * scale, scale


def norm_back(grad, unit, scale, gain):
    grad_unit = grad * gain
    first = jnp.mean(grad_unit, axis=-1, keepdims=True)
    second = jnp.mean(grad_unit * unit, axis=-1, keepdims=True)
    return scale * (grad_unit - first - unit * second)


def fetch_kernel(source, target, sem):
    copy = pltpu.make_async_copy(source, target, sem)
    copy.start()
    copy.wait()


def fetch(array):
    return pl.pallas_call(
        fetch_kernel,
        in_specs=[pl.BlockSpec(memory_space=pl.ANY)],
        out_specs=vmem(),
        out_shape=jax.ShapeDtypeStruct(array.shape, array.dtype),
        scratch_shapes=[pltpu.SemaphoreType.DMA],
        compiler_params=pltpu.CompilerParams(vmem_limit_bytes=8 * MIB),
        name="fetch",
    )(array)


def qkv_kernel(pieces, width, *refs):
    x_refs = refs[:pieces]
    small, w_ref, x_ref, normed_ref, q_ref, kv_ref = refs[pieces:]
    band = x_refs[0].shape[0]
    for j in range(pieces):
        x_ref[j * band : (j + 1) * band, :] = x_refs[j][...]
        unit, _ = norm_parts(x_refs[j][...].astype(F32))
        normed_ref[j * band : (j + 1) * band, :] = (unit * small[LN1_GAIN] + small[LN1_SHIFT]).astype(BF16)
    normed = normed_ref[...]
    q = dot_nn(normed, w_ref[:, :width])
    q_ref[...] = ((q + small[BIAS_Q]) * (width // HEADS) ** -0.5).astype(BF16)
    kv_ref[:, :width] = dot_nn(normed, w_ref[:, width : 2 * width]).astype(BF16)
    kv_ref[:, width:] = (dot_nn(normed, w_ref[:, 2 * width :]) + small[BIAS_V]).astype(BF16)


def forward_kernel(parts, wide, rows, *refs):
    q_ref = refs[0]
    k_refs = refs[1 : 1 + parts]
    v_refs = refs[1 + parts : 1 + 2 * parts]
    qf_ref, kf_ref, mix_ref, qfb_ref, k_aug, v_aug = refs[1 + 2 * parts :]
    tokens = q_ref.shape[0]
    low_half = (lane_index((1, 128)) < 64).astype(F32)
    halves = (low_half.astype(BF16), (1.0 - low_half).astype(BF16))
    for pair in range(wide):
        at = slice(128 * pair, 128 * (pair + 1))
        for parity in range(2):
            mine, other = halves[parity], halves[1 - parity]
            start = 0
            for k_ref, v_ref in zip(k_refs, v_refs):
                stop = start + k_ref.shape[0]
                k_aug[2 * pair + parity, start:stop, :] = k_ref[:, at] * mine + kf_ref[start:stop, :] * other
                v_aug[2 * pair + parity, start:stop, :] = v_ref[:, at] * mine + other
                start = stop
    lanes = lane_index((rows, 128))
    low = lanes < 64
    held = {}

    def scores_of(pair, block, parity):
        at, heads = slice(block * rows, (block + 1) * rows), slice(128 * pair, 128 * (pair + 1))
        q = q_ref[at, heads] * halves[parity] + qf_ref[at, :] * halves[1 - parity]
        return dot_nt(q, k_aug[2 * pair + parity])

    def use(pair, block, parity, scores):
        top = jnp.max(scores, axis=-1, keepdims=True)
        exps = jnp.exp(scores - top).astype(BF16)
        sums = dot_nn(exps, v_aug[2 * pair + parity])
        if parity == 0:
            held[0] = (sums, top)
            return
        (even, even_top), odd, odd_top = held[0], sums, top
        at, heads = slice(block * rows, (block + 1) * rows), slice(128 * pair, 128 * (pair + 1))
        total = jnp.where(low, odd, even)
        mix_ref[at, heads] = jnp.where(low, even, odd) / pltpu.roll(total, 64, 1)
        log_total = jnp.where(low, odd_top, even_top) + jnp.log(total)
        qfb_ref[at, heads] = (qf_ref[at, :].astype(F32) + three_lanes(-log_total, lanes)).astype(BF16)

    before = None
    for pair in range(wide):
        for block in range(tokens // rows):
            for parity in range(2):
                now = (pair, block, parity, scores_of(pair, block, parity))
                if before is not None:
                    use(*before)
                before = now
    use(*before)


def attention_forward(q, kvs, qf, kf, wide=2, rows=256):
    tokens, width = q.shape
    lanes = 128 * wide
    steps = width // lanes
    length = kf.shape[0]
    parts = len(kvs)
    in_specs = [pl.BlockSpec((tokens, lanes), lambda h: (0, h))]
    in_specs += [pl.BlockSpec((kv.shape[0], lanes), lambda h: (0, h)) for kv in kvs]
    in_specs += [pl.BlockSpec((kv.shape[0], lanes), lambda h: (0, steps + h)) for kv in kvs]
    in_specs += [
        pl.BlockSpec((tokens, 128), lambda h: (0, 0)),
        pl.BlockSpec((length, 128), lambda h: (0, 0)),
    ]
    return pl.pallas_call(
        functools.partial(forward_kernel, parts, wide, rows),
        grid=(steps,),
        in_specs=in_specs,
        out_specs=[
            pl.BlockSpec((tokens, lanes), lambda h: (0, h)),
            pl.BlockSpec((tokens, lanes), lambda h: (0, h)),
        ],
        out_shape=[
            jax.ShapeDtypeStruct((tokens, width), F32),
            jax.ShapeDtypeStruct((tokens, width), BF16),
        ],
        scratch_shapes=[pltpu.VMEM((2 * wide, length, 128), BF16), pltpu.VMEM((2 * wide, length, 128), BF16)],
        compiler_params=pltpu.CompilerParams(vmem_limit_bytes=(8 + 8 * length // 1024) * MIB),
        name="attention_forward",
        cost_estimate=pl.CostEstimate(
            flops=4 * tokens * length * width, bytes_accessed=8 * tokens * width,
            transcendentals=tokens * length * HEADS,
        ),
    )(q, *kvs, *kvs, qf, kf)


def backward_kernel(parts, count, rows, *refs):
    q_ref, gm_ref, qfb_ref, gmf_ref = refs[:4]
    k_refs = refs[4 : 4 + parts]
    v_refs = refs[4 + parts : 4 + 2 * parts]
    kf_ref = refs[4 + 2 * parts]
    rest = refs[5 + 2 * parts :]
    dq_ref = rest[0]
    pair_refs = rest[1 : 1 + parts]
    q_aug, gm_aug, dqt = rest[1 + parts :]
    low_half = (lane_index((1, 128)) < 64).astype(F32)
    halves = (low_half.astype(BF16), (1.0 - low_half).astype(BF16))
    low = lane_index((rows, 128)) < 64
    for pair in range(count):
        heads = slice(128 * pair, 128 * (pair + 1))
        for parity in range(2):
            mine, other = halves[parity], halves[1 - parity]
            q_aug[2 * pair + parity] = q_ref[:, heads] * mine + qfb_ref[:, heads] * other
            gm_aug[2 * pair + parity] = gm_ref[:, heads] * mine + gmf_ref[:, heads] * other
        start = 0
        for k_ref, v_ref, pair_ref in zip(k_refs, v_refs, pair_refs):
            for block in range(k_ref.shape[0] // rows):
                at = slice(block * rows, (block + 1) * rows)
                k, v = k_ref[at, heads], v_ref[at, heads]
                kf = kf_ref[start + block * rows : start + (block + 1) * rows, :]
                dks, dvs = [], []
                for parity in range(2):
                    mine, other = halves[parity], halves[1 - parity]
                    probs = jnp.exp(dot_nt(k * mine + kf * other, q_aug[2 * pair + parity]))
                    slopes = dot_nt(v * mine + other, gm_aug[2 * pair + parity])
                    grads = (probs * slopes).astype(BF16)
                    dvs.append(dot_nn(probs.astype(BF16), gm_ref[:, heads]))
                    dks.append(dot_nn(grads, q_ref[:, heads]))
                    term = dot_tn(k, grads)
                    if start + block == 0:
                        dqt[2 * pair + parity] = term
                    else:
                        dqt[2 * pair + parity] += term
                left, right = 256 * pair, 256 * pair + 128
                pair_ref[at, left:right] = jnp.where(low, dks[0], dks[1]).astype(pair_ref.dtype)
                pair_ref[at, right : right + 128] = jnp.where(low, dvs[0], dvs[1]).astype(pair_ref.dtype)
            start += k_ref.shape[0]
        dq_t = jnp.concatenate([dqt[2 * pair, :64, :], dqt[2 * pair + 1, 64:, :]], axis=0)
        dq_ref[:, heads] = dq_t.T.astype(BF16) * (64.0**-0.5)


def attention_backward(q, gm, qfb, gmf, kvs, kf, first, count, rows=512):
    tokens, width = q.shape
    length = kf.shape[0]
    parts = len(kvs)
    lanes = 128 * count
    steps = width // lanes
    own = lambda i: (0, first // count)
    in_specs = [pl.BlockSpec((tokens, lanes), own)] * 4
    in_specs += [pl.BlockSpec((kv.shape[0], lanes), own) for kv in kvs]
    in_specs += [pl.BlockSpec((kv.shape[0], lanes), lambda i: (0, steps + first // count)) for kv in kvs]
    in_specs += [pl.BlockSpec((length, 128), lambda i: (0, 0))]
    kinds = [F32] + [BF16] * (parts - 1)
    outs = [jax.ShapeDtypeStruct((tokens, 128 * count), BF16)]
    outs += [jax.ShapeDtypeStruct((kv.shape[0], 256 * count), kind) for kv, kind in zip(kvs, kinds)]
    return pl.pallas_call(
        functools.partial(backward_kernel, parts, count, rows),
        grid=(1,),
        in_specs=in_specs,
        out_specs=[pl.BlockSpec(out.shape, lambda i: (0, 0)) for out in outs],
        out_shape=outs,
        scratch_shapes=[
            pltpu.VMEM((2 * count, tokens, 128), BF16),
            pltpu.VMEM((2 * count, tokens, 128), BF16),
            pltpu.VMEM((2 * count, 128, tokens), F32),
        ],
        compiler_params=pltpu.CompilerParams(vmem_limit_bytes=(12 + 4 * length // 1024) * MIB),
        name="attention_backward",
        cost_estimate=pl.CostEstimate(
            flops=10 * tokens * length * 128 * count, bytes_accessed=12 * tokens * 128 * count,
            transcendentals=tokens * length * 2 * count,
        ),
    )(q, gm, qfb, gmf, *kvs, *kvs, kf)


def middle_kernel(pieces, rows, *refs):
    dy_refs = refs[:pieces]
    x_ref, mix_ref, small, w_out, w_up, w_down = refs[pieces : pieces + 6]
    outs = refs[pieces + 6 :]
    gain, shift = small[LN2_GAIN], small[LN2_SHIFT]
    out_refs = outs[:pieces]
    (mixed_ref, two_ref, active_ref, gh_ref, ga_ref, gmid_ref, gm_ref, gmf_ref, vec_ref, dy_ref) = outs[pieces:]
    band = dy_refs[0].shape[0]
    tokens, width = mix_ref.shape
    ff = w_up.shape[1]
    vec_ref[...] = jnp.zeros_like(vec_ref)
    c0 = 0.7978845608028654
    c1 = 0.044715
    row = lax.broadcasted_iota(jnp.int32, (width, width), 0) // 64
    column = lane_index((width, width)) // 64
    opposite = (row == (column + 1 - 2 * (column % 2))).astype(F32).astype(BF16)
    per = rows // band
    for t in range(tokens // rows):
        at = slice(t * rows, (t + 1) * rows)
        x = x_ref[at, :].astype(F32)
        dy = jnp.concatenate([dy_refs[t * per + j][...] for j in range(per)], axis=0)
        dy_ref[at, :] = dy
        mix = mix_ref[at, :]
        mixed = mix.astype(BF16)
        mixed_ref[at, :] = mixed
        middle = x + (dot_nn(mixed, w_out[...]) + small[BIAS_OUT])
        unit, scale = norm_parts(middle)
        two = (unit * gain + shift).astype(BF16)
        two_ref[at, :] = two
        out = middle + small[BIAS_DOWN]
        grad_two = jnp.zeros((rows, width), F32)
        step = 2 * width
        before = None
        for f in range(0, ff + step, step):
            if f < ff:
                fs = slice(f, f + step)
                bias = jnp.concatenate(
                    [small[BIAS_UP + i : BIAS_UP + i + 1] for i in range(f // width, (f + step) // width)], axis=1
                )
                now = (fs, dot_nn(two, w_up[:, fs]) + bias, dot_nt(dy, w_down[fs, :]))
            if before is not None:
                fs, hidden, grad = before
                square = hidden * hidden
                tanh = jnp.tanh(c0 * hidden * (1.0 + c1 * square))
                half = 0.5 * (1.0 + tanh)
                active = (hidden * half).astype(BF16)
                active_ref[at, fs] = active
                out = out + dot_nn(active, w_down[fs, :])
                slope = half + hidden * (0.5 * (1.0 - tanh * tanh)) * (c0 + (3.0 * c0 * c1) * square)
                grad_low = (grad * slope).astype(BF16)
                gh_ref[at, fs] = grad_low
                vec_ref[0:1, fs] += jnp.sum(grad_low.astype(F32), axis=0, keepdims=True)
                grad_two = grad_two + dot_nt(grad_low, w_up[:, fs])
            before = now
        for j in range(per):
            out_refs[t * per + j][...] = out[j * band : (j + 1) * band].astype(BF16)
        dy_wide = dy.astype(F32)
        grad_middle = dy_wide + norm_back(grad_two, unit, scale, gain)
        gmid_ref[at, :] = grad_middle
        vec_ref[1:2, :width] += jnp.sum(grad_two * unit, axis=0, keepdims=True)
        vec_ref[2:3, :width] += jnp.sum(grad_two, axis=0, keepdims=True)
        vec_ref[3:4, :width] += jnp.sum(dy_wide, axis=0, keepdims=True)
        grad_attn = grad_middle.astype(BF16)
        ga_ref[at, :] = grad_attn
        vec_ref[4:5, :width] += jnp.sum(grad_attn.astype(F32), axis=0, keepdims=True)
        gm = dot_nt(grad_attn, w_out[...]).astype(BF16)
        gm_ref[at, :] = gm
        high, mid, _ = split_three(gm.astype(F32) * mix)
        inner = dot_nn(high, opposite) + dot_nn(mid, opposite)
        gmf_ref[at, :] = three_lanes(-inner, lane_index((rows, width))).astype(BF16)


def middle_part(dys, x, mix, small, w_out, w_up, w_down, rows=512):
    tokens, width = mix.shape
    ff = w_up.shape[1]
    shape = jax.ShapeDtypeStruct
    return pl.pallas_call(
        functools.partial(middle_kernel, len(dys), rows),
        out_shape=[shape(dy.shape, BF16) for dy in dys]
        + [
            shape((tokens, width), BF16),
            shape((tokens, width), BF16),
            shape((tokens, ff), BF16),
            shape((tokens, ff), BF16),
            shape((tokens, width), BF16),
            shape((tokens, width), F32),
            shape((tokens, width), BF16),
            shape((tokens, width), BF16),
            shape((8, ff), F32),
            shape((tokens, width), BF16),
        ],
        compiler_params=pltpu.CompilerParams(vmem_limit_bytes=24 * MIB),
        name="middle_part",
        cost_estimate=pl.CostEstimate(
            flops=2 * tokens * width * (4 * ff + 5 * width), bytes_accessed=8 * 1024 * 1024,
            transcendentals=tokens * ff,
        ),
    )(*dys, x, mix, small, w_out, w_up, w_down)


def columns_by_way(mode, columns):
    middle = columns // 256 * 128
    return {
        "x": ((0, columns, 0),),
        "y": ((0, columns, 1),),
        "xy": ((0, middle, 0), (middle, columns, 1)),
    }[mode]


def place_pieces(marks, mode, total, keep_ref, send_ref):
    piece = total.shape[0] // PIECES
    for which, target in enumerate((keep_ref, send_ref)):
        for start, stop, way in columns_by_way(mode, total.shape[1]):

            def move(j, carry, which=which, target=target, start=start, stop=stop, way=way):
                source = pl.ds(pl.multiple_of((marks[2 * which + way] ^ j) * piece, piece), piece)
                spot = pl.ds(pl.multiple_of(j * piece, piece), piece)
                target[spot, start:stop] = total[source, start:stop].astype(BF16)
                return carry

            lax.fori_loop(0, PIECES // 2, move, 0)


def smem():
    return pl.BlockSpec(memory_space=pltpu.SMEM)


def vmem():
    return pl.BlockSpec(memory_space=pltpu.VMEM)


def weight_grad_kernel(count, mode, marks, *refs):
    pairs = refs[: 2 * count]
    keep_ref, send_ref, total = refs[2 * count :]
    start = 0
    for left, right in zip(pairs[0::2], pairs[1::2]):
        stop = start + right.shape[1]
        for r in range(0, left.shape[1], 256):
            total[r : r + 256, start:stop] = dot_tn(left[:, r : r + 256], right[...])
        start = stop
    place_pieces(marks, mode, total, keep_ref, send_ref)


def weight_grad(marks, mode, pairs, name):
    rows = pairs[0][0].shape[1]
    columns = sum(right.shape[1] for _, right in pairs)
    depth = pairs[0][0].shape[0]
    half = jax.ShapeDtypeStruct((rows // 2, columns), BF16)
    flat = [array for pair in pairs for array in pair]
    return pl.pallas_call(
        functools.partial(weight_grad_kernel, len(pairs), mode),
        in_specs=[smem()] + [vmem()] * len(flat),
        out_specs=[vmem(), vmem()],
        out_shape=[half, half],
        scratch_shapes=[pltpu.VMEM((rows, columns), F32)],
        compiler_params=pltpu.CompilerParams(vmem_limit_bytes=16 * MIB),
        name=name,
        cost_estimate=pl.CostEstimate(
            flops=2 * rows * columns * depth, bytes_accessed=6 * rows * columns, transcendentals=0
        ),
    )(marks, *flat)


def qkv_grad_kernel(count, mode, *refs):
    marks, normed, small, w_ref, vec_ref = refs[:5]
    dqs, owns, gots = (refs[5 + i * count : 5 + (i + 1) * count] for i in range(3))
    packed, keep_ref, send_ref, total = refs[5 + 3 * count :]
    width = normed.shape[1]
    share = width // count
    for t in range(count):
        packed[:, share * t : share * (t + 1)] = dqs[t][...]
        both = (owns[t][...] + gots[t][...].astype(F32)).astype(BF16)
        for i in range(2 * share // 128):
            at = (i % 2 + 1) * width + share * t + 128 * (i // 2)
            packed[:, at : at + 128] = both[:, 128 * i : 128 * (i + 1)]
    for r in range(0, width, 256):
        total[r : r + 256, : 3 * width] = dot_tn(normed[:, r : r + 256], packed[...])
    sums = jnp.sum(packed[...].astype(F32), axis=0, keepdims=True)
    terms = jnp.concatenate(split_three(jnp.broadcast_to(sums, (16, 3 * width))), axis=0)
    spread = dot_nt(terms, w_ref[...])
    shift_row = spread[0:1] + (spread[16:17] + spread[32:33])
    rows = jnp.zeros((width, 128), F32)
    for at in range(0, 3 * width, 128):
        rows = rows + total[:, at : at + 128] * w_ref[:, at : at + 128].astype(F32)
    gain_row = jnp.sum(rows.T, axis=0, keepdims=True)
    gain_row = (gain_row - small[LN1_SHIFT] * shift_row) / small[LN1_GAIN]
    vectors = [vec_ref[0:1, :]] + [vec_ref[i : i + 1, :width] for i in range(1, 5)]
    vectors += [sums[:, :width], sums[:, 2 * width :], gain_row, shift_row]
    tiles = [row[:, at : at + VECTOR_LANES] for row in vectors for at in range(0, row.shape[1], VECTOR_LANES)]
    piece = width // PIECES
    per = len(tiles) // PIECES
    total[:, 3 * width :] = jnp.zeros((width, VECTOR_LANES), F32)
    for i, tile in enumerate(tiles):
        at = (i // per) * piece + i % per
        total[at : at + 1, 3 * width :] = tile
    place_pieces(marks, mode, total, keep_ref, send_ref)


def qkv_grad(marks, mode, normed, small, w_qkv, vec, dqs, owns, gots):
    tokens, width = normed.shape
    columns = 3 * width + VECTOR_LANES
    half = jax.ShapeDtypeStruct((width // 2, columns), BF16)
    flat = [normed, small, w_qkv, vec, *dqs, *owns, *gots]
    return pl.pallas_call(
        functools.partial(qkv_grad_kernel, len(dqs), mode),
        in_specs=[smem()] + [vmem()] * len(flat),
        out_specs=[vmem()] * 3,
        out_shape=[jax.ShapeDtypeStruct((tokens, 3 * width), BF16), half, half],
        scratch_shapes=[pltpu.VMEM((width, columns), F32)],
        compiler_params=pltpu.CompilerParams(vmem_limit_bytes=16 * MIB),
        name="qkv_grad",
        cost_estimate=pl.CostEstimate(
            flops=6 * tokens * width * width, bytes_accessed=18 * tokens * width, transcendentals=0
        ),
    )(marks, *flat)


def last_kernel(pieces, packed, gmid_ref, small, w_ref, x_ref, *out_refs):
    band = out_refs[0].shape[0]
    grad = dot_nt(packed[...], w_ref[...])
    unit, scale = norm_parts(x_ref[...].astype(F32))
    result = (gmid_ref[...] + norm_back(grad, unit, scale, small[LN1_GAIN])).astype(BF16)
    for j in range(pieces):
        out_refs[j][...] = result[j * band : (j + 1) * band]


def last_part(packed, gmid, small, w_qkv, x, pieces):
    tokens, width = gmid.shape
    return pl.pallas_call(
        functools.partial(last_kernel, pieces),
        out_shape=[jax.ShapeDtypeStruct((tokens // pieces, width), BF16)] * pieces,
        compiler_params=pltpu.CompilerParams(vmem_limit_bytes=12 * MIB),
        name="last_part",
        cost_estimate=pl.CostEstimate(
            flops=6 * tokens * width * width, bytes_accessed=10 * tokens * width, transcendentals=0
        ),
    )(packed, gmid, small, w_qkv, x)


def assemble_kernel(segments, mode, per, marks, *refs):
    own_far, out_refs = refs[:2], refs[2:]
    half = PIECES // 2
    piece = own_far[0].shape[0] // half
    step = pl.program_id(0)

    def one(i, carry):
        index = step * per + i

        def fill(which):
            source = own_far[which]
            for low, high, way in columns_by_way(mode, source.shape[1]):
                at = pl.ds(pl.multiple_of(((index ^ marks[2 * which + way]) % half) * piece, piece), piece)
                for start, stop, which_out, tall, offset in segments:
                    first, last = max(start, low), min(stop, high)
                    if first < last:
                        spot = pl.ds(pl.multiple_of(i * tall + offset, piece), piece)
                        out_refs[which_out][spot, first - start : last - start] = source[at, first:last].astype(F32)

        mine = index // half == marks[0] // half
        pl.when(mine)(functools.partial(fill, 0))
        pl.when(jnp.logical_not(mine))(functools.partial(fill, 1))
        return carry

    lax.fori_loop(0, per, one, 0)


def assemble(marks, mode, parts, segments, shapes, name):
    steps = 2
    per = PIECES // steps
    size = sum(rows * columns for rows, columns in shapes)
    return pl.pallas_call(
        functools.partial(assemble_kernel, segments, mode, per),
        grid=(steps,),
        in_specs=[smem()] + [vmem()] * 2,
        out_specs=[pl.BlockSpec((rows // steps, w), lambda i: (i, 0)) for rows, w in shapes],
        out_shape=[jax.ShapeDtypeStruct(shape, F32) for shape in shapes],
        compiler_params=pltpu.CompilerParams(vmem_limit_bytes=16 * MIB),
        name=name,
        cost_estimate=pl.CostEstimate(flops=size, bytes_accessed=6 * size, transcendentals=0),
    )(marks, *parts)


def return_kernel(halves, row_ref, *refs):
    out, sems = refs[-2], refs[-1]
    copies = []
    for i, (ref, (j, half)) in enumerate(zip(refs, halves)):
        width = ref.shape[1]
        at = 0 if half is None else half * width
        copies.append(pltpu.make_async_copy(ref, out.at[row_ref[0] ^ j, :, at : at + width], sems.at[i]))
    for copy in copies:
        copy.start()
    for copy in copies:
        copy.wait()


def return_rows(row, own, halves, name):
    flat = [own] + [piece for half in halves for piece in half]
    places = [(0, None)] + [(j + 1, h) for h, half in enumerate(halves) for j in range(len(half))]
    pieces = len(halves[0]) + 1
    return pl.pallas_call(
        functools.partial(return_kernel, places),
        in_specs=[smem()] + [vmem()] * len(flat),
        out_specs=pl.BlockSpec(memory_space=pl.ANY),
        out_shape=jax.ShapeDtypeStruct((pieces, *own.shape), BF16),
        scratch_shapes=[pltpu.SemaphoreType.DMA((len(flat),))],
        compiler_params=pltpu.CompilerParams(vmem_limit_bytes=4 * MIB),
        name=name,
    )(row, *flat)


def swap(value, axis, size, mask):
    return lax.ppermute(value, axis, [(i, i ^ mask) for i in range(size)])


class Order:
    def __init__(self):
        self.last = ()

    def enter(self, *values):
        return lax.optimization_barrier((values, self.last))[0]

    def leave(self, *values):
        self.last = values


class Cargo:
    def __init__(self, pieces):
        self.pieces = pieces
        width = pieces[0].shape[1] // 2
        self.columns = [slice(0, width), slice(width, 2 * width)]
        self.came = [[None] * len(pieces) for _ in range(2)]
        self.onward = [None, None]

    def load(self, half, way, first):
        columns = self.columns[half]
        far = self.pieces[3][:, columns] if first else self.onward[half]
        return jnp.concatenate([self.pieces[way + 1][:, columns], far], axis=0)

    def land(self, half, way, first, got):
        band = got.shape[0] // 2
        self.came[half][way + 1] = got[:band]
        if first:
            self.onward[half] = got[band:]
        else:
            self.came[half][3] = got[band:]


def fold(value, rows):
    if rows < value.shape[0]:
        return jnp.concatenate([value[at : at + rows] for at in range(0, value.shape[0], rows)], axis=1)
    wide = value.shape[1] * value.shape[0] // rows
    return jnp.concatenate([value[:, at : at + wide] for at in range(0, value.shape[1], wide)], axis=0)


class Wave:
    def __init__(self, order, keep, send, marks, mode, layout, core, ways, deep, rest):
        self.order, self.core, self.ways, self.deep, self.rest = order, core, ways, deep, rest
        self.marks, self.mode, self.layout = marks, mode, layout
        self.parts = columns_by_way(mode, keep.shape[1])
        self.value, self.got = [keep], [core(send)]
        self.cargo, self.aboard = {}, None
        order.leave(send)

    def arrived(self):
        count = len(self.value)
        values = self.order.enter(*self.value, *self.got)
        kept, came = values[:count], list(values[count:])
        if self.aboard is not None:
            cargo, first, ways, shape = self.aboard
            for i, way in enumerate(ways):
                own = self.parts[i][1] - self.parts[i][0]
                cargo.land(i, way, first, fold(came[i][:, own:], shape[0]))
                came[i] = came[i][:, :own]
            self.aboard = None
        return list(zip(kept, came))

    def added(self):
        return [add_low(one, two) for one, two in self.arrived()]

    def split(self, value):
        return [value[:, start:stop] for start, stop, _ in self.parts]

    def travel(self, step, values, key):
        ways = [(step + way) % 2 for _, _, way in self.parts]
        if key in self.cargo:
            cargo, first = self.cargo[key]
            loads = [cargo.load(i, way, first) for i, way in enumerate(ways)]
            self.aboard = (cargo, first, ways, loads[0].shape)
            values = [
                jnp.concatenate([value, fold(load, value.shape[0])], axis=1) for value, load in zip(values, loads)
            ]
        self.got = [self.ways[way](value) for way, value in zip(ways, values)]
        self.order.leave(*values)

    def plane(self, step):
        values = self.added()
        if step == 0:
            values = self.split(values[0])
        half = values[0].shape[0] // 2
        self.value = [value[:half] for value in values]
        self.travel(step, [value[half:] for value in values], ("out", step))

    def line(self):
        values = self.added()
        half = values[0].shape[0] // 2
        self.value = [jnp.concatenate([value[:half] for value in values], axis=1)]
        sent = jnp.concatenate([value[half:] for value in values], axis=1)
        self.got = [self.deep(sent)]
        self.order.leave(sent)

    def exchanges(self):
        for send in self.rest:
            self.value = self.added()
            self.got = [send(self.value[0])]
            self.order.leave(*self.value)

    def line_back(self):
        self.value = self.added()
        self.got = [self.deep(self.value[0])]
        self.order.leave(*self.value)

    def joined(self):
        return [jnp.concatenate(pair, axis=0) for pair in self.arrived()]

    def plane_back(self, step):
        values = self.joined()
        self.value = self.split(values[0]) if step == 1 else values
        self.travel(step, self.value, ("back", step))

    def core_back(self):
        self.value = [jnp.concatenate(self.joined(), axis=1)]
        self.got = [self.core(self.value[0])]
        self.order.leave(*self.value)

    def wait(self):
        self.got = list(self.order.enter(*self.got))
        self.order.leave(*self.got)

    def finish(self):
        ((own, far),) = self.arrived()
        self.sums = assemble(self.marks, self.mode, (own, far), *self.layout)
        self.order.leave(*self.sums)

    def steps(self):
        yield functools.partial(self.plane, 0)
        yield functools.partial(self.plane, 1)
        yield self.line
        yield self.exchanges
        yield self.line_back
        yield functools.partial(self.plane_back, 1)
        yield functools.partial(self.plane_back, 0)
        yield self.core_back
        yield self.finish


def add_low(one, two):
    return (one.astype(F32) + two.astype(F32)).astype(BF16)


def after(value, *others):
    return lax.optimization_barrier((value, others))[0]


def bits_of(axis, size):
    found, mask = [], 1
    while mask < size:
        found.append((axis, size, mask, (lax.axis_index(axis) // mask) % 2))
        mask *= 2
    return found


def per_device(
    seq_size, row_size,
    block_input, segment_ids, ln1_gain, ln1_shift, w_qkv, bias_query, bias_value, w_out, bias_out,
    ln2_gain, ln2_shift, w_up, bias_up, w_down, bias_down, out_grad,
):
    rows, band, width = block_input.shape
    length = segment_ids.shape[1]
    share = seq_size // rows
    tokens = rows * band
    crops = max(length // (4 * band), 1)
    place = lax.axis_index("seq")
    my_row, my_part = place // share, place % share

    def deal(pieces):
        got = [pieces[0]]
        for j in range(1, rows):
            turn = [(s, ((s // share) ^ j) * share + s % share) for s in range(seq_size)]
            got.append(lax.ppermute(pieces[j], "seq", turn))
        return got

    def pick(array):
        return [lax.dynamic_index_in_dim(array, my_row ^ j, 0, False) for j in range(rows)]

    xs = deal(pick(block_input))
    dys = pick(out_grad)

    own_row = lax.dynamic_index_in_dim(segment_ids, my_row, 0, False).reshape(seq_size, band)
    key_ids = jnp.concatenate(
        [
            lax.dynamic_index_in_dim(own_row, (my_row ^ j) * share + (my_part ^ i), 0, False)
            for i in range(share)
            for j in range(rows)
        ]
    )
    spot = jnp.arange(128) % 64
    same = key_ids[:, None] == spot[None, :]
    used = spot[None, :] < crops
    ones = (spot >= LSE_LANE) & (spot < LSE_LANE + 3)
    kf = jnp.where(used, jnp.where(same, 0.0, -1.0), jnp.where(ones, 1.0, 0.0)).astype(BF16)
    qf = jnp.where(used & same, BIG, 0.0).astype(BF16)[:tokens]

    small = jnp.stack(
        [ln1_gain, ln1_shift, bias_query, bias_value, bias_out, ln2_gain, ln2_shift, bias_down]
    )
    small = jnp.concatenate([small, bias_up.reshape(-1, width)], axis=0)
    shape = jax.ShapeDtypeStruct
    x, normed, q, kv = pl.pallas_call(
        functools.partial(qkv_kernel, rows, width),
        out_shape=[
            shape((tokens, width), BF16),
            shape((tokens, width), BF16),
            shape((tokens, width), BF16),
            shape((tokens, 2 * width), BF16),
        ],
        compiler_params=pltpu.CompilerParams(vmem_limit_bytes=12 * MIB),
        name="norm_and_project",
    )(*xs, small, w_qkv)


    dys = list(lax.optimization_barrier((dys, kv))[0])
    dys = deal(dys)
    seq_bits = bits_of("seq", seq_size)
    row_bits = bits_of("row", row_size)
    part_bits = [bit for bit in seq_bits if bit[2] < share]
    kvs, whole = [kv], kv
    for axis, size, mask, own in part_bits:
        got = swap(whole, axis, size, mask)
        kvs.append(got)
        if mask * 2 < share:
            whole = jnp.concatenate([whole, got], 0)

    mix, qfb = attention_forward(q, kvs, qf, kf)
    *outs, mixed, two, active, grad_hidden, grad_attn, grad_middle, gm, gmf, vec, dy = middle_part(
        dys, x, mix, small, w_out, w_up, w_down
    )

    def straight(bit):
        return lambda value: swap(value, *bit[:3])

    plane = [bit for bit in seq_bits if bit[2] >= share]
    core, one, two_, deep = seq_bits[0][3], plane[0][3], plane[1][3], row_bits[0][3]
    ways = (straight(plane[0]), straight(plane[1]))
    rest = [straight(bit) for bit in row_bits[1:] + plane[2:] + part_bits[1:]]
    route = (straight(seq_bits[0]), ways, straight(row_bits[0]), rest)
    left, right = one * 4 + two_ * 2 + deep, two_ * 4 + one * 2 + deep
    mine, other = core * 8, 8 - core * 8
    marks = jnp.stack([mine + left, mine + right, other + left, other + right]).astype(jnp.int32)

    pairs = width // 128
    ff = w_up.shape[1]
    tall = width // PIECES
    down_layout = ([(0, width, 0, ff // PIECES, 0)], [(ff, width)], "assemble_down")
    up_segments = [(0, ff, 0, tall, 0), (ff, ff + width, 1, tall, 0)]
    up_layout = (up_segments, [(width, ff), (width, width)], "assemble_up_out")
    qkv_segments = [(0, 3 * width, 0, tall, 0), (3 * width, 3 * width + VECTOR_LANES, 1, tall, 0)]
    qkv_layout = (qkv_segments, [(width, 3 * width), (width, VECTOR_LANES)], "assemble_qkv")
    row = my_row.astype(jnp.int32).reshape(1)

    order = Order()
    terms, gots, steps, done = [], [], {}, {}

    def backward():
        (grad,) = order.enter(gm)
        terms.append(attention_backward(q, grad, qfb, gmf, kvs, kf, AT_ONCE * len(terms), AT_ONCE))
        order.leave(*terms[-1])
        if share == 2:
            gots.append(straight(part_bits[0])(terms[-1][2]))

    def start_wave(letter, pairs_of, name, layout):
        flat = order.enter(*[array for pair in pairs_of for array in pair])
        keep, send = weight_grad(marks, MODES[letter], list(zip(flat[0::2], flat[1::2])), name)
        done[letter] = Wave(order, keep, send, marks, MODES[letter], layout, *route)
        steps[letter] = done[letter].steps()
        if letter == "d":
            ride("d", outs, "out", "o")

    def start_qkv():
        own_terms, far_terms = [term[1] for term in terms], gots
        if share != 2:
            both = jnp.concatenate(
                [jnp.concatenate([part.astype(BF16) for part in term[1:]], 0) for term in terms], axis=1
            )
            for bit in reversed(part_bits):
                half = both.shape[0] // 2
                kept, got = both[:half], straight(bit)(both[half:])
                both = add_low(kept, got)
            cuts = [slice(256 * AT_ONCE * t, 256 * AT_ONCE * (t + 1)) for t in range(len(terms))]
            own_terms = [kept[:, cut].astype(F32) for cut in cuts]
            far_terms = [got[:, cut] for cut in cuts]
        (vec_,) = order.enter(vec)
        dqs = [term[0] for term in terms]
        done["p"], keep, send = qkv_grad(marks, MODES["q"], normed, small, w_qkv, vec_, dqs, own_terms, far_terms)
        done["q"] = Wave(order, keep, send, marks, MODES["q"], qkv_layout, *route)
        steps["q"] = done["q"].steps()

    def last():
        (packed,) = order.enter(done["p"])
        pieces = last_part(packed, grad_middle, small, w_qkv, x, rows)
        order.leave(*pieces)
        ride("u", pieces, "back", "i")

    def ride(letter, pieces, stage, name):
        done[name] = Cargo(pieces)
        steps_ = (0, 1) if stage == "out" else (1, 0)
        for i, step in enumerate(steps_):
            done[letter].cargo[(stage, step)] = (done[name], i == 0)

    def take_back(name):
        cargo = done[name]
        halves = [list(order.enter(*half[1:])) for half in cargo.came]
        done[name] = return_rows(row, cargo.pieces[0], halves, "return_rows")
        order.leave(done[name])

    actions = {
        "b": backward,
        "D": lambda: start_wave("d", [(active, dy)], "grad_down", down_layout),
        "U": lambda: start_wave("u", [(two, grad_hidden), (mixed, grad_attn)], "grad_up_out", up_layout),
        "G": start_qkv,
        "L": last,
        "O": lambda: take_back("o"),
        "I": lambda: take_back("i"),
        "d": lambda: next(steps["d"])(),
        "u": lambda: next(steps["u"])(),
        "q": lambda: next(steps["q"])(),
    }
    def wait(which):
        if which.isdigit():
            if share == 2:
                (gots[int(which)],) = order.enter(gots[int(which)])
                order.leave(gots[int(which)])
        else:
            done[which].wait()

    for word in SCHEDULE:
        if word[0] == "w":
            wait(word[1])
        else:
            actions[word]()
    result, input_grad = done["o"], done["i"]
    (sum_down,) = done["d"].sums
    sum_up, sum_out = done["u"].sums
    sum_qkv, tiles = done["q"].sums

    count = (ff + 8 * width) // VECTOR_LANES // PIECES
    vectors = tiles.reshape(PIECES, -1, VECTOR_LANES)[:, :count].reshape(-1)
    cuts = [ff + i * width for i in range(9)]
    names = [vectors[a:b] for a, b in zip(cuts[:-1], cuts[1:])]
    ln2_gain_sum, ln2_shift_sum, bias_down_sum, bias_out_sum = names[:4]
    bias_q_sum, bias_v_sum, ln1_gain_sum, ln1_shift_sum = names[4:]
    return (
        result,
        input_grad,
        ln1_gain_sum,
        ln1_shift_sum,
        sum_qkv,
        bias_q_sum,
        bias_v_sum,
        sum_out,
        bias_out_sum,
        ln2_gain_sum,
        ln2_shift_sum,
        sum_up,
        vectors[:ff],
        sum_down,
        bias_down_sum,
    )


def solution(mesh):
    split = P("row", "seq", None)
    placed = (split, P("row", None)) + (P(),) * 13 + (split,)
    return jax.shard_map(
        functools.partial(per_device, mesh.shape["seq"], mesh.shape["row"]),
        mesh=mesh,
        in_specs=placed,
        out_specs=(split, split) + (P(),) * 13,
        check_vma=False,
    )
```
